32 devices in a mesh: group: 2 (over x), seq: 16 (over z, y, core).
Axes of the slice: x: 2, y: 2, z: 4, core: 2. Of those that a mesh axis runs over, the one named last changes fastest.
Arguments:
- hidden: bfloat16 [8, 256, 1408], P('group', 'seq'), parts along dimension 0, may hold values from -14 to 14
- skip: bfloat16 [8, 256, 1408], P('group', 'seq'), parts along dimension 0, may hold values from -6 to 6
- timestep: int32 [8], P('group'), parts along dimension 0, may hold values from 0 to 999
- w_skip: bfloat16 [2816, 1408], P('seq'), may hold values from -0.109375 to 0.109375
- w_mod: bfloat16 [256, 4224], replicated, may hold values from -5 to 5
- w_qkv: bfloat16 [1408, 4224], P('seq'), may hold values from -0.15625 to 0.15625
- w_out: bfloat16 [1408, 1408], P('seq'), may hold values from -0.15625 to 0.15625
Outputs:
- result: bfloat16 [8, 256, 1408], P('group', 'seq'), parts along dimension 0
The draws below stay inside these ranges and needn't reach their ends.
There are 2 independent parts, one for each index of `group`. The reference program is written for one: setup_inputs(seed, part) draws one part's arguments, and reference() takes and returns one part's arrays. A program takes and returns all parts, laid end to end along the dimension named above; an argument that names none is the same for every part. Nothing has to cross between parts.
All inputs are finite; a program needn't handle non-finite values.
Results may differ from the reference program's by a relative error of at most 0.0095.
Values may be sent and summed in bfloat16 or wider, within the bound.
No kernel may reach another device: no remote copies, remote signals or barrier semaphores. Data moves between devices by JAX's collectives and lax.ppermute only.
A program may use at most 128 MiB of HBM per device.

```python
import math
import jax
import jax.numpy as jnp
from jax import lax

D = 1408
H = 16
HD = 88
TDIM = 256
SEQS = 4
LEN = 256


cluster_count = 8


def draw_hidden(key, part):
    key_center = jax.random.fold_in(key, 11)
    key_assign = jax.random.fold_in(key, 12)
    key_spread = jax.random.fold_in(key, 13)
    centers = jnp.clip(jax.random.normal(key_center, (SEQS, cluster_count, D), jnp.float32), -4.0, 4.0) * 2.0
    assign = jax.random.randint(key_assign, (SEQS, LEN), 0, cluster_count)
    picked = centers[jnp.arange(SEQS)[:, None], assign]
    spread_part = jnp.clip(jax.random.normal(key_spread, (SEQS, LEN, D), jnp.float32), -6.0, 6.0)
    return (picked + spread_part).astype(jnp.bfloat16)


def draw_w_mod(key, part):
    key_entries = jax.random.fold_in(key, 21)
    entries = jnp.clip(jax.random.normal(key_entries, (TDIM, 3 * D), jnp.float32), -4.0, 4.0)
    column_scale = jnp.where(jnp.arange(3 * D) >= 2 * D, 5.0, 1.0).astype(jnp.float32)
    return (entries * column_scale[None, :] * TDIM ** (-0.5)).astype(jnp.bfloat16)


def touch_ends(array, stream_key, smallest, largest):
    extent = array.shape
    index_at = [jax.random.randint(jax.random.fold_in(stream_key, axis), (), 0, extent[axis]) for axis in range(len(extent))]
    array = array.at[tuple(index_at)].set(smallest)
    longest = extent.index(max(extent))
    index_at[longest] = (index_at[longest] + 1) % extent[longest]
    return array.at[tuple(index_at)].set(largest)


def level_of(stream_key, extent, shards, smallest, largest):
    level = 1.0
    for dim, parts in shards:
        draws = jax.random.uniform(jax.random.fold_in(jax.random.fold_in(stream_key, 6), dim), (parts,), jnp.float32, smallest / len(shards), largest / len(shards))
        level = level * jnp.repeat(jnp.exp(draws), extent[dim] // parts).reshape((-1,) + (1,) * (len(extent) - 1 - dim))
    return level


def gaussian(rng, dims, scale, most, shards=(), kind=jnp.bfloat16):
    result = scale * jax.random.normal(rng, dims, jnp.float32)
    if shards:
        result = result * level_of(rng, dims, shards, -0.22, 0.18)
    return jnp.clip(result, -most, most).astype(kind)


def setup_inputs(seed: int = 0, part: int = 0) -> dict:
    seeds = jax.random.split(jax.random.key(seed), 8)
    own_keys = jax.random.split(jax.random.fold_in(seeds[7], part), 8)
    return {
        "hidden": draw_hidden(jax.random.fold_in(jax.random.fold_in(seeds[7], part), 71), part),
        "skip": gaussian(own_keys[1], (SEQS, LEN, D), 1.0, 6.0, ((1, 16),)),
        "timestep": touch_ends(jax.random.randint(own_keys[2], (SEQS,), 0, 1000), jax.random.fold_in(own_keys[2], 1), 0, 999).astype(jnp.int32),
        "w_skip": gaussian(seeds[3], (2 * D, D), (2 * D) ** -0.5, 0.109375, ((0, 16),)),
        "w_mod": draw_w_mod(jax.random.fold_in(seeds[7], 71), part),
        "w_qkv": gaussian(seeds[5], (D, 3 * D), D ** -0.5, 0.15625, ((0, 16),)),
        "w_out": gaussian(seeds[6], (D, D), D ** -0.5, 0.15625, ((0, 16),)),
    }


def layer_norm(x):
    mean = lax.optimization_barrier(jnp.mean(x, axis=-1, keepdims=True))
    var = lax.optimization_barrier(jnp.mean((x - mean) ** 2, axis=-1, keepdims=True))
    return (x - mean) * lax.rsqrt(var + 1e-06)

def reference(hidden, skip, timestep, w_skip, w_mod, w_qkv, w_out):
    combined = jnp.concatenate([hidden, skip], axis=2).reshape(SEQS * LEN, 2 * D)
    merged = jnp.dot(combined, w_skip, preferred_element_type=jnp.float32).astype(jnp.bfloat16)
    half = TDIM // 2
    freqs = jnp.exp(-math.log(10000.0) * jnp.arange(half, dtype=jnp.float32) / half)
    angles = timestep.astype(jnp.float32)[:, None] * freqs[None, :]
    embed = jnp.concatenate([jnp.cos(angles), jnp.sin(angles)], axis=1)
    act = jax.nn.silu(embed).astype(jnp.bfloat16)
    mod = jnp.dot(act, w_mod, preferred_element_type=jnp.float32)
    shift, scale, gate = (mod[:, :D], mod[:, D:2 * D], mod[:, 2 * D:])
    base = merged.astype(jnp.float32).reshape(SEQS, LEN, D)
    normed = (layer_norm(base) * (1.0 + scale[:, None, :]) + shift[:, None, :]).astype(jnp.bfloat16)
    qkv = jnp.dot(normed.reshape(SEQS * LEN, D), w_qkv, preferred_element_type=jnp.float32)
    qkv = qkv.reshape(SEQS, LEN, 3, H, HD)
    query = (layer_norm(qkv[:, :, 0]) * HD ** (-0.5)).astype(jnp.bfloat16)
    key = layer_norm(qkv[:, :, 1]).astype(jnp.bfloat16)
    value = qkv[:, :, 2].astype(jnp.bfloat16)
    query = jnp.transpose(query, (0, 2, 1, 3)).reshape(SEQS * H, LEN, HD)
    key = jnp.transpose(key, (0, 2, 1, 3)).reshape(SEQS * H, LEN, HD)
    value = jnp.transpose(value, (0, 2, 1, 3)).reshape(SEQS * H, LEN, HD)

    def attend(trio):
        qpair, kpair, vpair = trio
        scores = jnp.einsum('qd,kd->qk', qpair, kpair, preferred_element_type=jnp.float32)
        probs = jax.nn.softmax(scores, axis=-1).astype(jnp.bfloat16)
        return jnp.dot(probs, vpair, preferred_element_type=jnp.float32).astype(jnp.bfloat16)
    attended = lax.map(attend, (query, key, value))
    attended = jnp.transpose(attended.reshape(SEQS, H, LEN, HD), (0, 2, 1, 3)).reshape(SEQS * LEN, D)
    projected = jnp.dot(attended, w_out, preferred_element_type=jnp.float32).reshape(SEQS, LEN, D)
    return (base + gate[:, None, :] * projected).astype(jnp.bfloat16)
```

```python
import math

import jax
import jax.numpy as jnp
from jax import lax
from jax.sharding import PartitionSpec as P

H = 16
HD = 88
TDIM = 256
BF = jnp.bfloat16
F32 = jnp.float32


def layer_norm(x):
    mean = jnp.mean(x, axis=-1, keepdims=True)
    var = jnp.mean((x - mean) ** 2, axis=-1, keepdims=True)
    return (x - mean) * lax.rsqrt(var + 1e-06)


def modulation(timestep, w_mod):
    half = TDIM // 2
    freqs = jnp.exp(-math.log(10000.0) * jnp.arange(half, dtype=F32) / half)
    angles = timestep.astype(F32)[:, None] * freqs[None, :]
    embed = jnp.concatenate([jnp.cos(angles), jnp.sin(angles)], axis=1)
    act = jax.nn.silu(embed).astype(BF)
    return jnp.dot(act, w_mod, preferred_element_type=F32)


def attend_pair(trio):
    qpair, kpair, vpair = trio
    scores = jnp.einsum("qd,kd->qk", qpair, kpair, preferred_element_type=F32)
    probs = jax.nn.softmax(scores, axis=-1).astype(BF)
    return jnp.dot(probs, vpair, preferred_element_type=F32).astype(BF)


def to_heads(x, seqs, local):
    return jnp.transpose(x, (0, 2, 1, 3)).reshape(seqs * H, local, HD)


def gathered(hidden, skip, timestep, w_skip, w_mod, w_qkv, w_out):
    seqs, local, width = hidden.shape
    tok_rows = seqs * local
    combined = jnp.concatenate([hidden, skip], axis=2).reshape(tok_rows, 2 * width)
    full_skip = lax.all_gather(w_skip, "seq", axis=0, tiled=True)
    merged = jnp.dot(combined, full_skip, preferred_element_type=F32).astype(BF)
    mod = modulation(timestep, w_mod)
    shift, scale, gate = (mod[:, :width], mod[:, width : 2 * width], mod[:, 2 * width :])
    base = merged.astype(F32).reshape(seqs, local, width)
    normed = (layer_norm(base) * (1.0 + scale[:, None, :]) + shift[:, None, :]).astype(BF)
    full_qkv = lax.all_gather(w_qkv, "seq", axis=0, tiled=True)
    qkv = jnp.dot(normed.reshape(tok_rows, width), full_qkv, preferred_element_type=F32)
    qkv = qkv.reshape(seqs, local, 3, H, HD)
    query = (layer_norm(qkv[:, :, 0]) * HD ** (-0.5)).astype(BF)
    key = layer_norm(qkv[:, :, 1]).astype(BF)
    value = qkv[:, :, 2].astype(BF)
    trio = [
        lax.all_to_all(to_heads(x, seqs, local), "seq", split_axis=0, concat_axis=1, tiled=True)
        for x in (query, key, value)
    ]
    attended = lax.map(attend_pair, tuple(trio))
    attended = lax.all_to_all(attended, "seq", split_axis=1, concat_axis=0, tiled=True)
    attended = jnp.transpose(attended.reshape(seqs, H, local, HD), (0, 2, 1, 3))
    full_out = lax.all_gather(w_out, "seq", axis=0, tiled=True)
    projected = jnp.dot(
        attended.reshape(tok_rows, width), full_out, preferred_element_type=F32
    ).reshape(seqs, local, width)
    return (base + gate[:, None, :] * projected).astype(BF)


def in_planes(groups, n, hidden, skip, timestep, w_skip, w_mod, w_qkv, w_out):
    seqs, local, width = hidden.shape
    inner = n // seqs
    per = seqs // groups
    cols = width // groups
    g = lax.axis_index("group")
    j = lax.axis_index("seq")
    z = j // inner
    plane = [[p * inner + i for i in range(inner)] for p in range(seqs)]
    column = [[p * inner + i for p in range(seqs)] for i in range(inner)]
    toks = seqs * local

    rows = w_skip.shape[0]
    ws = lax.dynamic_slice(w_skip, (0, g * cols), (rows, cols))
    ws = lax.all_gather(ws, "seq", axis=0, tiled=True, axis_index_groups=column)
    qrows = w_qkv.shape[0]
    wq = w_qkv.reshape(qrows, 3, groups, per, inner, HD)
    wq = lax.dynamic_index_in_dim(wq, g, axis=2, keepdims=False)
    wq = wq.transpose(3, 0, 1, 2, 4).reshape(inner, qrows, 3 * per * HD)
    wq = lax.all_to_all(wq, "seq", 0, 0, tiled=True, axis_index_groups=plane)
    wq = wq.reshape(inner * qrows, 3 * per * HD)
    wq = lax.all_gather(wq, "seq", axis=0, tiled=True, axis_index_groups=column)
    wo = lax.dynamic_slice(w_out, (0, g * cols), (HD, cols))
    wo = lax.all_gather(wo, "seq", axis=0, tiled=True, axis_index_groups=column)

    times = lax.all_gather(timestep, "group", axis=0)
    mod = modulation(lax.dynamic_index_in_dim(times, z, axis=1, keepdims=False), w_mod)
    shift, scale, gate = (mod[:, :width], mod[:, width : 2 * width], mod[:, 2 * width :])
    gate = lax.dynamic_slice(gate, (0, g * cols), (groups, cols))

    x = jnp.concatenate([hidden, skip], axis=2).reshape(seqs, local, seqs, inner, rows)
    x = x.transpose(0, 3, 1, 2, 4).reshape(n, local, seqs * rows)
    x = lax.all_to_all(x, "seq", 0, 0, tiled=True).reshape(n * local, seqs * rows)
    x = lax.all_gather(x, "group", axis=0, tiled=True)
    part = jnp.dot(x, ws, preferred_element_type=F32).astype(BF)
    part = part.reshape(groups, seqs, inner, local, cols).transpose(2, 0, 1, 3, 4)
    part = part.reshape(inner, groups * toks, cols)
    part = lax.all_to_all(part, "seq", 0, 0, tiled=True, axis_index_groups=plane)
    base = jnp.sum(part.astype(F32), axis=0).astype(BF)

    merged = lax.all_gather(base, "group", axis=1, tiled=True).reshape(groups, toks, width)
    merged = jnp.stack(
        [
            lax.all_gather(merged[h], "seq", axis=0, tiled=True, axis_index_groups=plane)
            for h in range(groups)
        ]
    )
    normed = (
        layer_norm(merged.astype(F32)) * (1.0 + scale[:, None, :]) + shift[:, None, :]
    ).astype(BF)
    total = inner * toks
    qkv = jnp.dot(normed.reshape(groups * total, width), wq, preferred_element_type=F32)
    qkv = qkv.reshape(groups, total, 3, per, HD)
    query = (layer_norm(qkv[:, :, 0]) * HD ** (-0.5)).astype(BF)
    key = layer_norm(qkv[:, :, 1]).astype(BF)
    value = qkv[:, :, 2].astype(BF)
    scores = jnp.einsum("gqhd,gkhd->ghqk", query, key, preferred_element_type=F32)
    probs = jax.nn.softmax(scores, axis=-1).astype(BF)
    attended = jnp.einsum("ghqk,gkhd->gqhd", probs, value, preferred_element_type=F32)
    attended = attended.astype(BF).reshape(groups * total, per * HD)

    attended = lax.all_gather(attended, "group", axis=1, tiled=True)
    part = jnp.dot(attended, wo, preferred_element_type=F32).astype(BF)
    part = part.reshape(groups, inner, toks, cols).transpose(1, 0, 2, 3)
    part = lax.all_to_all(part, "seq", 0, 0, tiled=True, axis_index_groups=plane)
    projected = jnp.sum(part.astype(F32), axis=0)
    base = base.reshape(groups, toks, cols).astype(F32)
    out = (base + gate[:, None, :] * projected).astype(BF)
    out = lax.all_to_all(out, "group", 0, 2, tiled=True)
    out = out.reshape(seqs, local, width)
    return lax.all_to_all(out, "seq", 0, 0, tiled=True, axis_index_groups=column)


def solution(mesh):
    groups, n = mesh.shape["group"], mesh.shape["seq"]

    def per_device(*args):
        hidden, w_out = args[0], args[6]
        seqs, _, width = hidden.shape
        fits = n % seqs == 0 and w_out.shape[0] == HD and seqs % groups == 0 and width % groups == 0
        if fits:
            return in_planes(groups, n, *args)
        return gathered(*args)

    placed = (
        P("group", "seq", None),
        P("group", "seq", None),
        P("group"),
        P("seq", None),
        P(),
        P("seq", None),
        P("seq", None),
    )
    return jax.shard_map(
        per_device, mesh=mesh, in_specs=placed, out_specs=P("group", "seq", None), check_vma=False
    )
```

```python
import math
from functools import partial

import jax
import jax.numpy as jnp
from jax import lax
from jax.experimental import pallas as pl
from jax.experimental.pallas import tpu as pltpu
from jax.sharding import PartitionSpec as P

H = 16
HD = 88
TDIM = 256
BF = jnp.bfloat16
F32 = jnp.float32


def layer_norm(x):
    mean = jnp.mean(x, axis=-1, keepdims=True)
    var = jnp.mean((x - mean) ** 2, axis=-1, keepdims=True)
    return (x - mean) * lax.rsqrt(var + 1e-06)


def modulation(timestep, w_mod):
    half = TDIM // 2
    freqs = jnp.exp(-math.log(10000.0) * jnp.arange(half, dtype=F32) / half)
    angles = timestep.astype(F32)[:, None] * freqs[None, :]
    embed = jnp.concatenate([jnp.cos(angles), jnp.sin(angles)], axis=1)
    act = jax.nn.silu(embed).astype(BF)
    return jnp.dot(act, w_mod, preferred_element_type=F32)


def attend_pair(trio):
    qpair, kpair, vpair = trio
    scores = jnp.einsum("qd,kd->qk", qpair, kpair, preferred_element_type=F32)
    probs = jax.nn.softmax(scores, axis=-1).astype(BF)
    return jnp.dot(probs, vpair, preferred_element_type=F32).astype(BF)


def to_heads(x, seqs, local):
    return jnp.transpose(x, (0, 2, 1, 3)).reshape(seqs * H, local, HD)


def gathered(hidden, skip, timestep, w_skip, w_mod, w_qkv, w_out):
    seqs, local, width = hidden.shape
    tok_rows = seqs * local
    combined = jnp.concatenate([hidden, skip], axis=2).reshape(tok_rows, 2 * width)
    full_skip = lax.all_gather(w_skip, "seq", axis=0, tiled=True)
    merged = jnp.dot(combined, full_skip, preferred_element_type=F32).astype(BF)
    mod = modulation(timestep, w_mod)
    shift, scale, gate = (mod[:, :width], mod[:, width : 2 * width], mod[:, 2 * width :])
    base = merged.astype(F32).reshape(seqs, local, width)
    normed = (layer_norm(base) * (1.0 + scale[:, None, :]) + shift[:, None, :]).astype(BF)
    full_qkv = lax.all_gather(w_qkv, "seq", axis=0, tiled=True)
    qkv = jnp.dot(normed.reshape(tok_rows, width), full_qkv, preferred_element_type=F32)
    qkv = qkv.reshape(seqs, local, 3, H, HD)
    query = (layer_norm(qkv[:, :, 0]) * HD ** (-0.5)).astype(BF)
    key = layer_norm(qkv[:, :, 1]).astype(BF)
    value = qkv[:, :, 2].astype(BF)
    trio = [
        lax.all_to_all(to_heads(x, seqs, local), "seq", split_axis=0, concat_axis=1, tiled=True)
        for x in (query, key, value)
    ]
    attended = lax.map(attend_pair, tuple(trio))
    attended = lax.all_to_all(attended, "seq", split_axis=1, concat_axis=0, tiled=True)
    attended = jnp.transpose(attended.reshape(seqs, H, local, HD), (0, 2, 1, 3))
    full_out = lax.all_gather(w_out, "seq", axis=0, tiled=True)
    projected = jnp.dot(
        attended.reshape(tok_rows, width), full_out, preferred_element_type=F32
    ).reshape(seqs, local, width)
    return (base + gate[:, None, :] * projected).astype(BF)


class Place:
    def __init__(self, groups, n, seqs):
        self.G, self.S = groups, seqs
        self.Y = n // seqs // groups
        self.n = n
        g, j = lax.axis_index("group"), lax.axis_index("seq")
        self.x, self.z = g, j // (n // seqs)
        self.y, self.c = (j // groups) % self.Y, j % groups
        self.where = jnp.stack([self.x, self.z, self.y, self.c]).astype(jnp.int32)

    def send(self, value, to):
        pairs = []
        for x in range(self.G):
            for z in range(self.S):
                for y in range(self.Y):
                    for c in range(self.G):
                        tx, tz, ty, tc = to(x, z, y, c)
                        there = (tx % self.G, tz % self.S, ty % self.Y, tc % self.G)
                        pairs.append((self.flat(x, z, y, c), self.flat(*there)))
        return lax.ppermute(value, ("group", "seq"), pairs)

    def flat(self, x, z, y, c):
        return x * self.n + (z * self.Y + y) * self.G + c


def call(kernel, outs, where, *arrays, scratch=(), flops=0):
    moved = sum(a.size * a.dtype.itemsize for a in arrays)
    return pl.pallas_call(
        kernel,
        out_shape=[jax.ShapeDtypeStruct(s, d) for s, d in outs],
        in_specs=[pl.BlockSpec(memory_space=pltpu.SMEM)]
        + [pl.BlockSpec(memory_space=pltpu.VMEM)] * len(arrays),
        out_specs=[pl.BlockSpec(memory_space=pltpu.VMEM)] * len(outs),
        scratch_shapes=list(scratch),
        compiler_params=pltpu.CompilerParams(vmem_limit_bytes=40 * 2**20),
        cost_estimate=pl.CostEstimate(flops=flops, bytes_accessed=2 * moved, transcendentals=0),
    )(where, *arrays)


def pieces_kernel(S, where, hidden, skip, *outs):
    z = where[1]
    for s in range(S):
        outs[s][...] = hidden[(z + s) % S]
        outs[S + s][...] = skip[(z + s) % S]


def slices_kernel(G, S, Y, where, w_skip, w_qkv, w_out, *outs):
    x, y, c = where[0], where[2], where[3]
    width = w_skip.shape[1]
    block, part, half = width // (G * Y), S // G * HD, width // G
    skips, qkvs, rest = outs[:Y], outs[Y : Y + Y * G], outs[Y + Y * G :]
    for gx in range(G):
        for gy in range(Y):
            for e in range(Y):

                @pl.when((x == gx) & ((y + e) % Y == gy))
                def _():
                    b = gx * Y + gy
                    skips[e][...] = w_skip[:, b * block : (b + 1) * block]
                    for gc in range(G):
                        for f in range(G):

                            @pl.when((c + f) % G == gc)
                            def _():
                                for p in range(3):
                                    for t in range(S // G):
                                        head = ((gc * (S // G) + t) * Y + gy) * G + gx
                                        at = p * width + head * HD
                                        to = p * part + t * HD
                                        qkvs[e * G + f][:, to : to + HD] = w_qkv[:, at : at + HD]

    for gc in range(G):
        for f in range(G):

            @pl.when((c + f) % G == gc)
            def _():
                rest[f][...] = w_out[:, gc * half : (gc + 1) * half]


def merged_kernel(G, S, Y, where, *refs):
    z, y, c = where[1], where[2], where[3]
    blocks = Y * G
    hid, skp = refs[:blocks], refs[blocks : 2 * blocks]
    weights = refs[2 * blocks : 2 * blocks + G * S]
    out, xs, ws = refs[2 * blocks + G * S :]
    toks, width = hid[0].shape
    for k in range(blocks):
        xs[k * toks : (k + 1) * toks, :width] = hid[k][...]
        xs[k * toks : (k + 1) * toks, width:] = skp[k][...]
    rows = weights[0].shape[0] // Y
    for f in range(G):
        for s in range(S):
            for e in range(Y):
                j = (((z + S - s) % S) * Y + (y + Y - e) % Y) * G + (c + G - f) % G
                at = pl.multiple_of(j * rows, 16)
                ws[pl.ds(at, rows), :] = weights[f * S + s][e * rows : (e + 1) * rows, :]
    out[...] = jnp.dot(xs[...], ws[...], preferred_element_type=F32).astype(BF)


def norm88(v):
    mean = jnp.sum(v, axis=-1, keepdims=True) * (1.0 / HD)
    d = v - mean
    var = jnp.sum(d * d, axis=-1, keepdims=True) * (1.0 / HD)
    return d * lax.rsqrt(var + 1e-06)


def attend_kernel(G, S, Y, where, *refs):
    x, z, y, c = where[0], where[1], where[2], where[3]
    blocks = Y * G
    merged, (shift, scale) = refs[:blocks], refs[blocks : blocks + 2]
    refs = refs[blocks + 2 :]
    wq, wo, refs = refs[: G * S], refs[G * S : 2 * G * S], refs[2 * G * S :]
    outs, base, (norm, wqs, att) = refs[:blocks], refs[blocks], refs[blocks + 1 :]
    rows, cols = merged[0].shape
    toks = rows // blocks
    width = cols * blocks

    for f in range(G):
        for s in range(S):
            wqs[f, (z + S - s) % S] = wq[f * S + s][...]
    total = jnp.zeros((rows, 1), F32)
    wide = []
    for e in range(Y):
        for d in range(G):
            m = merged[e * G + d]
            own = [
                m[pl.ds((((em - e) % Y) * G + (dm - d) % G) * toks, toks), :]
                for em in range(Y)
                for dm in range(G)
            ]
            base[(x + d) % G * Y + (y + e) % Y] = own[0]
            wide.append(jnp.concatenate(own, axis=0).astype(F32))
            total = total + jnp.sum(wide[-1], axis=-1, keepdims=True)
    mean = total * (1.0 / width)
    square = jnp.zeros((rows, 1), F32)
    for m in wide:
        square = square + jnp.sum((m - mean) ** 2, axis=-1, keepdims=True)
    inv = lax.rsqrt(square * (1.0 / width) + 1e-06)
    for e in range(Y):
        for d in range(G):
            b = (x + d) % G * Y + (y + e) % Y
            m = wide[e * G + d]
            norm[b] = ((m - mean) * inv * (1.0 + scale[b]) + shift[b]).astype(BF)
    per = S // G
    for f in range(G):
        qkv = jnp.dot(norm[0], wqs[f, 0], preferred_element_type=F32)
        for b in range(1, blocks):
            qkv = qkv + jnp.dot(norm[b], wqs[f, b], preferred_element_type=F32)
        first = (c + G - f) % G * per
        for t in range(per):
            q, k, v = (qkv[:, (p * per + t) * HD : (p * per + t + 1) * HD] for p in range(3))
            q = (norm88(q) * HD ** (-0.5)).astype(BF)
            k = norm88(k).astype(BF)
            v = v.astype(BF)
            scores = lax.dot_general(q, k, (((1,), (1,)), ((), ())), preferred_element_type=F32)
            top = jnp.max(scores, axis=-1, keepdims=True)
            probs = jnp.exp(scores - top)
            probs = (probs / jnp.sum(probs, axis=-1, keepdims=True)).astype(BF)
            att[first + t] = jnp.dot(probs, v, preferred_element_type=F32).astype(BF)
    for f in range(G):
        acc = jnp.dot(att[z], wo[f * S][...], preferred_element_type=F32)
        for s in range(1, S):
            acc = acc + jnp.dot(
                att[(z + S - s) % S], wo[f * S + s][...], preferred_element_type=F32
            )
        acc = acc.astype(BF)
        for k in range(blocks):
            outs[k][(c + G - f) % G] = acc[k * toks : (k + 1) * toks, :]


def result_kernel(G, S, Y, where, gate, base, *refs):
    blocks = Y * G
    parts, outs = refs[:blocks], refs[blocks:]
    toks = base.shape[1]
    local = toks // S
    halves = []
    for h in range(G):
        acc = parts[0][h].astype(F32)
        for k in range(1, blocks):
            acc = acc + parts[k][h].astype(F32)
        halves.append(acc)
    projected = jnp.concatenate(halves, axis=1)
    merged = jnp.concatenate([base[b] for b in range(blocks)], axis=1).astype(F32)
    result = (merged + gate[...] * projected).astype(BF)
    for s in range(S):
        outs[s][...] = result[s * local : (s + 1) * local, :]


def home_kernel(S, where, *refs):
    z = where[1]
    for s in range(S):
        refs[S][(z + s) % S] = refs[s][...]


def in_planes(groups, n, hidden, skip, timestep, w_skip, w_mod, w_qkv, w_out):
    S, local, width = hidden.shape
    p = Place(groups, n, S)
    G, Y = p.G, p.Y
    blocks = Y * G
    cols, half = width // blocks, width // G
    toks, rows = S * local, w_skip.shape[0]
    per = S // G

    piece = ((local, width), BF)
    cut = call(partial(pieces_kernel, S), [piece] * (2 * S), p.where, hidden, skip)
    outs = [((rows, cols), BF)] * Y + [((HD, 3 * per * HD), BF)] * (Y * G) + [((HD, half), BF)] * G
    slices = call(partial(slices_kernel, G, S, Y), outs, p.where, w_skip, w_qkv, w_out)
    skips, qkvs, rest = slices[:Y], slices[Y : Y + Y * G], slices[Y + Y * G :]

    def to_plane(part):
        moved = [part[0]] + [
            p.send(part[s], lambda x, z, y, c, s=s: (x, z + s, y, c)) for s in range(1, S)
        ]
        return jnp.concatenate(moved, axis=0)

    def over_plane(value):
        return [
            p.send(value, lambda x, z, y, c, e=e, d=d: (c - d, z, y - e, x))
            for e in range(Y)
            for d in range(G)
        ]

    hid = over_plane(to_plane(cut[:S]))
    skp = over_plane(to_plane(cut[S:]))

    def ring(value):
        held = [value]
        for _ in range(1, S):
            held.append(p.send(held[-1], lambda x, z, y, c: (x, z + 1, y, c)))
        return held

    def over_cores(held):
        return held + [
            p.send(v, lambda x, z, y, c, f=f: (x, z, y, c + f)) for f in range(1, G) for v in held
        ]

    ws = [skips[0]] + [
        p.send(skips[e], lambda x, z, y, c, e=e: (x, z, y + e, c)) for e in range(1, Y)
    ]
    ws = over_cores(ring(jnp.concatenate(ws, axis=0)))

    got = {}
    for e in range(Y):
        for f in range(G):
            v = qkvs[e * G + f]
            if e or f:
                v = p.send(v, lambda x, z, y, c, e=e, f=f: (x, z, y + e, c + f))
            got[e, f] = v
    ordered = []
    for gy in range(Y):
        for gc in range(G):
            v = got[0, 0]
            for e in range(Y):
                for f in range(G):
                    if e or f:
                        here = ((p.y - e) % Y == gy) & ((p.c - f) % G == gc)
                        v = jnp.where(here, got[e, f], v)
            ordered.append(v)
    wq = over_cores(ring(jnp.concatenate(ordered, axis=0)))

    wo = rest[0]
    for f in range(1, G):
        other = lax.ppermute(
            rest[f],
            ("group", "seq"),
            [
                (p.flat(x, z, y, x), p.flat(x, z, y, (x + f) % G))
                for x in range(G)
                for z in range(S)
                for y in range(Y)
            ],
        )
        wo = jnp.where((p.c - p.x) % G == f, other, wo)
    wo = over_cores(ring(wo))

    times = lax.all_gather(timestep, "group", axis=0)
    mine = lax.dynamic_slice(times, (p.c, p.z), (1, 1)).reshape(1)
    mod = modulation(mine, w_mod)
    shift = mod[:, :width].reshape(blocks, 1, cols)
    scale = mod[:, width : 2 * width].reshape(blocks, 1, cols)
    gate = mod[:, 2 * width :]

    every = blocks * toks
    (merged,) = call(
        partial(merged_kernel, G, S, Y),
        [((every, cols), BF)],
        p.where,
        *hid,
        *skp,
        *ws,
        scratch=[pltpu.VMEM((every, 2 * width), BF), pltpu.VMEM((2 * width, cols), BF)],
        flops=4 * every * width * cols,
    )
    merged = [
        p.send(merged, lambda x, z, y, c, e=e, d=d: (x - d, z, y - e, c)) if e or d else merged
        for e in range(Y)
        for d in range(G)
    ]
    *parts, base = call(
        partial(attend_kernel, G, S, Y),
        [((G, toks, half), BF)] * blocks + [((blocks, toks, cols), BF)],
        p.where,
        *merged,
        shift,
        scale,
        *wq,
        *wo,
        scratch=[
            pltpu.VMEM((blocks, every, cols), BF),
            pltpu.VMEM((G, S, cols, 3 * per * HD), BF),
            pltpu.VMEM((S, every, HD), BF),
        ],
        flops=10 * every * width * cols,
    )
    parts = [
        p.send(parts[e * G + d], lambda x, z, y, c, e=e, d=d: (x + d, z, y + e, c))
        if e or d
        else parts[0]
        for e in range(Y)
        for d in range(G)
    ]
    result = call(partial(result_kernel, G, S, Y), [piece] * S, p.where, gate, base, *parts)
    result = [
        p.send(result[s], lambda x, z, y, c, s=s: (c, z - s, y, x)) for s in range(S)
    ]
    (out,) = call(partial(home_kernel, S), [((S, local, width), BF)], p.where, *result)
    return out


def solution(mesh):
    groups, n = mesh.shape["group"], mesh.shape["seq"]

    def per_device(*args):
        hidden, w_out = args[0], args[6]
        seqs, _, width = hidden.shape
        blocks = n // seqs
        fits = (
            n % seqs == 0
            and blocks % groups == 0
            and blocks == seqs
            and seqs % groups == 0
            and w_out.shape[0] == HD
            and width % blocks == 0
            and (width // blocks) % 16 == 0
        )
        return in_planes(groups, n, *args) if fits else gathered(*args)

    placed = (
        P("group", "seq", None),
        P("group", "seq", None),
        P("group"),
        P("seq", None),
        P(),
        P("seq", None),
        P("seq", None),
    )
    return jax.shard_map(
        per_device, mesh=mesh, in_specs=placed, out_specs=P("group", "seq", None), check_vma=False
    )
```

```python
import math
from functools import partial

import jax
import jax.numpy as jnp
from jax import lax
from jax.experimental import pallas as pl
from jax.experimental.pallas import tpu as pltpu
from jax.sharding import PartitionSpec as P

H = 16
HD = 88
TDIM = 256
BF = jnp.bfloat16
F32 = jnp.float32


def layer_norm(x):
    mean = jnp.mean(x, axis=-1, keepdims=True)
    var = jnp.mean((x - mean) ** 2, axis=-1, keepdims=True)
    return (x - mean) * lax.rsqrt(var + 1e-06)


def modulation(timestep, w_mod):
    half = TDIM // 2
    freqs = jnp.exp(-math.log(10000.0) * jnp.arange(half, dtype=F32) / half)
    angles = timestep.astype(F32)[:, None] * freqs[None, :]
    embed = jnp.concatenate([jnp.cos(angles), jnp.sin(angles)], axis=1)
    act = jax.nn.silu(embed).astype(BF)
    return jnp.dot(act, w_mod, preferred_element_type=F32)


def attend_pair(trio):
    qpair, kpair, vpair = trio
    scores = jnp.einsum("qd,kd->qk", qpair, kpair, preferred_element_type=F32)
    probs = jax.nn.softmax(scores, axis=-1).astype(BF)
    return jnp.dot(probs, vpair, preferred_element_type=F32).astype(BF)


def to_heads(x, seqs, local):
    return jnp.transpose(x, (0, 2, 1, 3)).reshape(seqs * H, local, HD)


def gathered(hidden, skip, timestep, w_skip, w_mod, w_qkv, w_out):
    seqs, local, width = hidden.shape
    tok_rows = seqs * local
    combined = jnp.concatenate([hidden, skip], axis=2).reshape(tok_rows, 2 * width)
    full_skip = lax.all_gather(w_skip, "seq", axis=0, tiled=True)
    merged = jnp.dot(combined, full_skip, preferred_element_type=F32).astype(BF)
    mod = modulation(timestep, w_mod)
    shift, scale, gate = (mod[:, :width], mod[:, width : 2 * width], mod[:, 2 * width :])
    base = merged.astype(F32).reshape(seqs, local, width)
    normed = (layer_norm(base) * (1.0 + scale[:, None, :]) + shift[:, None, :]).astype(BF)
    full_qkv = lax.all_gather(w_qkv, "seq", axis=0, tiled=True)
    qkv = jnp.dot(normed.reshape(tok_rows, width), full_qkv, preferred_element_type=F32)
    qkv = qkv.reshape(seqs, local, 3, H, HD)
    query = (layer_norm(qkv[:, :, 0]) * HD ** (-0.5)).astype(BF)
    key = layer_norm(qkv[:, :, 1]).astype(BF)
    value = qkv[:, :, 2].astype(BF)
    trio = [
        lax.all_to_all(to_heads(x, seqs, local), "seq", split_axis=0, concat_axis=1, tiled=True)
        for x in (query, key, value)
    ]
    attended = lax.map(attend_pair, tuple(trio))
    attended = lax.all_to_all(attended, "seq", split_axis=1, concat_axis=0, tiled=True)
    attended = jnp.transpose(attended.reshape(seqs, H, local, HD), (0, 2, 1, 3))
    full_out = lax.all_gather(w_out, "seq", axis=0, tiled=True)
    projected = jnp.dot(
        attended.reshape(tok_rows, width), full_out, preferred_element_type=F32
    ).reshape(seqs, local, width)
    return (base + gate[:, None, :] * projected).astype(BF)


class Place:
    def __init__(self, groups, n, seqs):
        self.G, self.S = groups, seqs
        self.Y = n // seqs // groups
        self.n = n
        g, j = lax.axis_index("group"), lax.axis_index("seq")
        self.x, self.z = g, j // (n // seqs)
        self.y, self.c = (j // groups) % self.Y, j % groups
        self.where = jnp.stack([self.x, self.z, self.y, self.c]).astype(jnp.int32)
        self.cores = [[k * groups + f for f in range(groups)] for k in range(n // groups)]
        self.column = [[k * n // seqs + i for k in range(seqs)] for i in range(n // seqs)]

    def send(self, value, to):
        pairs = []
        for x in range(self.G):
            for z in range(self.S):
                for y in range(self.Y):
                    for c in range(self.G):
                        tx, tz, ty, tc = to(x, z, y, c)
                        there = (tx % self.G, tz % self.S, ty % self.Y, tc % self.G)
                        pairs.append((self.flat(x, z, y, c), self.flat(*there)))
        return lax.ppermute(value, ("group", "seq"), pairs)

    def flat(self, x, z, y, c):
        return x * self.n + (z * self.Y + y) * self.G + c


def call(kernel, outs, where, *arrays, scratch=(), copies=0, flops=0, vmem_out=True, vmem_in=False):
    moved = sum(a.size * a.dtype.itemsize for a in arrays)
    space = pltpu.VMEM if vmem_in else pl.ANY
    where_out = pltpu.VMEM if vmem_out else pl.ANY
    sems = [pltpu.SemaphoreType.DMA((copies,))] if copies else []
    return pl.pallas_call(
        kernel,
        out_shape=[jax.ShapeDtypeStruct(s, d) for s, d in outs],
        in_specs=[pl.BlockSpec(memory_space=pltpu.SMEM)]
        + [pl.BlockSpec(memory_space=space)] * len(arrays),
        out_specs=[pl.BlockSpec(memory_space=where_out)] * len(outs),
        scratch_shapes=list(scratch) + sems,
        compiler_params=pltpu.CompilerParams(vmem_limit_bytes=40 * 2**20),
        cost_estimate=pl.CostEstimate(flops=flops, bytes_accessed=2 * moved, transcendentals=0),
    )(where, *arrays)


def copy_all(pairs, sems):
    copies = [pltpu.make_async_copy(a, b, sems.at[k]) for k, (a, b) in enumerate(pairs)]
    for copy in copies:
        copy.start()
    for copy in copies:
        copy.wait()


def pieces_kernel(S, where, hidden, skip, *refs):
    outs, sems = refs[:S], refs[S]
    z = where[1]
    local = hidden.shape[1]
    pairs = []
    for s in range(S):
        at = (z + s) % S
        pairs.append((hidden.at[at], outs[s].at[pl.ds(0, local)]))
        pairs.append((skip.at[at], outs[s].at[pl.ds(local, local)]))
    copy_all(pairs, sems)


def slices_kernel(G, S, Y, where, w_skip_any, w_qkv_any, w_out_any, *refs):
    outs, (w_skip, w_qkv, w_out, sems) = refs[:-4], refs[-4:]
    copy_all([(w_skip_any, w_skip), (w_qkv_any, w_qkv), (w_out_any, w_out)], sems)
    x, y, c = where[0], where[2], where[3]
    width = w_skip.shape[1]
    block, part, half = width // (G * Y), S // G * HD, width // G
    skips, qkvs, rest = outs[:Y], outs[Y : Y + Y * G], outs[Y + Y * G]
    for gx in range(G):
        for gy in range(Y):
            for e in range(Y):

                @pl.when((x == gx) & ((y + e) % Y == gy))
                def _():
                    b = gx * Y + gy
                    skips[e][...] = w_skip[:, b * block : (b + 1) * block]
                    for gc in range(G):
                        for f in range(G):

                            @pl.when((c + f) % G == gc)
                            def _():
                                for p in range(3):
                                    for t in range(S // G):
                                        head = ((gc * (S // G) + t) * Y + gy) * G + gx
                                        at = p * width + head * HD
                                        to = p * part + t * HD
                                        qkvs[e * G + f][:, to : to + HD] = w_qkv[:, at : at + HD]

    for gc in range(G):
        for f in range(G):

            @pl.when((c + f) % G == gc)
            def _():
                to = rest if f == 0 else qkvs[f]
                at = 0 if f == 0 else 3 * part
                to[:, at : at + half] = w_out[:, gc * half : (gc + 1) * half]


def join_kernel(S, where, *refs):
    rows = refs[0].shape[0]
    copy_all([(refs[s], refs[S].at[pl.ds(s * rows, rows)]) for s in range(S)], refs[S + 1])


def shards_kernel(G, S, Y, where, *refs):
    skips, qkvs, rest = refs[:Y], refs[Y : Y + Y * G], refs[Y + Y * G]
    ring, qkv, out = refs[Y + Y * G + 1 :]
    x, y, c = where[0], where[2], where[3]
    rows, part = skips[0].shape[0], S // G * HD
    for e in range(Y):
        ring[e * rows : (e + 1) * rows, :] = skips[e][...]
    for gy in range(Y):
        for gc in range(G):
            for e in range(Y):
                for f in range(G):

                    @pl.when(((y + Y - e) % Y == gy) & ((c + G - f) % G == gc))
                    def _():
                        at = (gy * G + gc) * HD
                        qkv[at : at + HD, :] = qkvs[e * G + f][:, : 3 * part]

    out[...] = rest[...]
    for f in range(1, G):

        @pl.when((c + G - f) % G == x)
        def _():
            out[...] = qkvs[f][:, 3 * part :]


def merged_kernel(G, S, Y, where, *refs):
    z, y = where[1], where[2]
    blocks = Y * G
    parts, weights, held = refs[:blocks], refs[blocks : blocks + S], refs[blocks + S]
    out, on, xs, ws, sems = refs[blocks + S + 1 :]
    width = parts[0].shape[1]
    local = parts[0].shape[0] // (2 * S)
    rows = weights[0].shape[1] // Y
    pairs = [(held, on)]
    for k in range(blocks):
        for s in range(S):
            for h in range(2):
                pairs.append(
                    (
                        parts[k].at[pl.ds((2 * s + h) * local, local)],
                        xs.at[pl.ds((k * S + s) * local, local), pl.ds(h * width, width)],
                    )
                )
    for s in range(S):
        for f in range(G):
            for e in range(Y):
                j = (((z + S - s) % S) * Y + (y + Y - e) % Y) * G + f
                at = pl.multiple_of(j * rows, 16)
                pairs.append((weights[s].at[f, pl.ds(e * rows, rows)], ws.at[pl.ds(at, rows)]))
    copy_all(pairs, sems)
    out[...] = jnp.dot(xs[...], ws[...], preferred_element_type=F32).astype(BF)


def norm88(v):
    mean = jnp.sum(v, axis=-1, keepdims=True) * (1.0 / HD)
    d = v - mean
    var = jnp.sum(d * d, axis=-1, keepdims=True) * (1.0 / HD)
    return d * lax.rsqrt(var + 1e-06)


def attend_kernel(G, S, Y, where, *refs):
    x, z, y = where[0], where[1], where[2]
    blocks = Y * G
    merged_any, (shift, scale) = refs[:blocks], refs[blocks : blocks + 2]
    wq_any, wo_any, refs = refs[blocks + 2], refs[blocks + 3 : blocks + 3 + S], refs[blocks + 3 + S :]
    outs, base, (merged, norm, shifts, scales, wq, wo, att, sems) = (
        refs[:blocks],
        refs[blocks],
        refs[blocks + 1 :],
    )
    rows, cols = merged_any[0].shape
    toks = rows // blocks
    width = cols * blocks

    pairs = [(shift, shifts), (scale, scales), (wq_any, wq)]
    for s in range(S):
        pairs.append((wo_any[s], wo.at[(z + S - s) % S]))
    for e in range(Y):
        for d in range(G):
            b = (x + d) % G * Y + (y + e) % Y
            for em in range(Y):
                for dm in range(G):
                    at = (((em - e) % Y) * G + (dm - d) % G) * toks
                    to = (em * G + dm) * toks
                    pairs.append(
                        (merged_any[e * G + d].at[pl.ds(at, toks)], merged.at[b, pl.ds(to, toks)])
                    )
    copy_all(pairs, sems)
    total = jnp.zeros((rows, 1), F32)
    wide = []
    for b in range(blocks):
        base[b] = merged[b, :toks, :]
        wide.append(merged[b].astype(F32))
        total = total + jnp.sum(wide[-1], axis=-1, keepdims=True)
    mean = total * (1.0 / width)
    square = jnp.zeros((rows, 1), F32)
    for m in wide:
        square = square + jnp.sum((m - mean) ** 2, axis=-1, keepdims=True)
    inv = lax.rsqrt(square * (1.0 / width) + 1e-06)
    for b in range(blocks):
        norm[b] = ((wide[b] - mean) * inv * (1.0 + scales[b]) + shifts[b]).astype(BF)
    per = S // G
    for f in range(G):
        qkv = jnp.dot(norm[0], wq[f, :cols], preferred_element_type=F32)
        for b in range(1, blocks):
            qkv = qkv + jnp.dot(
                norm[b], wq[f, b * cols : (b + 1) * cols], preferred_element_type=F32
            )
        for t in range(per):
            q, k, v = (qkv[:, (p * per + t) * HD : (p * per + t + 1) * HD] for p in range(3))
            q = (norm88(q) * HD ** (-0.5)).astype(BF)
            k = norm88(k).astype(BF)
            v = v.astype(BF)
            scores = lax.dot_general(q, k, (((1,), (1,)), ((), ())), preferred_element_type=F32)
            top = jnp.max(scores, axis=-1, keepdims=True)
            probs = jnp.exp(scores - top)
            probs = (probs / jnp.sum(probs, axis=-1, keepdims=True)).astype(BF)
            att[f * per + t] = jnp.dot(probs, v, preferred_element_type=F32).astype(BF)
    for f in range(G):
        acc = jnp.dot(att[0], wo[0, f], preferred_element_type=F32)
        for s in range(1, S):
            acc = acc + jnp.dot(att[s], wo[s, f], preferred_element_type=F32)
        acc = acc.astype(BF)
        for k in range(blocks):
            outs[k][f] = acc[k * toks : (k + 1) * toks, :]


def result_kernel(G, S, Y, where, gate, base, *refs):
    blocks = Y * G
    parts, outs = refs[:blocks], refs[blocks:]
    toks = base.shape[1]
    local = toks // S
    halves = []
    for h in range(G):
        acc = parts[0][h].astype(F32)
        for k in range(1, blocks):
            acc = acc + parts[k][h].astype(F32)
        halves.append(acc)
    projected = jnp.concatenate(halves, axis=1)
    merged = jnp.concatenate([base[b] for b in range(blocks)], axis=1).astype(F32)
    result = (merged + gate[...] * projected).astype(BF)
    for s in range(S):
        outs[s][...] = result[s * local : (s + 1) * local, :]


def home_kernel(S, where, *refs):
    z = where[1]
    copy_all([(refs[s], refs[S].at[(z + s) % S]) for s in range(S)], refs[S + 1])


def in_planes(groups, n, hidden, skip, timestep, w_skip, w_mod, w_qkv, w_out):
    S, local, width = hidden.shape
    p = Place(groups, n, S)
    G, Y = p.G, p.Y
    blocks = Y * G
    cols, half = width // blocks, width // G
    toks, rows = S * local, w_skip.shape[0]
    part = 3 * (S // G) * HD
    every = blocks * toks

    cut = call(
        partial(pieces_kernel, S),
        [((2 * local, width), BF)] * S,
        p.where,
        hidden,
        skip,
        copies=2 * S,
        vmem_out=False,
    )
    outs = [((rows, cols), BF)] * Y
    for e in range(Y):
        for f in range(G):
            outs.append(((HD, part + (half if f and not e else 0)), BF))
    outs.append(((HD, half), BF))
    slices = call(
        partial(slices_kernel, G, S, Y),
        outs,
        p.where,
        w_skip,
        w_qkv,
        w_out,
        scratch=[pltpu.VMEM(w.shape, BF) for w in (w_skip, w_qkv, w_out)],
        copies=3,
    )
    skips, qkvs, rest = list(slices[:Y]), list(slices[Y : Y + Y * G]), slices[Y + Y * G]

    cut = [cut[0]] + [
        p.send(cut[s], lambda x, z, y, c, s=s: (x, z + s, y, c)) for s in range(1, S)
    ]
    (joined,) = call(
        partial(join_kernel, S), [((2 * toks, width), BF)], p.where, *cut, copies=S, vmem_out=False
    )
    parts = [
        p.send(joined, lambda x, z, y, c, e=e, d=d: (c - d, z, y - e, x))
        for e in range(Y)
        for d in range(G)
    ]

    for e in range(1, Y):
        skips[e] = p.send(skips[e], lambda x, z, y, c, e=e: (x, z, y + e, c))
    for e in range(Y):
        for f in range(G):
            if e or f:
                qkvs[e * G + f] = p.send(
                    qkvs[e * G + f], lambda x, z, y, c, e=e, f=f: (x, z, y + e, c + f)
                )
    ring, wq, wo = call(
        partial(shards_kernel, G, S, Y),
        [((Y * rows, cols), BF), ((blocks * HD, part), BF), ((HD, half), BF)],
        p.where,
        *skips,
        *qkvs,
        rest,
        vmem_in=True,
    )

    def round_planes(value):
        held = [value]
        for _ in range(1, S):
            held.append(p.send(held[-1], lambda x, z, y, c: (x, z + 1, y, c)))
        return held

    def both_cores(value):
        return lax.all_gather(value, "seq", axis=0, axis_index_groups=p.cores)

    ws = [both_cores(v) for v in round_planes(ring)]
    wq = lax.all_gather(wq, "seq", axis=0, tiled=True, axis_index_groups=p.column)
    wq = both_cores(wq)

    times = p.send(timestep, lambda x, z, y, c: (c, z, y, x))
    mod = modulation(lax.dynamic_slice(times, (p.z,), (1,)), w_mod)
    shift = mod[:, :width].reshape(blocks, 1, cols)
    scale = mod[:, width : 2 * width].reshape(blocks, 1, cols)
    gate = mod[:, 2 * width :]

    merged, wo = call(
        partial(merged_kernel, G, S, Y),
        [((every, cols), BF), ((HD, half), BF)],
        p.where,
        *parts,
        *ws,
        wo,
        scratch=[pltpu.VMEM((every, 2 * width), BF), pltpu.VMEM((2 * width, cols), BF)],
        copies=1 + 2 * blocks * S + S * G * Y,
        flops=4 * every * width * cols,
    )
    wo = [both_cores(v) for v in round_planes(wo)]
    merged = [
        p.send(merged, lambda x, z, y, c, e=e, d=d: (x - d, z, y - e, c)) if e or d else merged
        for e in range(Y)
        for d in range(G)
    ]
    *parts, base = call(
        partial(attend_kernel, G, S, Y),
        [((G, toks, half), BF)] * blocks + [((blocks, toks, cols), BF)],
        p.where,
        *merged,
        shift,
        scale,
        wq,
        *wo,
        scratch=[
            pltpu.VMEM((blocks, every, cols), BF),
            pltpu.VMEM((blocks, every, cols), BF),
            pltpu.VMEM((blocks, 1, cols), F32),
            pltpu.VMEM((blocks, 1, cols), F32),
            pltpu.VMEM((G, width, part), BF),
            pltpu.VMEM((S, G, HD, half), BF),
            pltpu.VMEM((S, every, HD), BF),
        ],
        copies=3 + S + blocks * blocks,
        flops=10 * every * width * cols,
    )
    parts = [
        p.send(parts[e * G + d], lambda x, z, y, c, e=e, d=d: (x + d, z, y + e, c))
        if e or d
        else parts[0]
        for e in range(Y)
        for d in range(G)
    ]
    result = call(
        partial(result_kernel, G, S, Y),
        [((local, width), BF)] * S,
        p.where,
        gate,
        base,
        *parts,
        vmem_in=True,
    )
    result = [p.send(result[s], lambda x, z, y, c, s=s: (c, z - s, y, x)) for s in range(S)]
    (out,) = call(
        partial(home_kernel, S),
        [((S, local, width), BF)],
        p.where,
        *result,
        copies=S,
        vmem_out=False,
    )
    return out


def solution(mesh):
    groups, n = mesh.shape["group"], mesh.shape["seq"]

    def per_device(*args):
        hidden, w_out = args[0], args[6]
        seqs, _, width = hidden.shape
        blocks = n // seqs
        fits = (
            n % seqs == 0
            and blocks % groups == 0
            and blocks == seqs
            and seqs % groups == 0
            and w_out.shape[0] == HD
            and width % blocks == 0
            and (width // blocks) % 16 == 0
        )
        return in_planes(groups, n, *args) if fits else gathered(*args)

    placed = (
        P("group", "seq", None),
        P("group", "seq", None),
        P("group"),
        P("seq", None),
        P(),
        P("seq", None),
        P("seq", None),
    )
    return jax.shard_map(
        per_device, mesh=mesh, in_specs=placed, out_specs=P("group", "seq", None), check_vma=False
    )
```

```python
import math
from functools import partial

import jax
import jax.numpy as jnp
from jax import lax
from jax.experimental import pallas as pl
from jax.experimental.pallas import tpu as pltpu
from jax.sharding import PartitionSpec as P

H = 16
HD = 88
TDIM = 256
BF = jnp.bfloat16
F32 = jnp.float32


def layer_norm(x):
    mean = jnp.mean(x, axis=-1, keepdims=True)
    var = jnp.mean((x - mean) ** 2, axis=-1, keepdims=True)
    return (x - mean) * lax.rsqrt(var + 1e-06)


def modulation(timestep, w_mod):
    half = TDIM // 2
    freqs = jnp.exp(-math.log(10000.0) * jnp.arange(half, dtype=F32) / half)
    angles = timestep.astype(F32)[:, None] * freqs[None, :]
    embed = jnp.concatenate([jnp.cos(angles), jnp.sin(angles)], axis=1)
    act = jax.nn.silu(embed).astype(BF)
    return jnp.dot(act, w_mod, preferred_element_type=F32)


def attend_pair(trio):
    qpair, kpair, vpair = trio
    scores = jnp.einsum("qd,kd->qk", qpair, kpair, preferred_element_type=F32)
    probs = jax.nn.softmax(scores, axis=-1).astype(BF)
    return jnp.dot(probs, vpair, preferred_element_type=F32).astype(BF)


def to_heads(x, seqs, local):
    return jnp.transpose(x, (0, 2, 1, 3)).reshape(seqs * H, local, HD)


def gathered(hidden, skip, timestep, w_skip, w_mod, w_qkv, w_out):
    seqs, local, width = hidden.shape
    tok_rows = seqs * local
    combined = jnp.concatenate([hidden, skip], axis=2).reshape(tok_rows, 2 * width)
    full_skip = lax.all_gather(w_skip, "seq", axis=0, tiled=True)
    merged = jnp.dot(combined, full_skip, preferred_element_type=F32).astype(BF)
    mod = modulation(timestep, w_mod)
    shift, scale, gate = (mod[:, :width], mod[:, width : 2 * width], mod[:, 2 * width :])
    base = merged.astype(F32).reshape(seqs, local, width)
    normed = (layer_norm(base) * (1.0 + scale[:, None, :]) + shift[:, None, :]).astype(BF)
    full_qkv = lax.all_gather(w_qkv, "seq", axis=0, tiled=True)
    qkv = jnp.dot(normed.reshape(tok_rows, width), full_qkv, preferred_element_type=F32)
    qkv = qkv.reshape(seqs, local, 3, H, HD)
    query = (layer_norm(qkv[:, :, 0]) * HD ** (-0.5)).astype(BF)
    key = layer_norm(qkv[:, :, 1]).astype(BF)
    value = qkv[:, :, 2].astype(BF)
    trio = [
        lax.all_to_all(to_heads(x, seqs, local), "seq", split_axis=0, concat_axis=1, tiled=True)
        for x in (query, key, value)
    ]
    attended = lax.map(attend_pair, tuple(trio))
    attended = lax.all_to_all(attended, "seq", split_axis=1, concat_axis=0, tiled=True)
    attended = jnp.transpose(attended.reshape(seqs, H, local, HD), (0, 2, 1, 3))
    full_out = lax.all_gather(w_out, "seq", axis=0, tiled=True)
    projected = jnp.dot(
        attended.reshape(tok_rows, width), full_out, preferred_element_type=F32
    ).reshape(seqs, local, width)
    return (base + gate[:, None, :] * projected).astype(BF)


class Place:
    def __init__(self, groups, n, seqs):
        self.G, self.S = groups, seqs
        self.Y = n // seqs // groups
        self.n = n
        g, j = lax.axis_index("group"), lax.axis_index("seq")
        self.x, self.z = g, j // (n // seqs)
        self.y, self.c = (j // groups) % self.Y, j % groups
        self.where = jnp.stack([self.x, self.z, self.y, self.c]).astype(jnp.int32)
        self.cores = [[k * groups + f for f in range(groups)] for k in range(n // groups)]
        self.column = [[k * n // seqs + i for k in range(seqs)] for i in range(n // seqs)]

    def send(self, value, to):
        pairs = []
        for x in range(self.G):
            for z in range(self.S):
                for y in range(self.Y):
                    for c in range(self.G):
                        tx, tz, ty, tc = to(x, z, y, c)
                        there = (tx % self.G, tz % self.S, ty % self.Y, tc % self.G)
                        pairs.append((self.flat(x, z, y, c), self.flat(*there)))
        return lax.ppermute(value, ("group", "seq"), pairs)

    def flat(self, x, z, y, c):
        return x * self.n + (z * self.Y + y) * self.G + c


def call(kernel, outs, where, *arrays, scratch=(), copies=0, flops=0, fast=(), fast_in=False):
    moved = sum(a.size * a.dtype.itemsize for a in arrays)
    space = pltpu.VMEM if fast_in else pltpu.HBM
    sems = [pltpu.SemaphoreType.DMA((copies,))] if copies else []
    return pl.pallas_call(
        kernel,
        out_shape=[jax.ShapeDtypeStruct(s, BF) for s in outs],
        in_specs=[pl.BlockSpec(memory_space=pltpu.SMEM)]
        + [pl.BlockSpec(memory_space=space)] * len(arrays),
        out_specs=[
            pl.BlockSpec(memory_space=pltpu.VMEM if k in fast else pl.ANY)
            for k in range(len(outs))
        ],
        scratch_shapes=list(scratch) + sems,
        compiler_params=pltpu.CompilerParams(vmem_limit_bytes=40 * 2**20),
        cost_estimate=pl.CostEstimate(flops=flops, bytes_accessed=2 * moved, transcendentals=0),
    )(where, *arrays)


def after(value, *others):
    return lax.optimization_barrier((value, *others))[0]


def copy_all(pairs, sems):
    copies = [pltpu.make_async_copy(a, b, sems.at[k]) for k, (a, b) in enumerate(pairs)]
    for copy in copies:
        copy.start()
    for copy in copies:
        copy.wait()


def join_kernel(where, hidden, skip, out, sems):
    copy_all([(hidden, out.at[0]), (skip, out.at[1])], sems)


def cut_kernel(G, S, Y, where, w_skip_any, w_qkv_any, w_out_any, *refs):
    outs, (w_skip, w_qkv, w_out, sems) = refs[:-4], refs[-4:]
    skips, qkvs, rest = outs[0], outs[1 : 1 + Y * G], outs[1 + Y * G]
    copy_all([(w_skip_any, w_skip), (w_qkv_any, w_qkv), (w_out_any, w_out)], sems)
    x, y, c = where[0], where[2], where[3]
    width = w_skip.shape[1]
    block, part, half = width // (G * Y), 3 * (S // G) * HD, width // G
    rows = w_skip.shape[0]
    for gx in range(G):
        for gy in range(Y):
            for e in range(Y):

                @pl.when((x == gx) & ((y + e) % Y == gy))
                def _():
                    b = gx * Y + gy
                    if e == 0:
                        skips[...] = w_skip[:, b * block : (b + 1) * block]
                    else:
                        for r in range(rows // HD):
                            qkvs[e * G][:, part + r * block : part + (r + 1) * block] = w_skip[
                                r * HD : (r + 1) * HD, b * block : (b + 1) * block
                            ]
                    for gc in range(G):
                        for f in range(G):

                            @pl.when((c + f) % G == gc)
                            def _():
                                for p in range(3):
                                    for t in range(S // G):
                                        head = ((gc * (S // G) + t) * Y + gy) * G + gx
                                        at = p * width + head * HD
                                        to = (p * (S // G) + t) * HD
                                        qkvs[e * G + f][:, to : to + HD] = w_qkv[:, at : at + HD]

    for gc in range(G):
        for f in range(G):

            @pl.when((c + f) % G == gc)
            def _():
                to = rest if f == 0 else qkvs[f]
                at = 0 if f == 0 else part
                to[:, at : at + half] = w_out[:, gc * half : (gc + 1) * half]

def stack_kernel(where, *refs):
    *pieces, out, sems = refs
    copy_all([(v, out.at[s]) for s, v in enumerate(pieces)], sems)


def ring_kernel(Y, part, where, own, *refs):
    others, out = refs[:-1], refs[-1]
    y = where[2]
    rows, cols = own.shape

    def place(e):
        return pl.multiple_of((y + Y - e) % Y * rows, 16)

    out[pl.ds(place(0), rows), :] = own[...]
    for e in range(1, Y):
        v = others[e - 1]
        both = [v[:, part + r * cols : part + (r + 1) * cols] for r in range(rows // HD)]
        out[pl.ds(place(e), rows), :] = jnp.concatenate(both, axis=0)


def shards_kernel(G, S, Y, where, *refs):
    qkvs, rest = refs[: Y * G], refs[Y * G]
    qkv, out = refs[Y * G + 1 :]
    x, y, c = where[0], where[2], where[3]
    part = 3 * (S // G) * HD
    for gy in range(Y):
        for gc in range(G):
            for e in range(Y):
                for f in range(G):

                    @pl.when(((y + Y - e) % Y == gy) & ((c + G - f) % G == gc))
                    def _():
                        at = (gy * G + gc) * HD
                        qkv[at : at + HD, :] = qkvs[e * G + f][:, :part]

    out[...] = rest[...]
    for f in range(1, G):

        @pl.when((c + G - f) % G == x)
        def _():
            out[...] = qkvs[f][:, part:]


def merged_kernel(G, S, Y, where, *refs):
    z, c = where[1], where[3]
    blocks = Y * G
    parts, weights = refs[:blocks], refs[blocks : blocks + G * S]
    outs, (xs, ws, ms, sems) = refs[blocks + G * S : -4], refs[-4:]
    width = parts[0].shape[3]
    rows = weights[0].shape[0] // Y
    pairs = []
    for k in range(blocks):
        for h in range(2):
            pairs.append((parts[k].at[h], xs.at[k, :, :, pl.ds(h * width, width)]))
    for f in range(G):
        for s in range(S):
            for y in range(Y):
                to = ws.at[(z + S - s) % S, y, (c + G - f) % G]
                pairs.append((weights[f * S + s].at[pl.ds(y * rows, rows)], to))
    copy_all(pairs, sems)
    weight = ws[...].reshape(2 * width, ws.shape[-1])
    tokens = xs[...].reshape(-1, 2 * width)
    merged = jnp.dot(tokens, weight, preferred_element_type=F32).astype(BF)
    ms[...] = merged.reshape(ms.shape)
    for s in range(S):
        outs[s][...] = ms[:, (z + s) % S]


def norm88(v):
    mean = jnp.sum(v, axis=-1, keepdims=True) * (1.0 / HD)
    d = v - mean
    var = jnp.sum(d * d, axis=-1, keepdims=True) * (1.0 / HD)
    return d * lax.rsqrt(var + 1e-06)


def attend_kernel(G, S, Y, where, *refs):
    x, z, y, c = where[0], where[1], where[2], where[3]
    blocks = Y * G
    merged_any, (shift, scale) = refs[:blocks], refs[blocks : blocks + 2]
    refs = refs[blocks + 2 :]
    wq_any, wo_any, refs = refs[: G * S], refs[G * S : 2 * G * S], refs[2 * G * S :]
    outs, base, (merged, norm, shifts, scales, wq, wo, att, sems) = (
        refs[:blocks],
        refs[blocks],
        refs[blocks + 1 :],
    )
    cols = merged_any[0].shape[3]
    toks = S * merged_any[0].shape[2]
    rows = blocks * toks
    width = cols * blocks

    pairs = [(shift, shifts), (scale, scales)]
    for f in range(G):
        for s in range(S):
            pairs.append((wq_any[f * S + s], wq.at[(c + G - f) % G, (z + S - s) % S]))
        for s in range(S):
            pairs.append((wo_any[f * S + s], wo.at[(z + S - s) % S, (c + G - f) % G]))
    for e in range(Y):
        for d in range(G):
            b = (x + d) % G * Y + (y + e) % Y
            for em in range(Y):
                for dm in range(G):
                    at = (em - e) % Y * G + (dm - d) % G
                    pairs.append(
                        (merged_any[e * G + d].at[:, at], merged.at[b, em * G + dm])
                    )
    copy_all(pairs, sems)
    total = jnp.zeros((rows, 1), F32)
    wide = []
    for b in range(blocks):
        base[b] = merged[b, 0].reshape(toks, cols)
        wide.append(merged[b].reshape(rows, cols).astype(F32))
        total = total + jnp.sum(wide[-1], axis=-1, keepdims=True)
    mean = total * (1.0 / width)
    square = jnp.zeros((rows, 1), F32)
    for m in wide:
        square = square + jnp.sum((m - mean) ** 2, axis=-1, keepdims=True)
    inv = lax.rsqrt(square * (1.0 / width) + 1e-06)
    for b in range(blocks):
        norm[b] = ((wide[b] - mean) * inv * (1.0 + scales[b]) + shifts[b]).astype(BF)
    per = S // G
    for f in range(G):
        qkv = jnp.dot(norm[0], wq[f, 0], preferred_element_type=F32)
        for b in range(1, blocks):
            qkv = qkv + jnp.dot(norm[b], wq[f, b], preferred_element_type=F32)
        for t in range(per):
            q, k, v = (qkv[:, (p * per + t) * HD : (p * per + t + 1) * HD] for p in range(3))
            q = (norm88(q) * HD ** (-0.5)).astype(BF)
            k = norm88(k).astype(BF)
            v = v.astype(BF)
            scores = lax.dot_general(q, k, (((1,), (1,)), ((), ())), preferred_element_type=F32)
            top = jnp.max(scores, axis=-1, keepdims=True)
            probs = jnp.exp(scores - top)
            probs = (probs / jnp.sum(probs, axis=-1, keepdims=True)).astype(BF)
            att[f * per + t] = jnp.dot(probs, v, preferred_element_type=F32).astype(BF)
    for f in range(G):
        acc = jnp.dot(att[0], wo[0, f], preferred_element_type=F32)
        for s in range(1, S):
            acc = acc + jnp.dot(att[s], wo[s, f], preferred_element_type=F32)
        acc = acc.astype(BF)
        for k in range(blocks):
            outs[k][f] = acc[k * toks : (k + 1) * toks, :]


def result_kernel(G, S, Y, where, gate, base, *refs):
    blocks = Y * G
    parts, outs = refs[:blocks], refs[blocks:]
    toks = base.shape[1]
    local = toks // S
    halves = []
    for h in range(G):
        acc = parts[0][h].astype(F32)
        for k in range(1, blocks):
            acc = acc + parts[k][h].astype(F32)
        halves.append(acc)
    projected = jnp.concatenate(halves, axis=1)
    merged = jnp.concatenate([base[b] for b in range(blocks)], axis=1).astype(F32)
    result = (merged + gate[...] * projected).astype(BF)
    for s in range(S):
        outs[s][...] = result[s * local : (s + 1) * local, :]


def home_kernel(S, where, *refs):
    z = where[1]
    copy_all([(refs[s], refs[S].at[(z + s) % S]) for s in range(S)], refs[S + 1])


def in_planes(groups, n, hidden, skip, timestep, w_skip, w_mod, w_qkv, w_out):
    S, local, width = hidden.shape
    p = Place(groups, n, S)
    G, Y = p.G, p.Y
    blocks = Y * G
    cols, half = width // blocks, width // G
    toks, rows = S * local, w_skip.shape[0]
    part = 3 * (S // G) * HD
    every = blocks * toks

    def swap(value, e, f):
        return p.send(value, lambda x, z, y, c: (x, z, y + e, c + f))

    (joined,) = call(
        join_kernel, [(2, S, local, width)], p.where, hidden, skip, copies=2
    )
    outs = [(rows, cols)]
    for e in range(Y):
        for f in range(G):
            more = (half if f and not e else 0) + (2 * cols if e and not f else 0)
            outs.append((HD, part + more))
    outs.append((HD, half))
    skips, *qkvs, rest = call(
        partial(cut_kernel, G, S, Y),
        outs,
        p.where,
        w_skip,
        w_qkv,
        w_out,
        scratch=[pltpu.VMEM(w.shape, BF) for w in (w_skip, w_qkv, w_out)],
        copies=3,
        fast=range(len(outs)),
    )
    own = qkvs[0]
    qkvs = [swap(qkvs[e * G + f], e, f) if e or f else own for e in range(Y) for f in range(G)]
    parts = []
    for e in range(Y):
        for d in range(G):
            value = joined if len(parts) < 2 else after(joined, qkvs[G], qkvs[len(parts)])
            parts.append(p.send(value, lambda x, z, y, c, e=e, d=d: (c - d, z, y - e, x)))

    def step(value):
        return p.send(value, lambda x, z, y, c: (x, z + 1, y, c))

    def over_cores(held):
        return held + [swap(v, 0, f) for f in range(1, G) for v in held]

    (ring,) = call(
        partial(ring_kernel, Y, part),
        [(Y * rows, cols)],
        p.where,
        skips,
        *[qkvs[e * G] for e in range(1, Y)],
        fast=[0],
        fast_in=True,
    )
    wq, wo = call(
        partial(shards_kernel, G, S, Y),
        [(blocks * HD, part), (HD, half)],
        p.where,
        *qkvs,
        rest,
        fast=[0, 1],
        fast_in=True,
    )
    ws = [ring]
    for _ in range(1, S):
        ws.append(step(ws[-1]))
    wq = [after(wq, ws[2])]
    for _ in range(1, S):
        wq.append(step(wq[-1]))
    wo = [after(wo, wq[2])]
    for _ in range(1, S):
        wo.append(step(wo[-1]))
    ws, wq, wo = over_cores(ws), over_cores(wq), over_cores(wo)

    times = p.send(timestep, lambda x, z, y, c: (c, z, y, x))
    mod = modulation(lax.dynamic_slice(times, (p.z,), (1,)), w_mod)
    shift = mod[:, :width].reshape(blocks, 1, cols)
    scale = mod[:, width : 2 * width].reshape(blocks, 1, cols)
    gate = mod[:, 2 * width :]
    parts[0] = after(parts[0], mod)

    pieces = call(
        partial(merged_kernel, G, S, Y),
        [(blocks, local, cols)] * S,
        p.where,
        *parts,
        *ws,
        scratch=[
            pltpu.VMEM((blocks, S, local, 2 * width), BF),
            pltpu.VMEM((S, Y, G, rows, cols), BF),
            pltpu.VMEM((blocks, S, local, cols), BF),
        ],
        copies=2 * blocks + S * G * Y,
        flops=4 * every * width * cols,
        fast=range(S),
    )
    pieces = [pieces[0]] + [
        p.send(pieces[s], lambda x, z, y, c, s=s: (x, z + s, y, c)) for s in range(1, S)
    ]
    (merged,) = call(stack_kernel, [(S, blocks, local, cols)], p.where, *pieces, copies=S)
    merged = [
        p.send(merged, lambda x, z, y, c, e=e, d=d: (x - d, z, y - e, c)) if e or d else merged
        for e in range(Y)
        for d in range(G)
    ]
    *parts, base = call(
        partial(attend_kernel, G, S, Y),
        [(G, toks, half)] * blocks + [(blocks, toks, cols)],
        p.where,
        *merged,
        shift,
        scale,
        *wq,
        *wo,
        scratch=[
            pltpu.VMEM((blocks, blocks, S, local, cols), BF),
            pltpu.VMEM((blocks, every, cols), BF),
            pltpu.VMEM((blocks, 1, cols), F32),
            pltpu.VMEM((blocks, 1, cols), F32),
            pltpu.VMEM((G, S, cols, part), BF),
            pltpu.VMEM((S, G, HD, half), BF),
            pltpu.VMEM((S, every, HD), BF),
        ],
        copies=2 + 2 * G * S + blocks * blocks,
        flops=10 * every * width * cols,
        fast=range(blocks + 1),
    )
    parts = [
        p.send(parts[e * G + d], lambda x, z, y, c, e=e, d=d: (x + d, z, y + e, c))
        if e or d
        else parts[0]
        for e in range(Y)
        for d in range(G)
    ]
    result = call(
        partial(result_kernel, G, S, Y),
        [(local, width)] * S,
        p.where,
        gate,
        base,
        *parts,
        fast=range(S),
        fast_in=True,
    )
    result = [p.send(result[s], lambda x, z, y, c, s=s: (c, z - s, y, x)) for s in range(S)]
    (out,) = call(
        partial(home_kernel, S), [(S, local, width)], p.where, *result, copies=S
    )
    return out


def solution(mesh):
    groups, n = mesh.shape["group"], mesh.shape["seq"]

    def per_device(*args):
        hidden, w_out = args[0], args[6]
        seqs, _, width = hidden.shape
        blocks = n // seqs
        fits = (
            n % seqs == 0
            and blocks % groups == 0
            and blocks == seqs
            and seqs % groups == 0
            and w_out.shape[0] == HD
            and width % blocks == 0
            and (width // blocks) % 16 == 0
        )
        return in_planes(groups, n, *args) if fits else gathered(*args)

    placed = (
        P("group", "seq", None),
        P("group", "seq", None),
        P("group"),
        P("seq", None),
        P(),
        P("seq", None),
        P("seq", None),
    )
    return jax.shard_map(
        per_device, mesh=mesh, in_specs=placed, out_specs=P("group", "seq", None), check_vma=False
    )
```

```python
import math
from functools import partial

import jax
import jax.numpy as jnp
from jax import lax
from jax.experimental import pallas as pl
from jax.experimental.pallas import tpu as pltpu
from jax.sharding import PartitionSpec as P

H = 16
HD = 88
TDIM = 256
BF = jnp.bfloat16
F32 = jnp.float32


def layer_norm(x):
    mean = jnp.mean(x, axis=-1, keepdims=True)
    var = jnp.mean((x - mean) ** 2, axis=-1, keepdims=True)
    return (x - mean) * lax.rsqrt(var + 1e-06)


def modulation(timestep, w_mod):
    half = TDIM // 2
    freqs = jnp.exp(-math.log(10000.0) * jnp.arange(half, dtype=F32) / half)
    angles = timestep.astype(F32)[:, None] * freqs[None, :]
    embed = jnp.concatenate([jnp.cos(angles), jnp.sin(angles)], axis=1)
    act = jax.nn.silu(embed).astype(BF)
    return jnp.dot(act, w_mod, preferred_element_type=F32)


def attend_pair(trio):
    qpair, kpair, vpair = trio
    scores = jnp.einsum("qd,kd->qk", qpair, kpair, preferred_element_type=F32)
    probs = jax.nn.softmax(scores, axis=-1).astype(BF)
    return jnp.dot(probs, vpair, preferred_element_type=F32).astype(BF)


def to_heads(x, seqs, local):
    return jnp.transpose(x, (0, 2, 1, 3)).reshape(seqs * H, local, HD)


def gathered(hidden, skip, timestep, w_skip, w_mod, w_qkv, w_out):
    seqs, local, width = hidden.shape
    tok_rows = seqs * local
    combined = jnp.concatenate([hidden, skip], axis=2).reshape(tok_rows, 2 * width)
    full_skip = lax.all_gather(w_skip, "seq", axis=0, tiled=True)
    merged = jnp.dot(combined, full_skip, preferred_element_type=F32).astype(BF)
    mod = modulation(timestep, w_mod)
    shift, scale, gate = (mod[:, :width], mod[:, width : 2 * width], mod[:, 2 * width :])
    base = merged.astype(F32).reshape(seqs, local, width)
    normed = (layer_norm(base) * (1.0 + scale[:, None, :]) + shift[:, None, :]).astype(BF)
    full_qkv = lax.all_gather(w_qkv, "seq", axis=0, tiled=True)
    qkv = jnp.dot(normed.reshape(tok_rows, width), full_qkv, preferred_element_type=F32)
    qkv = qkv.reshape(seqs, local, 3, H, HD)
    query = (layer_norm(qkv[:, :, 0]) * HD ** (-0.5)).astype(BF)
    key = layer_norm(qkv[:, :, 1]).astype(BF)
    value = qkv[:, :, 2].astype(BF)
    trio = [
        lax.all_to_all(to_heads(x, seqs, local), "seq", split_axis=0, concat_axis=1, tiled=True)
        for x in (query, key, value)
    ]
    attended = lax.map(attend_pair, tuple(trio))
    attended = lax.all_to_all(attended, "seq", split_axis=1, concat_axis=0, tiled=True)
    attended = jnp.transpose(attended.reshape(seqs, H, local, HD), (0, 2, 1, 3))
    full_out = lax.all_gather(w_out, "seq", axis=0, tiled=True)
    projected = jnp.dot(
        attended.reshape(tok_rows, width), full_out, preferred_element_type=F32
    ).reshape(seqs, local, width)
    return (base + gate[:, None, :] * projected).astype(BF)


class Place:
    def __init__(self, groups, n, seqs):
        self.G, self.S = groups, seqs
        self.Y = n // seqs // groups
        self.n = n
        g, j = lax.axis_index("group"), lax.axis_index("seq")
        self.x, self.z = g, j // (n // seqs)
        self.y, self.c = (j // groups) % self.Y, j % groups
        self.where = jnp.stack([self.x, self.z, self.y, self.c]).astype(jnp.int32)
        self.cores = [[k * groups + f for f in range(groups)] for k in range(n // groups)]
        self.column = [[k * n // seqs + i for k in range(seqs)] for i in range(n // seqs)]

    def send(self, value, to):
        pairs = []
        for x in range(self.G):
            for z in range(self.S):
                for y in range(self.Y):
                    for c in range(self.G):
                        tx, tz, ty, tc = to(x, z, y, c)
                        there = (tx % self.G, tz % self.S, ty % self.Y, tc % self.G)
                        pairs.append((self.flat(x, z, y, c), self.flat(*there)))
        return lax.ppermute(value, ("group", "seq"), pairs)

    def flat(self, x, z, y, c):
        return x * self.n + (z * self.Y + y) * self.G + c


def call(kernel, outs, where, *arrays, scratch=(), copies=0, flops=0, fast=(), fast_in=False, still=False):
    moved = sum(a.size * a.dtype.itemsize for a in arrays)
    space = pltpu.VMEM if fast_in else pltpu.HBM
    sems = [pltpu.SemaphoreType.DMA((copies,))] if copies else []
    return pl.pallas_call(
        kernel,
        out_shape=[jax.ShapeDtypeStruct(s, BF) for s in outs],
        in_specs=[pl.BlockSpec(memory_space=pltpu.SMEM)]
        + [pl.BlockSpec(memory_space=space)] * len(arrays),
        out_specs=[
            pl.BlockSpec(memory_space=pltpu.VMEM if k in fast else pl.ANY)
            for k in range(len(outs))
        ],
        scratch_shapes=list(scratch) + sems,
        compiler_params=pltpu.CompilerParams(vmem_limit_bytes=40 * 2**20),
        cost_estimate=pl.CostEstimate(flops=flops, bytes_accessed=2 * moved, transcendentals=0),
    )(where, *(pltpu.with_memory_space_constraint(a, pltpu.HBM) if still else a for a in arrays))


def after(value, *others):
    return lax.optimization_barrier((value, *others))[0]


def copy_all(pairs, sems):
    copies = [pltpu.make_async_copy(a, b, sems.at[k]) for k, (a, b) in enumerate(pairs)]
    for copy in copies:
        copy.start()
    for copy in copies:
        copy.wait()


def join_kernel(where, hidden, skip, out, sems):
    copy_all([(hidden, out.at[0]), (skip, out.at[1])], sems)


def cut_kernel(G, S, Y, where, w_skip_any, w_qkv_any, w_out_any, *refs):
    outs, (w_skip, w_qkv, w_out, sems) = refs[:-4], refs[-4:]
    skips, qkvs, rest = outs[0], outs[1 : 1 + Y * G], outs[1 + Y * G]
    copy_all([(w_skip_any, w_skip), (w_qkv_any, w_qkv), (w_out_any, w_out)], sems)
    x, y, c = where[0], where[2], where[3]
    width = w_skip.shape[1]
    block, part, half = width // (G * Y), 3 * (S // G) * HD, width // G
    rows = w_skip.shape[0]
    for gx in range(G):
        for gy in range(Y):
            for e in range(Y):

                @pl.when((x == gx) & ((y + e) % Y == gy))
                def _():
                    b = gx * Y + gy
                    if e == 0:
                        skips[...] = w_skip[:, b * block : (b + 1) * block]
                    else:
                        for r in range(rows // HD):
                            qkvs[e * G][:, part + r * block : part + (r + 1) * block] = w_skip[
                                r * HD : (r + 1) * HD, b * block : (b + 1) * block
                            ]
                    for gc in range(G):
                        for f in range(G):

                            @pl.when((c + f) % G == gc)
                            def _():
                                for p in range(3):
                                    for t in range(S // G):
                                        head = ((gc * (S // G) + t) * Y + gy) * G + gx
                                        at = p * width + head * HD
                                        to = (p * (S // G) + t) * HD
                                        qkvs[e * G + f][:, to : to + HD] = w_qkv[:, at : at + HD]

    for gc in range(G):
        for f in range(G):

            @pl.when((c + f) % G == gc)
            def _():
                to = rest if f == 0 else qkvs[f]
                at = 0 if f == 0 else part
                to[:, at : at + half] = w_out[:, gc * half : (gc + 1) * half]

def stack_kernel(where, *refs):
    *pieces, out, sems = refs
    copy_all([(v, out.at[s]) for s, v in enumerate(pieces)], sems)


def ring_kernel(Y, part, where, own, *refs):
    others, out = refs[:-1], refs[-1]
    y = where[2]
    rows, cols = own.shape

    def place(e):
        return pl.multiple_of((y + Y - e) % Y * rows, 16)

    out[pl.ds(place(0), rows), :] = own[...]
    for e in range(1, Y):
        v = others[e - 1]
        both = [v[:, part + r * cols : part + (r + 1) * cols] for r in range(rows // HD)]
        out[pl.ds(place(e), rows), :] = jnp.concatenate(both, axis=0)


def shards_kernel(G, S, Y, where, *refs):
    qkvs, rest = refs[: Y * G], refs[Y * G]
    qkv, out = refs[Y * G + 1 :]
    x, y, c = where[0], where[2], where[3]
    part = 3 * (S // G) * HD
    for gy in range(Y):
        for gc in range(G):
            for e in range(Y):
                for f in range(G):

                    @pl.when(((y + Y - e) % Y == gy) & ((c + G - f) % G == gc))
                    def _():
                        at = (gy * G + gc) * HD
                        qkv[at : at + HD, :] = qkvs[e * G + f][:, :part]

    out[...] = rest[...]
    for f in range(1, G):

        @pl.when((c + G - f) % G == x)
        def _():
            out[...] = qkvs[f][:, part:]


def merged_kernel(G, S, Y, where, *refs):
    z, c = where[1], where[3]
    blocks = Y * G
    parts, weights = refs[:blocks], refs[blocks : blocks + G * S]
    outs, (xs, ws, ms, sems) = refs[blocks + G * S : -4], refs[-4:]
    width = parts[0].shape[3]
    rows = weights[0].shape[0] // Y
    pairs = []
    for k in range(blocks):
        for h in range(2):
            pairs.append((parts[k].at[h], xs.at[k, :, :, pl.ds(h * width, width)]))
    for f in range(G):
        for s in range(S):
            for y in range(Y):
                to = ws.at[(z + S - s) % S, y, (c + G - f) % G]
                pairs.append((weights[f * S + s].at[pl.ds(y * rows, rows)], to))
    copy_all(pairs, sems)
    weight = ws[...].reshape(2 * width, ws.shape[-1])
    tokens = xs[...].reshape(-1, 2 * width)
    merged = jnp.dot(tokens, weight, preferred_element_type=F32).astype(BF)
    ms[...] = merged.reshape(ms.shape)
    for s in range(S):
        outs[s][...] = ms[:, (z + s) % S]


def norm88(v):
    mean = jnp.sum(v, axis=-1, keepdims=True) * (1.0 / HD)
    d = v - mean
    var = jnp.sum(d * d, axis=-1, keepdims=True) * (1.0 / HD)
    return d * lax.rsqrt(var + 1e-06)


def attend_kernel(G, S, Y, where, *refs):
    x, z, y, c = where[0], where[1], where[2], where[3]
    blocks = Y * G
    merged_any, (shift, scale) = refs[:blocks], refs[blocks : blocks + 2]
    refs = refs[blocks + 2 :]
    wq_any, wo_any, refs = refs[: G * S], refs[G * S : 2 * G * S], refs[2 * G * S :]
    outs, base, (merged, norm, shifts, scales, wq, wo, att, sems) = (
        refs[:blocks],
        refs[blocks],
        refs[blocks + 1 :],
    )
    cols = merged_any[0].shape[3]
    toks = S * merged_any[0].shape[2]
    rows = blocks * toks
    width = cols * blocks

    pairs = [(shift, shifts), (scale, scales)]
    for f in range(G):
        for s in range(S):
            pairs.append((wq_any[f * S + s], wq.at[(c + G - f) % G, (z + S - s) % S]))
        for s in range(S):
            pairs.append((wo_any[f * S + s], wo.at[(z + S - s) % S, (c + G - f) % G]))
    for e in range(Y):
        for d in range(G):
            b = (x + d) % G * Y + (y + e) % Y
            for em in range(Y):
                for dm in range(G):
                    at = (em - e) % Y * G + (dm - d) % G
                    pairs.append(
                        (merged_any[e * G + d].at[:, at], merged.at[b, em * G + dm])
                    )
    copy_all(pairs, sems)
    total = jnp.zeros((rows, 1), F32)
    wide = []
    for b in range(blocks):
        base[b] = merged[b, 0].reshape(toks, cols)
        wide.append(merged[b].reshape(rows, cols).astype(F32))
        total = total + jnp.sum(wide[-1], axis=-1, keepdims=True)
    mean = total * (1.0 / width)
    square = jnp.zeros((rows, 1), F32)
    for m in wide:
        square = square + jnp.sum((m - mean) ** 2, axis=-1, keepdims=True)
    inv = lax.rsqrt(square * (1.0 / width) + 1e-06)
    for b in range(blocks):
        norm[b] = ((wide[b] - mean) * inv * (1.0 + scales[b]) + shifts[b]).astype(BF)
    per = S // G
    for f in range(G):
        qkv = jnp.dot(norm[0], wq[f, 0], preferred_element_type=F32)
        for b in range(1, blocks):
            qkv = qkv + jnp.dot(norm[b], wq[f, b], preferred_element_type=F32)
        for t in range(per):
            q, k, v = (qkv[:, (p * per + t) * HD : (p * per + t + 1) * HD] for p in range(3))
            q = (norm88(q) * HD ** (-0.5)).astype(BF)
            k = norm88(k).astype(BF)
            v = v.astype(BF)
            scores = lax.dot_general(q, k, (((1,), (1,)), ((), ())), preferred_element_type=F32)
            top = jnp.max(scores, axis=-1, keepdims=True)
            probs = jnp.exp(scores - top)
            probs = (probs / jnp.sum(probs, axis=-1, keepdims=True)).astype(BF)
            att[f * per + t] = jnp.dot(probs, v, preferred_element_type=F32).astype(BF)
    for f in range(G):
        acc = jnp.dot(att[0], wo[0, f], preferred_element_type=F32)
        for s in range(1, S):
            acc = acc + jnp.dot(att[s], wo[s, f], preferred_element_type=F32)
        acc = acc.astype(BF)
        for k in range(blocks):
            outs[k][f] = acc[k * toks : (k + 1) * toks, :]


def result_kernel(G, S, Y, where, gate, base, *refs):
    blocks = Y * G
    parts, outs = refs[:blocks], refs[blocks:]
    toks = base.shape[1]
    local = toks // S
    halves = []
    for h in range(G):
        acc = parts[0][h].astype(F32)
        for k in range(1, blocks):
            acc = acc + parts[k][h].astype(F32)
        halves.append(acc)
    projected = jnp.concatenate(halves, axis=1)
    merged = jnp.concatenate([base[b] for b in range(blocks)], axis=1).astype(F32)
    result = (merged + gate[...] * projected).astype(BF)
    for s in range(S):
        outs[s][...] = result[s * local : (s + 1) * local, :]


def home_kernel(S, where, *refs):
    z = where[1]
    copy_all([(refs[s], refs[S].at[(z + s) % S]) for s in range(S)], refs[S + 1])


def in_planes(groups, n, hidden, skip, timestep, w_skip, w_mod, w_qkv, w_out):
    S, local, width = hidden.shape
    p = Place(groups, n, S)
    G, Y = p.G, p.Y
    blocks = Y * G
    cols, half = width // blocks, width // G
    toks, rows = S * local, w_skip.shape[0]
    part = 3 * (S // G) * HD
    every = blocks * toks

    def swap(value, e, f):
        return p.send(value, lambda x, z, y, c: (x, z, y + e, c + f))

    outs = [(rows, cols)]
    for e in range(Y):
        for f in range(G):
            more = (half if f and not e else 0) + (2 * cols if e and not f else 0)
            outs.append((HD, part + more))
    outs.append((HD, half))
    skips, *qkvs, rest = call(
        partial(cut_kernel, G, S, Y),
        outs,
        p.where,
        w_skip,
        w_qkv,
        w_out,
        scratch=[pltpu.VMEM(w.shape, BF) for w in (w_skip, w_qkv, w_out)],
        copies=3,
        fast=range(len(outs)),
        still=True,
    )
    (joined,) = call(
        join_kernel, [(2, S, local, width)], p.where, hidden, skip, copies=2, fast=[0], still=True
    )
    own = qkvs[0]
    parts = [
        p.send(joined, lambda x, z, y, c, e=e, d=d: (c - d, z, y - e, x))
        for e in range(Y)
        for d in range(G)
    ]
    for e in range(Y):
        for f in range(G):
            if f:
                qkvs[e * G + f] = swap(after(qkvs[e * G + f], *parts[:1]), e, f)
            elif e:
                qkvs[e * G] = swap(qkvs[e * G], e, 0)

    def step(value):
        return p.send(value, lambda x, z, y, c: (x, z + 1, y, c))

    def over_cores(held):
        return held + [swap(v, 0, f) for f in range(1, G) for v in held]

    (ring,) = call(
        partial(ring_kernel, Y, part),
        [(Y * rows, cols)],
        p.where,
        skips,
        *[qkvs[e * G] for e in range(1, Y)],
        fast=[0],
        fast_in=True,
    )
    wq, wo = call(
        partial(shards_kernel, G, S, Y),
        [(blocks * HD, part), (HD, half)],
        p.where,
        *qkvs,
        rest,
        fast=[0, 1],
        fast_in=True,
    )
    ws = [ring]
    ws.append(step(ring))
    ws.append(step(after(ws[1], *parts[:G])))
    ws.append(step(after(ws[2], *parts[G:])))
    wq = [after(wq, ws[2])]
    for _ in range(1, S):
        wq.append(step(wq[-1]))
    wo = [after(wo, ws[2])]
    for _ in range(1, S):
        wo.append(step(wo[-1]))
    ws, wq, wo = over_cores(ws), over_cores(wq), over_cores(wo)

    times = p.send(timestep, lambda x, z, y, c: (c, z, y, x))
    mod = modulation(lax.dynamic_slice(times, (p.z,), (1,)), w_mod)
    shift = mod[:, :width].reshape(blocks, 1, cols)
    scale = mod[:, width : 2 * width].reshape(blocks, 1, cols)
    gate = mod[:, 2 * width :]
    parts[0] = after(parts[0], mod)

    pieces = call(
        partial(merged_kernel, G, S, Y),
        [(blocks, local, cols)] * S,
        p.where,
        *parts,
        *ws,
        scratch=[
            pltpu.VMEM((blocks, S, local, 2 * width), BF),
            pltpu.VMEM((S, Y, G, rows, cols), BF),
            pltpu.VMEM((blocks, S, local, cols), BF),
        ],
        copies=2 * blocks + S * G * Y,
        flops=4 * every * width * cols,
        still=True,
        fast=range(S),
    )
    pieces = [pieces[0]] + [
        p.send(pieces[s], lambda x, z, y, c, s=s: (x, z + s, y, c)) for s in range(1, S)
    ]
    (merged,) = call(stack_kernel, [(S, blocks, local, cols)], p.where, *pieces, copies=S)
    merged = [
        p.send(merged, lambda x, z, y, c, e=e, d=d: (x - d, z, y - e, c)) if e or d else merged
        for e in range(Y)
        for d in range(G)
    ]
    *parts, base = call(
        partial(attend_kernel, G, S, Y),
        [(G, toks, half)] * blocks + [(blocks, toks, cols)],
        p.where,
        *merged,
        shift,
        scale,
        *wq,
        *wo,
        scratch=[
            pltpu.VMEM((blocks, blocks, S, local, cols), BF),
            pltpu.VMEM((blocks, every, cols), BF),
            pltpu.VMEM((blocks, 1, cols), F32),
            pltpu.VMEM((blocks, 1, cols), F32),
            pltpu.VMEM((G, S, cols, part), BF),
            pltpu.VMEM((S, G, HD, half), BF),
            pltpu.VMEM((S, every, HD), BF),
        ],
        copies=2 + 2 * G * S + blocks * blocks,
        flops=10 * every * width * cols,
        still=True,
        fast=range(blocks + 1),
    )
    parts = [
        p.send(parts[e * G + d], lambda x, z, y, c, e=e, d=d: (x + d, z, y + e, c))
        if e or d
        else parts[0]
        for e in range(Y)
        for d in range(G)
    ]
    result = call(
        partial(result_kernel, G, S, Y),
        [(local, width)] * S,
        p.where,
        gate,
        base,
        *parts,
        fast=range(S),
        fast_in=True,
    )
    result = [p.send(result[s], lambda x, z, y, c, s=s: (c, z - s, y, x)) for s in range(S)]
    (out,) = call(
        partial(home_kernel, S), [(S, local, width)], p.where, *result, copies=S
    )
    return out


def solution(mesh):
    groups, n = mesh.shape["group"], mesh.shape["seq"]

    def per_device(*args):
        hidden, w_out = args[0], args[6]
        seqs, _, width = hidden.shape
        blocks = n // seqs
        fits = (
            n % seqs == 0
            and blocks % groups == 0
            and blocks == seqs
            and seqs % groups == 0
            and w_out.shape[0] == HD
            and width % blocks == 0
            and (width // blocks) % 16 == 0
        )
        return in_planes(groups, n, *args) if fits else gathered(*args)

    placed = (
        P("group", "seq", None),
        P("group", "seq", None),
        P("group"),
        P("seq", None),
        P(),
        P("seq", None),
        P("seq", None),
    )
    return jax.shard_map(
        per_device, mesh=mesh, in_specs=placed, out_specs=P("group", "seq", None), check_vma=False
    )
```

```python
import math
from functools import partial

import jax
import jax.numpy as jnp
from jax import lax
from jax.experimental import pallas as pl
from jax.experimental.pallas import tpu as pltpu
from jax.sharding import PartitionSpec as P

H = 16
HD = 88
TDIM = 256
BF = jnp.bfloat16
F32 = jnp.float32


def layer_norm(x):
    mean = jnp.mean(x, axis=-1, keepdims=True)
    var = jnp.mean((x - mean) ** 2, axis=-1, keepdims=True)
    return (x - mean) * lax.rsqrt(var + 1e-06)


def modulation(timestep, w_mod):
    half = TDIM // 2
    freqs = jnp.exp(-math.log(10000.0) * jnp.arange(half, dtype=F32) / half)
    angles = timestep.astype(F32)[:, None] * freqs[None, :]
    embed = jnp.concatenate([jnp.cos(angles), jnp.sin(angles)], axis=1)
    act = jax.nn.silu(embed).astype(BF)
    return jnp.dot(act, w_mod, preferred_element_type=F32)


def attend_pair(trio):
    qpair, kpair, vpair = trio
    scores = jnp.einsum("qd,kd->qk", qpair, kpair, preferred_element_type=F32)
    probs = jax.nn.softmax(scores, axis=-1).astype(BF)
    return jnp.dot(probs, vpair, preferred_element_type=F32).astype(BF)


def to_heads(x, seqs, local):
    return jnp.transpose(x, (0, 2, 1, 3)).reshape(seqs * H, local, HD)


def gathered(hidden, skip, timestep, w_skip, w_mod, w_qkv, w_out):
    seqs, local, width = hidden.shape
    tok_rows = seqs * local
    combined = jnp.concatenate([hidden, skip], axis=2).reshape(tok_rows, 2 * width)
    full_skip = lax.all_gather(w_skip, "seq", axis=0, tiled=True)
    merged = jnp.dot(combined, full_skip, preferred_element_type=F32).astype(BF)
    mod = modulation(timestep, w_mod)
    shift, scale, gate = (mod[:, :width], mod[:, width : 2 * width], mod[:, 2 * width :])
    base = merged.astype(F32).reshape(seqs, local, width)
    normed = (layer_norm(base) * (1.0 + scale[:, None, :]) + shift[:, None, :]).astype(BF)
    full_qkv = lax.all_gather(w_qkv, "seq", axis=0, tiled=True)
    qkv = jnp.dot(normed.reshape(tok_rows, width), full_qkv, preferred_element_type=F32)
    qkv = qkv.reshape(seqs, local, 3, H, HD)
    query = (layer_norm(qkv[:, :, 0]) * HD ** (-0.5)).astype(BF)
    key = layer_norm(qkv[:, :, 1]).astype(BF)
    value = qkv[:, :, 2].astype(BF)
    trio = [
        lax.all_to_all(to_heads(x, seqs, local), "seq", split_axis=0, concat_axis=1, tiled=True)
        for x in (query, key, value)
    ]
    attended = lax.map(attend_pair, tuple(trio))
    attended = lax.all_to_all(attended, "seq", split_axis=1, concat_axis=0, tiled=True)
    attended = jnp.transpose(attended.reshape(seqs, H, local, HD), (0, 2, 1, 3))
    full_out = lax.all_gather(w_out, "seq", axis=0, tiled=True)
    projected = jnp.dot(
        attended.reshape(tok_rows, width), full_out, preferred_element_type=F32
    ).reshape(seqs, local, width)
    return (base + gate[:, None, :] * projected).astype(BF)


class Place:
    def __init__(self, groups, n, seqs):
        self.G, self.S = groups, seqs
        self.Y = n // seqs // groups
        self.n = n
        g, j = lax.axis_index("group"), lax.axis_index("seq")
        self.x, self.z = g, j // (n // seqs)
        self.y, self.c = (j // groups) % self.Y, j % groups
        self.where = jnp.stack([self.x, self.z, self.y, self.c]).astype(jnp.int32)
        self.cores = [[k * groups + f for f in range(groups)] for k in range(n // groups)]
        self.column = [[k * n // seqs + i for k in range(seqs)] for i in range(n // seqs)]

    def send(self, value, to):
        pairs = []
        for x in range(self.G):
            for z in range(self.S):
                for y in range(self.Y):
                    for c in range(self.G):
                        tx, tz, ty, tc = to(x, z, y, c)
                        there = (tx % self.G, tz % self.S, ty % self.Y, tc % self.G)
                        pairs.append((self.flat(x, z, y, c), self.flat(*there)))
        return lax.ppermute(value, ("group", "seq"), pairs)

    def flat(self, x, z, y, c):
        return x * self.n + (z * self.Y + y) * self.G + c


def call(kernel, outs, where, *arrays, scratch=(), copies=0, flops=0, fast=(), fast_in=False, still=False):
    moved = sum(a.size * a.dtype.itemsize for a in arrays)
    space = pltpu.VMEM if fast_in else pltpu.HBM
    sems = [pltpu.SemaphoreType.DMA((copies,))] if copies else []
    return pl.pallas_call(
        kernel,
        out_shape=[jax.ShapeDtypeStruct(s, BF) for s in outs],
        in_specs=[pl.BlockSpec(memory_space=pltpu.SMEM)]
        + [pl.BlockSpec(memory_space=space)] * len(arrays),
        out_specs=[
            pl.BlockSpec(memory_space=pltpu.VMEM if k in fast else pl.ANY)
            for k in range(len(outs))
        ],
        scratch_shapes=list(scratch) + sems,
        compiler_params=pltpu.CompilerParams(vmem_limit_bytes=40 * 2**20),
        cost_estimate=pl.CostEstimate(flops=flops, bytes_accessed=2 * moved, transcendentals=0),
    )(where, *(pltpu.with_memory_space_constraint(a, pltpu.HBM) if still else a for a in arrays))


def after(value, *others):
    return lax.optimization_barrier((value, *others))[0]


def copy_all(pairs, sems):
    copies = [pltpu.make_async_copy(a, b, sems.at[k]) for k, (a, b) in enumerate(pairs)]
    for copy in copies:
        copy.start()
    for copy in copies:
        copy.wait()


def join_kernel(where, hidden, skip, out, sems):
    copy_all([(hidden, out.at[0]), (skip, out.at[1])], sems)


def cut_kernel(G, S, Y, where, w_skip_any, w_qkv_any, w_out_any, *refs):
    outs, (w_skip, w_qkv, w_out, sems) = refs[:-4], refs[-4:]
    skips, qkvs, rest = outs[0], outs[1 : 1 + Y * G], outs[1 + Y * G]
    copy_all([(w_skip_any, w_skip), (w_qkv_any, w_qkv), (w_out_any, w_out)], sems)
    x, y, c = where[0], where[2], where[3]
    width = w_skip.shape[1]
    block, part, half = width // (G * Y), 3 * (S // G) * HD, width // G
    rows = w_skip.shape[0]
    for gx in range(G):
        for gy in range(Y):
            for e in range(Y):

                @pl.when((x == gx) & ((y + e) % Y == gy))
                def _():
                    b = gx * Y + gy
                    if e == 0:
                        skips[...] = w_skip[:, b * block : (b + 1) * block]
                    else:
                        for r in range(rows // HD):
                            qkvs[e * G][:, part + r * block : part + (r + 1) * block] = w_skip[
                                r * HD : (r + 1) * HD, b * block : (b + 1) * block
                            ]
                    for gc in range(G):
                        for f in range(G):

                            @pl.when((c + f) % G == gc)
                            def _():
                                for p in range(3):
                                    for t in range(S // G):
                                        head = ((gc * (S // G) + t) * Y + gy) * G + gx
                                        at = p * width + head * HD
                                        to = (p * (S // G) + t) * HD
                                        qkvs[e * G + f][:, to : to + HD] = w_qkv[:, at : at + HD]

    for gc in range(G):
        for f in range(G):

            @pl.when((c + f) % G == gc)
            def _():
                to = rest if f == 0 else qkvs[f]
                at = 0 if f == 0 else part
                to[:, at : at + half] = w_out[:, gc * half : (gc + 1) * half]

def stack_kernel(where, *refs):
    *pieces, out, sems = refs
    copy_all([(v, out.at[s]) for s, v in enumerate(pieces)], sems)


def ring_kernel(Y, part, where, own, *refs):
    others, out = refs[:-1], refs[-1]
    y = where[2]
    rows, cols = own.shape

    def place(e):
        return pl.multiple_of((y + Y - e) % Y * rows, 16)

    out[pl.ds(place(0), rows), :] = own[...]
    for e in range(1, Y):
        v = others[e - 1]
        both = [v[:, part + r * cols : part + (r + 1) * cols] for r in range(rows // HD)]
        out[pl.ds(place(e), rows), :] = jnp.concatenate(both, axis=0)


def shards_kernel(G, S, Y, where, *refs):
    qkvs, rest, out = refs[: Y * G], refs[Y * G], refs[Y * G + 1]
    x, y, c = where[0], where[2], where[3]
    part = 3 * (S // G) * HD
    wide = out.shape[1] - part
    for gy in range(Y):
        for gc in range(G):
            at = (gy * G + gc) * HD
            for e in range(Y):
                for f in range(G):

                    @pl.when(((y + Y - e) % Y == gy) & ((c + G - f) % G == gc))
                    def _():
                        out[at : at + HD, :part] = qkvs[e * G + f][:, :part]

            for f in range(G):

                @pl.when((c + G - f) % G == x)
                def _():
                    v, off = (qkvs[f], part) if f else (rest, 0)
                    k = gy * G + gc
                    out[at : at + HD, part:] = v[:, off + k * wide : off + (k + 1) * wide]


def merged_kernel(G, S, Y, where, *refs):
    z, c = where[1], where[3]
    blocks = Y * G
    parts, weights = refs[:blocks], refs[blocks : blocks + G * S]
    outs, (xs, ws, ms, sems) = refs[blocks + G * S : -4], refs[-4:]
    width = parts[0].shape[3]
    rows = weights[0].shape[0] // Y
    pairs = []
    for k in range(blocks):
        for h in range(2):
            pairs.append((parts[k].at[h], xs.at[k, :, :, pl.ds(h * width, width)]))
    for f in range(G):
        for s in range(S):
            for y in range(Y):
                to = ws.at[(z + S - s) % S, y, (c + G - f) % G]
                pairs.append((weights[f * S + s].at[pl.ds(y * rows, rows)], to))
    copy_all(pairs, sems)
    weight = ws[...].reshape(2 * width, ws.shape[-1])
    tokens = xs[...].reshape(-1, 2 * width)
    merged = jnp.dot(tokens, weight, preferred_element_type=F32).astype(BF)
    ms[...] = merged.reshape(ms.shape)
    for s in range(S):
        outs[s][...] = ms[:, (z + s) % S]


def norm88(v):
    mean = jnp.sum(v, axis=-1, keepdims=True) * (1.0 / HD)
    d = v - mean
    var = jnp.sum(d * d, axis=-1, keepdims=True) * (1.0 / HD)
    return d * lax.rsqrt(var + 1e-06)


def attend_kernel(G, S, Y, where, *refs):
    x, z, y, c = where[0], where[1], where[2], where[3]
    blocks = Y * G
    merged_any, (shift, scale) = refs[:blocks], refs[blocks : blocks + 2]
    refs = refs[blocks + 2 :]
    w_any, refs = refs[: G * S], refs[G * S :]
    outs, base, (merged, norm, shifts, scales, ws, att, sems) = (
        refs[:blocks],
        refs[blocks],
        refs[blocks + 1 :],
    )
    cols = merged_any[0].shape[3]
    toks = S * merged_any[0].shape[2]
    rows = blocks * toks
    width = cols * blocks

    pairs = [(shift, shifts), (scale, scales)]
    for f in range(G):
        for s in range(S):
            at = pl.multiple_of((z ^ s) * cols, 16)
            pairs.append((w_any[f * S + s], ws.at[(c + G - f) % G, pl.ds(at, cols)]))
    for e in range(Y):
        for d in range(G):
            b = (x + d) % G * Y + (y + e) % Y
            for em in range(Y):
                for dm in range(G):
                    at = (em - e) % Y * G + (dm - d) % G
                    pairs.append(
                        (merged_any[e * G + d].at[:, at], merged.at[b, em * G + dm])
                    )
    copy_all(pairs, sems)
    total = jnp.zeros((rows, 1), F32)
    wide = []
    for b in range(blocks):
        base[b] = merged[b, 0].reshape(toks, cols)
        wide.append(merged[b].reshape(rows, cols).astype(F32))
        total = total + jnp.sum(wide[-1], axis=-1, keepdims=True)
    mean = total * (1.0 / width)
    square = jnp.zeros((rows, 1), F32)
    for m in wide:
        square = square + jnp.sum((m - mean) ** 2, axis=-1, keepdims=True)
    inv = lax.rsqrt(square * (1.0 / width) + 1e-06)
    for b in range(blocks):
        norm[b] = ((wide[b] - mean) * inv * (1.0 + scales[b]) + shifts[b]).astype(BF)
    per = S // G
    part = 3 * per * HD
    for f in range(G):
        qkv = jnp.dot(norm[0], ws[f, :cols, :part], preferred_element_type=F32)
        for b in range(1, blocks):
            rows_b = slice(b * cols, (b + 1) * cols)
            qkv = qkv + jnp.dot(norm[b], ws[f, rows_b, :part], preferred_element_type=F32)
        for t in range(per):
            q, k, v = (qkv[:, (p * per + t) * HD : (p * per + t + 1) * HD] for p in range(3))
            q = (norm88(q) * HD ** (-0.5)).astype(BF)
            k = norm88(k).astype(BF)
            v = v.astype(BF)
            scores = lax.dot_general(q, k, (((1,), (1,)), ((), ())), preferred_element_type=F32)
            top = jnp.max(scores, axis=-1, keepdims=True)
            probs = jnp.exp(scores - top)
            probs = (probs / jnp.sum(probs, axis=-1, keepdims=True)).astype(BF)
            att[f * per + t] = jnp.dot(probs, v, preferred_element_type=F32).astype(BF)
    wide = ws.shape[2] - part
    for f in range(G):
        whole = []
        for s in range(S):
            pieces = [
                ws[f, s * cols + k * HD : s * cols + (k + 1) * HD, part:] for k in range(blocks)
            ]
            whole.append(jnp.concatenate(pieces, axis=1))
        acc = jnp.dot(att[0], whole[0], preferred_element_type=F32)
        for s in range(1, S):
            acc = acc + jnp.dot(att[s], whole[s], preferred_element_type=F32)
        acc = acc.astype(BF)
        for k in range(blocks):
            outs[k][f] = acc[k * toks : (k + 1) * toks, :]


def result_kernel(G, S, Y, where, gate, base, *refs):
    blocks = Y * G
    parts, outs = refs[:blocks], refs[blocks:]
    toks = base.shape[1]
    local = toks // S
    halves = []
    for h in range(G):
        acc = parts[0][h].astype(F32)
        for k in range(1, blocks):
            acc = acc + parts[k][h].astype(F32)
        halves.append(acc)
    projected = jnp.concatenate(halves, axis=1)
    merged = jnp.concatenate([base[b] for b in range(blocks)], axis=1).astype(F32)
    result = (merged + gate[...] * projected).astype(BF)
    for s in range(S):
        outs[s][...] = result[s * local : (s + 1) * local, :]


def home_kernel(S, where, *refs):
    z = where[1]
    copy_all([(refs[s], refs[S].at[(z + s) % S]) for s in range(S)], refs[S + 1])


def in_planes(groups, n, hidden, skip, timestep, w_skip, w_mod, w_qkv, w_out):
    S, local, width = hidden.shape
    p = Place(groups, n, S)
    G, Y = p.G, p.Y
    blocks = Y * G
    cols, half = width // blocks, width // G
    toks, rows = S * local, w_skip.shape[0]
    part = 3 * (S // G) * HD
    every = blocks * toks

    def swap(value, e, f):
        return p.send(value, lambda x, z, y, c: (x, z, y + e, c + f))

    outs = [(rows, cols)]
    for e in range(Y):
        for f in range(G):
            more = (half if f and not e else 0) + (2 * cols if e and not f else 0)
            outs.append((HD, part + more))
    outs.append((HD, half))
    skips, *qkvs, rest = call(
        partial(cut_kernel, G, S, Y),
        outs,
        p.where,
        w_skip,
        w_qkv,
        w_out,
        scratch=[pltpu.VMEM(w.shape, BF) for w in (w_skip, w_qkv, w_out)],
        copies=3,
        fast=range(len(outs)),
        still=True,
    )
    (joined,) = call(
        join_kernel, [(2, S, local, width)], p.where, hidden, skip, copies=2, fast=[0], still=True
    )
    own = qkvs[0]
    qkvs[1 * G] = swap(qkvs[1 * G], 1, 0)
    parts = [
        p.send(joined, lambda x, z, y, c, e=e, d=d: (c - d, z, y - e, x))
        for e in range(Y)
        for d in range(G)
    ]
    for e in range(Y):
        for f in range(1, G):
            qkvs[e * G + f] = swap(after(qkvs[e * G + f], *parts[G:]), e, f)

    def step(value):
        return p.send(value, lambda x, z, y, c: (x, z + 1, y, c))

    def over_cores(held):
        return held + [swap(v, 0, f) for f in range(1, G) for v in held]

    (ring,) = call(
        partial(ring_kernel, Y, part),
        [(Y * rows, cols)],
        p.where,
        skips,
        *[qkvs[e * G] for e in range(1, Y)],
        fast=[0],
        fast_in=True,
    )
    (held,) = call(
        partial(shards_kernel, G, S, Y),
        [(blocks * HD, part + half // blocks)],
        p.where,
        *qkvs,
        rest,
        fast=[0],
        fast_in=True,
    )
    ws = [ring]
    ws.append(step(ring))
    ws.append(step(after(ws[1], *parts[:G])))
    ws.append(step(after(ws[2], *parts[G:])))
    ws = over_cores(ws)
    held = [after(held, ws[2])]
    held += [p.send(held[0], lambda x, z, y, c, k=k: (x, z ^ k, y, c)) for k in (1, 2)]

    times = p.send(timestep, lambda x, z, y, c: (c, z, y, x))
    mod = modulation(lax.dynamic_slice(times, (p.z,), (1,)), w_mod)
    shift = mod[:, :width].reshape(blocks, 1, cols)
    scale = mod[:, width : 2 * width].reshape(blocks, 1, cols)
    gate = mod[:, 2 * width :]
    parts[0] = after(parts[0], mod)

    pieces = call(
        partial(merged_kernel, G, S, Y),
        [(blocks, local, cols)] * S,
        p.where,
        *parts,
        *ws,
        scratch=[
            pltpu.VMEM((blocks, S, local, 2 * width), BF),
            pltpu.VMEM((S, Y, G, rows, cols), BF),
            pltpu.VMEM((blocks, S, local, cols), BF),
        ],
        copies=2 * blocks + S * G * Y,
        flops=4 * every * width * cols,
        still=True,
        fast=range(S),
    )
    pieces = [pieces[0]] + [
        p.send(after(pieces[s], held[1]), lambda x, z, y, c, s=s: (x, z + s, y, c)) for s in range(1, S)
    ]
    (merged,) = call(stack_kernel, [(S, blocks, local, cols)], p.where, *pieces, copies=S)
    held.append(p.send(after(held[2], merged), lambda x, z, y, c: (x, z ^ 1, y, c)))
    merged = [
        p.send(merged, lambda x, z, y, c, e=e, d=d: (x - d, z, y - e, c)) if e or d else merged
        for e in range(Y)
        for d in range(G)
    ]
    early = [after(v, *merged[1:]) for v in held[:3]]
    held += [swap(v, 0, f) for f in range(1, G) for v in (*early, held[3])]
    *parts, base = call(
        partial(attend_kernel, G, S, Y),
        [(G, toks, half)] * blocks + [(blocks, toks, cols)],
        p.where,
        *merged,
        shift,
        scale,
        *held,
        scratch=[
            pltpu.VMEM((blocks, blocks, S, local, cols), BF),
            pltpu.VMEM((blocks, every, cols), BF),
            pltpu.VMEM((blocks, 1, cols), F32),
            pltpu.VMEM((blocks, 1, cols), F32),
            pltpu.VMEM((G, width, part + half // blocks), BF),
            pltpu.VMEM((S, every, HD), BF),
        ],
        copies=2 + G * S + blocks * blocks,
        flops=10 * every * width * cols,
        still=True,
        fast=range(blocks + 1),
    )
    parts = [
        p.send(parts[e * G + d], lambda x, z, y, c, e=e, d=d: (x + d, z, y + e, c))
        if e or d
        else parts[0]
        for e in range(Y)
        for d in range(G)
    ]
    result = call(
        partial(result_kernel, G, S, Y),
        [(local, width)] * S,
        p.where,
        gate,
        base,
        *parts,
        fast=range(S),
        fast_in=True,
    )
    result = [p.send(result[s], lambda x, z, y, c, s=s: (c, z - s, y, x)) for s in range(S)]
    (out,) = call(
        partial(home_kernel, S), [(S, local, width)], p.where, *result, copies=S
    )
    return out


def solution(mesh):
    groups, n = mesh.shape["group"], mesh.shape["seq"]

    def per_device(*args):
        hidden, w_out = args[0], args[6]
        seqs, _, width = hidden.shape
        blocks = n // seqs
        fits = (
            n % seqs == 0
            and blocks % groups == 0
            and blocks == seqs
            and seqs % groups == 0
            and w_out.shape[0] == HD
            and width % blocks == 0
            and (width // blocks) % 16 == 0
        )
        return in_planes(groups, n, *args) if fits else gathered(*args)

    placed = (
        P("group", "seq", None),
        P("group", "seq", None),
        P("group"),
        P("seq", None),
        P(),
        P("seq", None),
        P("seq", None),
    )
    return jax.shard_map(
        per_device, mesh=mesh, in_specs=placed, out_specs=P("group", "seq", None), check_vma=False
    )
```

```python
import math
from functools import partial

import jax
import jax.numpy as jnp
from jax import lax
from jax.experimental import pallas as pl
from jax.experimental.pallas import tpu as pltpu
from jax.sharding import PartitionSpec as P

H = 16
HD = 88
TDIM = 256
BF = jnp.bfloat16
F32 = jnp.float32


def layer_norm(x):
    mean = jnp.mean(x, axis=-1, keepdims=True)
    var = jnp.mean((x - mean) ** 2, axis=-1, keepdims=True)
    return (x - mean) * lax.rsqrt(var + 1e-06)


def modulation(timestep, w_mod):
    half = TDIM // 2
    freqs = jnp.exp(-math.log(10000.0) * jnp.arange(half, dtype=F32) / half)
    angles = timestep.astype(F32)[:, None] * freqs[None, :]
    embed = jnp.concatenate([jnp.cos(angles), jnp.sin(angles)], axis=1)
    act = jax.nn.silu(embed).astype(BF)
    return jnp.dot(act, w_mod, preferred_element_type=F32)


def attend_pair(trio):
    qpair, kpair, vpair = trio
    scores = jnp.einsum("qd,kd->qk", qpair, kpair, preferred_element_type=F32)
    probs = jax.nn.softmax(scores, axis=-1).astype(BF)
    return jnp.dot(probs, vpair, preferred_element_type=F32).astype(BF)


def to_heads(x, seqs, local):
    return jnp.transpose(x, (0, 2, 1, 3)).reshape(seqs * H, local, HD)


def gathered(hidden, skip, timestep, w_skip, w_mod, w_qkv, w_out):
    seqs, local, width = hidden.shape
    tok_rows = seqs * local
    combined = jnp.concatenate([hidden, skip], axis=2).reshape(tok_rows, 2 * width)
    full_skip = lax.all_gather(w_skip, "seq", axis=0, tiled=True)
    merged = jnp.dot(combined, full_skip, preferred_element_type=F32).astype(BF)
    mod = modulation(timestep, w_mod)
    shift, scale, gate = (mod[:, :width], mod[:, width : 2 * width], mod[:, 2 * width :])
    base = merged.astype(F32).reshape(seqs, local, width)
    normed = (layer_norm(base) * (1.0 + scale[:, None, :]) + shift[:, None, :]).astype(BF)
    full_qkv = lax.all_gather(w_qkv, "seq", axis=0, tiled=True)
    qkv = jnp.dot(normed.reshape(tok_rows, width), full_qkv, preferred_element_type=F32)
    qkv = qkv.reshape(seqs, local, 3, H, HD)
    query = (layer_norm(qkv[:, :, 0]) * HD ** (-0.5)).astype(BF)
    key = layer_norm(qkv[:, :, 1]).astype(BF)
    value = qkv[:, :, 2].astype(BF)
    trio = [
        lax.all_to_all(to_heads(x, seqs, local), "seq", split_axis=0, concat_axis=1, tiled=True)
        for x in (query, key, value)
    ]
    attended = lax.map(attend_pair, tuple(trio))
    attended = lax.all_to_all(attended, "seq", split_axis=1, concat_axis=0, tiled=True)
    attended = jnp.transpose(attended.reshape(seqs, H, local, HD), (0, 2, 1, 3))
    full_out = lax.all_gather(w_out, "seq", axis=0, tiled=True)
    projected = jnp.dot(
        attended.reshape(tok_rows, width), full_out, preferred_element_type=F32
    ).reshape(seqs, local, width)
    return (base + gate[:, None, :] * projected).astype(BF)


class Place:
    def __init__(self, groups, n, seqs):
        self.G, self.S = groups, seqs
        self.Y = n // seqs // groups
        self.n = n
        g, j = lax.axis_index("group"), lax.axis_index("seq")
        self.x, self.z = g, j // (n // seqs)
        self.y, self.c = (j // groups) % self.Y, j % groups
        self.where = jnp.stack([self.x, self.z, self.y, self.c]).astype(jnp.int32)
        self.cores = [[k * groups + f for f in range(groups)] for k in range(n // groups)]
        self.column = [[k * n // seqs + i for k in range(seqs)] for i in range(n // seqs)]

    def send(self, value, to):
        pairs = []
        for x in range(self.G):
            for z in range(self.S):
                for y in range(self.Y):
                    for c in range(self.G):
                        tx, tz, ty, tc = to(x, z, y, c)
                        there = (tx % self.G, tz % self.S, ty % self.Y, tc % self.G)
                        pairs.append((self.flat(x, z, y, c), self.flat(*there)))
        return lax.ppermute(value, ("group", "seq"), pairs)

    def flat(self, x, z, y, c):
        return x * self.n + (z * self.Y + y) * self.G + c


def call(kernel, outs, where, *arrays, scratch=(), copies=0, flops=0, fast=(), fast_in=(), still=False):
    moved = sum(a.size * a.dtype.itemsize for a in arrays)
    fast_in = range(len(arrays)) if fast_in is True else fast_in
    sems = [pltpu.SemaphoreType.DMA((copies,))] if copies else []
    return pl.pallas_call(
        kernel,
        out_shape=[jax.ShapeDtypeStruct(s, BF) for s in outs],
        in_specs=[pl.BlockSpec(memory_space=pltpu.SMEM)]
        + [
            pl.BlockSpec(memory_space=pltpu.VMEM if k in fast_in else pl.ANY)
            for k in range(len(arrays))
        ],
        out_specs=[
            pl.BlockSpec(memory_space=pltpu.VMEM if k in fast else pl.ANY)
            for k in range(len(outs))
        ],
        scratch_shapes=list(scratch) + sems,
        compiler_params=pltpu.CompilerParams(vmem_limit_bytes=40 * 2**20),
        cost_estimate=pl.CostEstimate(flops=flops, bytes_accessed=2 * moved, transcendentals=0),
    )(
        where,
        *(
            pltpu.with_memory_space_constraint(a, pltpu.HBM) if still and k not in fast_in else a
            for k, a in enumerate(arrays)
        ),
    )


def after(value, *others):
    return lax.optimization_barrier((value, *others))[0]


def copy_all(pairs, sems):
    copies = [pltpu.make_async_copy(a, b, sems.at[k]) for k, (a, b) in enumerate(pairs)]
    for copy in copies:
        copy.start()
    for copy in copies:
        copy.wait()


def join_kernel(where, hidden, skip, out, sems):
    copy_all([(hidden, out.at[0]), (skip, out.at[1])], sems)


def cut_kernel(G, S, Y, where, w_skip_any, w_qkv_any, w_out_any, *refs):
    outs, (w_skip, w_qkv, w_out, sems) = refs[:-4], refs[-4:]
    skips, qkvs, rest = outs[0], outs[1 : 1 + Y * G], outs[1 + Y * G]
    copy_all([(w_skip_any, w_skip), (w_qkv_any, w_qkv), (w_out_any, w_out)], sems)
    x, y, c = where[0], where[2], where[3]
    width = w_skip.shape[1]
    block, part, half = width // (G * Y), 3 * (S // G) * HD, width // G
    rows = w_skip.shape[0]
    for gx in range(G):
        for gy in range(Y):
            for e in range(Y):

                @pl.when((x == gx) & ((y + e) % Y == gy))
                def _():
                    b = gx * Y + gy
                    if e == 0:
                        skips[...] = w_skip[:, b * block : (b + 1) * block]
                    else:
                        for r in range(rows // HD):
                            qkvs[e * G][:, part + r * block : part + (r + 1) * block] = w_skip[
                                r * HD : (r + 1) * HD, b * block : (b + 1) * block
                            ]
                    for gc in range(G):
                        for f in range(G):

                            @pl.when((c + f) % G == gc)
                            def _():
                                for p in range(3):
                                    for t in range(S // G):
                                        head = ((gc * (S // G) + t) * Y + gy) * G + gx
                                        at = p * width + head * HD
                                        to = (p * (S // G) + t) * HD
                                        qkvs[e * G + f][:, to : to + HD] = w_qkv[:, at : at + HD]

    for gc in range(G):
        for f in range(G):

            @pl.when((c + f) % G == gc)
            def _():
                to = rest if f == 0 else qkvs[f]
                at = 0 if f == 0 else part
                to[:, at : at + half] = w_out[:, gc * half : (gc + 1) * half]

def stack_kernel(where, *refs):
    *pieces, out, sems = refs
    copy_all([(v, out.at[s]) for s, v in enumerate(pieces)], sems)


def ring_kernel(Y, part, where, own, *refs):
    others, out = refs[:-1], refs[-1]
    y = where[2]
    rows, cols = own.shape

    def place(e):
        return pl.multiple_of((y + Y - e) % Y * rows, 16)

    out[pl.ds(place(0), rows), :] = own[...]
    for e in range(1, Y):
        v = others[e - 1]
        both = [v[:, part + r * cols : part + (r + 1) * cols] for r in range(rows // HD)]
        out[pl.ds(place(e), rows), :] = jnp.concatenate(both, axis=0)


def shards_kernel(G, S, Y, where, *refs):
    qkvs, rest, out = refs[: Y * G], refs[Y * G], refs[Y * G + 1]
    x, y, c = where[0], where[2], where[3]
    part = 3 * (S // G) * HD
    wide = out.shape[1] - part
    for gy in range(Y):
        for gc in range(G):
            at = (gy * G + gc) * HD
            for e in range(Y):
                for f in range(G):

                    @pl.when(((y + Y - e) % Y == gy) & ((c + G - f) % G == gc))
                    def _():
                        out[at : at + HD, :part] = qkvs[e * G + f][:, :part]

            for f in range(G):

                @pl.when((c + G - f) % G == x)
                def _():
                    v, off = (qkvs[f], part) if f else (rest, 0)
                    k = gy * G + gc
                    out[at : at + HD, part:] = v[:, off + k * wide : off + (k + 1) * wide]


def merged_kernel(G, S, Y, where, *refs):
    z, c = where[1], where[3]
    blocks = Y * G
    parts, weights = refs[:blocks], refs[blocks : blocks + G * S]
    outs, (xs, ws, ms, sems) = refs[blocks + G * S : -4], refs[-4:]
    width = parts[0].shape[3]
    rows = weights[0].shape[0] // Y
    pairs = []
    for k in range(blocks):
        for h in range(2):
            pairs.append((parts[k].at[h], xs.at[k, :, :, pl.ds(h * width, width)]))
    for f in range(G):
        for s in range(S):
            for y in range(Y):
                to = ws.at[(z + S - s) % S, y, (c + G - f) % G]
                pairs.append((weights[f * S + s].at[pl.ds(y * rows, rows)], to))
    copy_all(pairs, sems)
    weight = ws[...].reshape(2 * width, ws.shape[-1])
    tokens = xs[...].reshape(-1, 2 * width)
    merged = jnp.dot(tokens, weight, preferred_element_type=F32).astype(BF)
    ms[...] = merged.reshape(ms.shape)
    for s in range(S):
        outs[s][...] = ms[:, (z + s) % S]


def norm88(v):
    mean = jnp.sum(v, axis=-1, keepdims=True) * (1.0 / HD)
    d = v - mean
    var = jnp.sum(d * d, axis=-1, keepdims=True) * (1.0 / HD)
    return d * lax.rsqrt(var + 1e-06)


def norm_kernel(G, S, Y, where, *refs):
    x, y = where[0], where[2]
    blocks = Y * G
    merged_any, mods_any = refs[:blocks], refs[blocks]
    norm, base, merged, mods, sems = refs[blocks + 1 :]
    cols = merged_any[0].shape[3]
    toks = S * merged_any[0].shape[2]
    rows = blocks * toks
    width = cols * blocks

    pairs = [(mods_any, mods)]
    for e in range(Y):
        for d in range(G):
            b = (x + d) % G * Y + (y + e) % Y
            for em in range(Y):
                for dm in range(G):
                    at = (em - e) % Y * G + (dm - d) % G
                    pairs.append(
                        (merged_any[e * G + d].at[:, at], merged.at[b, em * G + dm])
                    )
    copy_all(pairs, sems)
    total = jnp.zeros((rows, 1), F32)
    wide = []
    for b in range(blocks):
        base[b] = merged[b, 0].reshape(toks, cols)
        wide.append(merged[b].reshape(rows, cols).astype(F32))
        total = total + jnp.sum(wide[-1], axis=-1, keepdims=True)
    mean = total * (1.0 / width)
    square = jnp.zeros((rows, 1), F32)
    for m in wide:
        square = square + jnp.sum((m - mean) ** 2, axis=-1, keepdims=True)
    inv = lax.rsqrt(square * (1.0 / width) + 1e-06)
    for b in range(blocks):
        norm[b] = ((wide[b] - mean) * inv * (1.0 + mods[blocks + b]) + mods[b]).astype(BF)


def attend_kernel(G, S, Y, where, norm, *refs):
    z, c = where[1], where[3]
    blocks = Y * G
    ws, refs = refs[: G * S], refs[G * S :]
    outs, att = refs[:blocks], refs[blocks]
    rows = norm.shape[1]
    toks = rows // blocks
    per = S // G
    part = 3 * per * HD
    for f in range(G):
        qkv = jnp.dot(norm[z], ws[f * S][:, :part], preferred_element_type=F32)
        for s in range(1, S):
            qkv = qkv + jnp.dot(
                norm[z ^ s], ws[f * S + s][:, :part], preferred_element_type=F32
            )
        for t in range(per):
            q, k, v = (qkv[:, (p * per + t) * HD : (p * per + t + 1) * HD] for p in range(3))
            q = (norm88(q) * HD ** (-0.5)).astype(BF)
            k = norm88(k).astype(BF)
            v = v.astype(BF)
            scores = lax.dot_general(q, k, (((1,), (1,)), ((), ())), preferred_element_type=F32)
            probs = jnp.exp(scores)
            scaled = 1.0 / jnp.sum(probs, axis=-1, keepdims=True)
            mixed = jnp.dot(probs.astype(BF), v, preferred_element_type=F32)
            att[(c + G - f) % G * per + t] = (mixed * scaled).astype(BF)
    for f in range(G):
        whole = []
        for s in range(S):
            pieces = [
                ws[f * S + s][k * HD : (k + 1) * HD, part:] for k in range(blocks)
            ]
            whole.append(jnp.concatenate(pieces, axis=1))
        acc = jnp.dot(att[z], whole[0], preferred_element_type=F32)
        for s in range(1, S):
            acc = acc + jnp.dot(att[z ^ s], whole[s], preferred_element_type=F32)
        acc = acc.astype(BF)
        for k in range(blocks):
            outs[k][(c + G - f) % G] = acc[k * toks : (k + 1) * toks, :]


def result_kernel(G, S, Y, where, mods, base, *refs):
    blocks = Y * G
    parts, outs = refs[:blocks], refs[blocks:]
    toks = base.shape[1]
    local = toks // S
    halves = []
    for h in range(G):
        acc = parts[0][h].astype(F32)
        for k in range(1, blocks):
            acc = acc + parts[k][h].astype(F32)
        halves.append(acc)
    projected = jnp.concatenate(halves, axis=1)
    merged = jnp.concatenate([base[b] for b in range(blocks)], axis=1).astype(F32)
    gate = jnp.concatenate([mods[2 * blocks + b] for b in range(blocks)], axis=1)
    result = (merged + gate * projected).astype(BF)
    for s in range(S):
        outs[s][...] = result[s * local : (s + 1) * local, :]


def home_kernel(S, where, *refs):
    z = where[1]
    copy_all([(refs[s], refs[S].at[(z + s) % S]) for s in range(S)], refs[S + 1])


def in_planes(groups, n, hidden, skip, timestep, w_skip, w_mod, w_qkv, w_out):
    S, local, width = hidden.shape
    p = Place(groups, n, S)
    G, Y = p.G, p.Y
    blocks = Y * G
    cols, half = width // blocks, width // G
    toks, rows = S * local, w_skip.shape[0]
    part = 3 * (S // G) * HD
    every = blocks * toks

    def swap(value, e, f):
        return p.send(value, lambda x, z, y, c: (x, z, y + e, c + f))

    outs = [(rows, cols)]
    for e in range(Y):
        for f in range(G):
            more = (half if f and not e else 0) + (2 * cols if e and not f else 0)
            outs.append((HD, part + more))
    outs.append((HD, half))
    skips, *qkvs, rest = call(
        partial(cut_kernel, G, S, Y),
        outs,
        p.where,
        w_skip,
        w_qkv,
        w_out,
        scratch=[pltpu.VMEM(w.shape, BF) for w in (w_skip, w_qkv, w_out)],
        copies=3,
        fast=range(len(outs)),
        still=True,
    )
    (joined,) = call(
        join_kernel, [(2, S, local, width)], p.where, hidden, skip, copies=2, fast=[0], still=True
    )
    own = qkvs[0]
    qkvs[1 * G] = swap(qkvs[1 * G], 1, 0)
    parts = [
        p.send(joined, lambda x, z, y, c, e=e, d=d: (c - d, z, y - e, x))
        for e in range(Y)
        for d in range(G)
    ]
    for e in range(Y):
        for f in range(1, G):
            qkvs[e * G + f] = swap(after(qkvs[e * G + f], *parts[G:]), e, f)

    def step(value):
        return p.send(value, lambda x, z, y, c: (x, z + 1, y, c))

    def over_cores(held):
        return held + [swap(v, 0, f) for f in range(1, G) for v in held]

    (ring,) = call(
        partial(ring_kernel, Y, part),
        [(Y * rows, cols)],
        p.where,
        skips,
        *[qkvs[e * G] for e in range(1, Y)],
        fast=[0],
        fast_in=True,
    )
    (held,) = call(
        partial(shards_kernel, G, S, Y),
        [(blocks * HD, part + half // blocks)],
        p.where,
        *qkvs,
        rest,
        fast=[0],
        fast_in=True,
    )
    ws = [ring]
    ws.append(step(ring))
    ws.append(step(after(ws[1], *parts[:G])))
    ws.append(step(after(ws[2], *parts[G:])))
    ws = over_cores(ws)
    held = [after(held, ws[2])]
    held += [p.send(held[0], lambda x, z, y, c, k=k: (x, z ^ k, y, c)) for k in (1, 2)]

    times = p.send(timestep, lambda x, z, y, c: (c, z, y, x))
    mod = modulation(lax.dynamic_slice(times, (p.z,), (1,)), w_mod)
    mods = after(mod, p.where).reshape(3 * blocks, 1, cols)

    pieces = call(
        partial(merged_kernel, G, S, Y),
        [(blocks, local, cols)] * S,
        p.where,
        *parts,
        *ws,
        scratch=[
            pltpu.VMEM((blocks, S, local, 2 * width), BF),
            pltpu.VMEM((S, Y, G, rows, cols), BF),
            pltpu.VMEM((blocks, S, local, cols), BF),
        ],
        copies=2 * blocks + S * G * Y,
        flops=4 * every * width * cols,
        still=True,
        fast=range(S),
    )
    pieces = [pieces[0]] + [
        p.send(after(pieces[s], held[1], mods), lambda x, z, y, c, s=s: (x, z + s, y, c)) for s in range(1, S)
    ]
    (merged,) = call(stack_kernel, [(S, blocks, local, cols)], p.where, *pieces, copies=S)
    held.append(p.send(after(held[2], merged), lambda x, z, y, c: (x, z ^ 1, y, c)))
    merged = [
        p.send(merged, lambda x, z, y, c, e=e, d=d: (x - d, z, y - e, c)) if e or d else merged
        for e in range(Y)
        for d in range(G)
    ]
    early = [after(v, *merged[1:]) for v in held[:3]]
    held += [swap(v, 0, f) for f in range(1, G) for v in (*early, held[3])]
    norm, base = call(
        partial(norm_kernel, G, S, Y),
        [(blocks, every, cols), (blocks, toks, cols)],
        p.where,
        *merged,
        mods,
        scratch=[
            pltpu.VMEM((blocks, blocks, S, local, cols), BF),
            pltpu.VMEM((3 * blocks, 1, cols), F32),
        ],
        copies=1 + blocks * blocks,
        fast=range(2),
        still=True,
    )
    parts = call(
        partial(attend_kernel, G, S, Y),
        [(G, toks, half)] * blocks,
        p.where,
        norm,
        *held,
        scratch=[pltpu.VMEM((S, every, HD), BF)],
        flops=10 * every * width * cols,
        fast=range(blocks),
        fast_in=True,
    )
    parts = [
        p.send(parts[e * G + d], lambda x, z, y, c, e=e, d=d: (x + d, z, y + e, c))
        if e or d
        else parts[0]
        for e in range(Y)
        for d in range(G)
    ]
    result = call(
        partial(result_kernel, G, S, Y),
        [(local, width)] * S,
        p.where,
        mods,
        base,
        *parts,
        fast=range(S),
        fast_in=True,
    )
    result = [p.send(result[s], lambda x, z, y, c, s=s: (c, z - s, y, x)) for s in range(S)]
    (out,) = call(
        partial(home_kernel, S), [(S, local, width)], p.where, *result, copies=S
    )
    return out


def solution(mesh):
    groups, n = mesh.shape["group"], mesh.shape["seq"]

    def per_device(*args):
        hidden, w_out = args[0], args[6]
        seqs, _, width = hidden.shape
        blocks = n // seqs
        fits = (
            n % seqs == 0
            and blocks % groups == 0
            and blocks == seqs
            and seqs % groups == 0
            and w_out.shape[0] == HD
            and width % blocks == 0
            and (width // blocks) % 16 == 0
        )
        return in_planes(groups, n, *args) if fits else gathered(*args)

    placed = (
        P("group", "seq", None),
        P("group", "seq", None),
        P("group"),
        P("seq", None),
        P(),
        P("seq", None),
        P("seq", None),
    )
    return jax.shard_map(
        per_device, mesh=mesh, in_specs=placed, out_specs=P("group", "seq", None), check_vma=False
    )
```

```python
import math
from functools import partial

import jax
import jax.numpy as jnp
from jax import lax
from jax.experimental import pallas as pl
from jax.experimental.pallas import tpu as pltpu
from jax.sharding import PartitionSpec as P

H = 16
HD = 88
TDIM = 256
BF = jnp.bfloat16
F32 = jnp.float32


def layer_norm(x):
    mean = jnp.mean(x, axis=-1, keepdims=True)
    var = jnp.mean((x - mean) ** 2, axis=-1, keepdims=True)
    return (x - mean) * lax.rsqrt(var + 1e-06)


def modulation(timestep, w_mod):
    half = TDIM // 2
    freqs = jnp.exp(-math.log(10000.0) * jnp.arange(half, dtype=F32) / half)
    angles = timestep.astype(F32)[:, None] * freqs[None, :]
    embed = jnp.concatenate([jnp.cos(angles), jnp.sin(angles)], axis=1)
    act = jax.nn.silu(embed).astype(BF)
    return jnp.dot(act, w_mod, preferred_element_type=F32)


def attend_pair(trio):
    qpair, kpair, vpair = trio
    scores = jnp.einsum("qd,kd->qk", qpair, kpair, preferred_element_type=F32)
    probs = jax.nn.softmax(scores, axis=-1).astype(BF)
    return jnp.dot(probs, vpair, preferred_element_type=F32).astype(BF)


def to_heads(x, seqs, local):
    return jnp.transpose(x, (0, 2, 1, 3)).reshape(seqs * H, local, HD)


def gathered(hidden, skip, timestep, w_skip, w_mod, w_qkv, w_out):
    seqs, local, width = hidden.shape
    tok_rows = seqs * local
    combined = jnp.concatenate([hidden, skip], axis=2).reshape(tok_rows, 2 * width)
    full_skip = lax.all_gather(w_skip, "seq", axis=0, tiled=True)
    merged = jnp.dot(combined, full_skip, preferred_element_type=F32).astype(BF)
    mod = modulation(timestep, w_mod)
    shift, scale, gate = (mod[:, :width], mod[:, width : 2 * width], mod[:, 2 * width :])
    base = merged.astype(F32).reshape(seqs, local, width)
    normed = (layer_norm(base) * (1.0 + scale[:, None, :]) + shift[:, None, :]).astype(BF)
    full_qkv = lax.all_gather(w_qkv, "seq", axis=0, tiled=True)
    qkv = jnp.dot(normed.reshape(tok_rows, width), full_qkv, preferred_element_type=F32)
    qkv = qkv.reshape(seqs, local, 3, H, HD)
    query = (layer_norm(qkv[:, :, 0]) * HD ** (-0.5)).astype(BF)
    key = layer_norm(qkv[:, :, 1]).astype(BF)
    value = qkv[:, :, 2].astype(BF)
    trio = [
        lax.all_to_all(to_heads(x, seqs, local), "seq", split_axis=0, concat_axis=1, tiled=True)
        for x in (query, key, value)
    ]
    attended = lax.map(attend_pair, tuple(trio))
    attended = lax.all_to_all(attended, "seq", split_axis=1, concat_axis=0, tiled=True)
    attended = jnp.transpose(attended.reshape(seqs, H, local, HD), (0, 2, 1, 3))
    full_out = lax.all_gather(w_out, "seq", axis=0, tiled=True)
    projected = jnp.dot(
        attended.reshape(tok_rows, width), full_out, preferred_element_type=F32
    ).reshape(seqs, local, width)
    return (base + gate[:, None, :] * projected).astype(BF)


class Place:
    def __init__(self, groups, n, seqs):
        self.G, self.S = groups, seqs
        self.Y = n // seqs // groups
        self.n = n
        g, j = lax.axis_index("group"), lax.axis_index("seq")
        self.x, self.z = g, j // (n // seqs)
        self.y, self.c = (j // groups) % self.Y, j % groups
        self.where = jnp.stack([self.x, self.z, self.y, self.c]).astype(jnp.int32)
        self.cores = [[k * groups + f for f in range(groups)] for k in range(n // groups)]
        self.column = [[k * n // seqs + i for k in range(seqs)] for i in range(n // seqs)]

    def send(self, value, to):
        pairs = []
        for x in range(self.G):
            for z in range(self.S):
                for y in range(self.Y):
                    for c in range(self.G):
                        tx, tz, ty, tc = to(x, z, y, c)
                        there = (tx % self.G, tz % self.S, ty % self.Y, tc % self.G)
                        pairs.append((self.flat(x, z, y, c), self.flat(*there)))
        return lax.ppermute(value, ("group", "seq"), pairs)

    def flat(self, x, z, y, c):
        return x * self.n + (z * self.Y + y) * self.G + c


def call(kernel, outs, where, *arrays, scratch=(), copies=0, flops=0, fast=(), fast_in=(), still=False):
    moved = sum(a.size * a.dtype.itemsize for a in arrays)
    fast_in = range(len(arrays)) if fast_in is True else fast_in
    sems = [pltpu.SemaphoreType.DMA((copies,))] if copies else []
    return pl.pallas_call(
        kernel,
        out_shape=[jax.ShapeDtypeStruct(s, BF) for s in outs],
        in_specs=[pl.BlockSpec(memory_space=pltpu.SMEM)]
        + [
            pl.BlockSpec(memory_space=pltpu.VMEM if k in fast_in else pl.ANY)
            for k in range(len(arrays))
        ],
        out_specs=[
            pl.BlockSpec(memory_space=pltpu.VMEM if k in fast else pl.ANY)
            for k in range(len(outs))
        ],
        scratch_shapes=list(scratch) + sems,
        compiler_params=pltpu.CompilerParams(vmem_limit_bytes=40 * 2**20),
        cost_estimate=pl.CostEstimate(flops=flops, bytes_accessed=2 * moved, transcendentals=0),
    )(
        where,
        *(
            pltpu.with_memory_space_constraint(a, pltpu.HBM) if still and k not in fast_in else a
            for k, a in enumerate(arrays)
        ),
    )


def after(value, *others):
    return lax.optimization_barrier((value, *others))[0]


def copy_all(pairs, sems):
    copies = [pltpu.make_async_copy(a, b, sems.at[k]) for k, (a, b) in enumerate(pairs)]
    for copy in copies:
        copy.start()
    for copy in copies:
        copy.wait()


def join_kernel(where, hidden, skip, out, sems):
    copy_all([(hidden, out.at[0]), (skip, out.at[1])], sems)


def cut_kernel(G, S, Y, where, w_skip_any, w_qkv_any, w_out_any, *refs):
    outs, (w_skip, w_qkv, w_out, sems) = refs[:-4], refs[-4:]
    skips, qkvs, rest = outs[0], outs[1 : 1 + Y * G], outs[1 + Y * G]
    copy_all([(w_skip_any, w_skip), (w_qkv_any, w_qkv), (w_out_any, w_out)], sems)
    x, y, c = where[0], where[2], where[3]
    width = w_skip.shape[1]
    block, part, half = width // (G * Y), 3 * (S // G) * HD, width // G
    rows = w_skip.shape[0]
    for gx in range(G):
        for gy in range(Y):
            for e in range(Y):

                @pl.when((x == gx) & ((y + e) % Y == gy))
                def _():
                    b = gx * Y + gy
                    if e == 0:
                        skips[...] = w_skip[:, b * block : (b + 1) * block]
                    else:
                        for r in range(rows // HD):
                            qkvs[e * G][:, part + r * block : part + (r + 1) * block] = w_skip[
                                r * HD : (r + 1) * HD, b * block : (b + 1) * block
                            ]
                    for gc in range(G):
                        for f in range(G):

                            @pl.when((c + f) % G == gc)
                            def _():
                                for p in range(3):
                                    for t in range(S // G):
                                        head = ((gc * (S // G) + t) * Y + gy) * G + gx
                                        at = p * width + head * HD
                                        to = (p * (S // G) + t) * HD
                                        qkvs[e * G + f][:, to : to + HD] = w_qkv[:, at : at + HD]

    for gc in range(G):
        for f in range(G):

            @pl.when((c + f) % G == gc)
            def _():
                to = rest if f == 0 else qkvs[f]
                at = 0 if f == 0 else part
                to[:, at : at + half] = w_out[:, gc * half : (gc + 1) * half]

def stack_kernel(where, *refs):
    *pieces, out, sems = refs
    copy_all([(v, out.at[s]) for s, v in enumerate(pieces)], sems)


def ring_kernel(Y, part, where, own, *refs):
    others, out = refs[:-1], refs[-1]
    y = where[2]
    rows, cols = own.shape

    def place(e):
        return pl.multiple_of((y + Y - e) % Y * rows, 16)

    out[pl.ds(place(0), rows), :] = own[...]
    for e in range(1, Y):
        v = others[e - 1]
        both = [v[:, part + r * cols : part + (r + 1) * cols] for r in range(rows // HD)]
        out[pl.ds(place(e), rows), :] = jnp.concatenate(both, axis=0)


def shards_kernel(G, S, Y, where, *refs):
    qkvs, rest, out = refs[: Y * G], refs[Y * G], refs[Y * G + 1]
    x, y, c = where[0], where[2], where[3]
    part = 3 * (S // G) * HD
    wide = out.shape[1] - part
    for gy in range(Y):
        for gc in range(G):
            at = (gy * G + gc) * HD
            for e in range(Y):
                for f in range(G):

                    @pl.when(((y + Y - e) % Y == gy) & ((c + G - f) % G == gc))
                    def _():
                        out[at : at + HD, :part] = qkvs[e * G + f][:, :part]

            for f in range(G):

                @pl.when((c + G - f) % G == x)
                def _():
                    v, off = (qkvs[f], part) if f else (rest, 0)
                    k = gy * G + gc
                    out[at : at + HD, part:] = v[:, off + k * wide : off + (k + 1) * wide]


def merged_kernel(G, S, Y, where, *refs):
    z, c = where[1], where[3]
    blocks = Y * G
    parts, weights = refs[:blocks], refs[blocks : blocks + G * S]
    outs, (xs, ws, ms, sems) = refs[blocks + G * S : -4], refs[-4:]
    width = parts[0].shape[3]
    rows = weights[0].shape[0] // Y
    pairs = []
    for k in range(blocks):
        for h in range(2):
            pairs.append((parts[k].at[h], xs.at[k, :, :, pl.ds(h * width, width)]))
    for f in range(G):
        for s in range(S):
            for y in range(Y):
                to = ws.at[(z + S - s) % S, y, (c + G - f) % G]
                pairs.append((weights[f * S + s].at[pl.ds(y * rows, rows)], to))
    copy_all(pairs, sems)
    weight = ws[...].reshape(2 * width, ws.shape[-1])
    tokens = xs[...].reshape(-1, 2 * width)
    merged = jnp.dot(tokens, weight, preferred_element_type=F32).astype(BF)
    ms[...] = merged.reshape(ms.shape)
    for s in range(S):
        outs[s][...] = ms[:, (z + s) % S]


def norm88(v):
    mean = jnp.sum(v, axis=-1, keepdims=True) * (1.0 / HD)
    d = v - mean
    var = jnp.sum(d * d, axis=-1, keepdims=True) * (1.0 / HD)
    return d * lax.rsqrt(var + 1e-06)


def norm_kernel(G, S, Y, where, *refs):
    x, y = where[0], where[2]
    blocks = Y * G
    merged, mods, norm, base = refs[:blocks], refs[blocks], refs[blocks + 1], refs[blocks + 2]
    cols = merged[0].shape[3]
    toks = S * merged[0].shape[2]
    rows = blocks * toks
    width = cols * blocks

    total = jnp.zeros((rows, 1), F32)
    wide = []
    for e in range(Y):
        for d in range(G):
            own = [
                merged[e * G + d][:, (em - e) % Y * G + (dm - d) % G].reshape(toks, cols)
                for em in range(Y)
                for dm in range(G)
            ]
            base[(x + d) % G * Y + (y + e) % Y] = own[0]
            wide.append(jnp.concatenate(own, axis=0).astype(F32))
            total = total + jnp.sum(wide[-1], axis=-1, keepdims=True)
    mean = total * (1.0 / width)
    square = jnp.zeros((rows, 1), F32)
    for m in wide:
        square = square + jnp.sum((m - mean) ** 2, axis=-1, keepdims=True)
    inv = lax.rsqrt(square * (1.0 / width) + 1e-06)
    for e in range(Y):
        for d in range(G):
            b = (x + d) % G * Y + (y + e) % Y
            m = wide[e * G + d]
            norm[b] = ((m - mean) * inv * (1.0 + mods[blocks + b]) + mods[b]).astype(BF)


def attend_kernel(G, S, Y, where, norm, *refs):
    z, c = where[1], where[3]
    blocks = Y * G
    ws, refs = refs[: G * S], refs[G * S :]
    outs, att = refs[:blocks], refs[blocks]
    rows = norm.shape[1]
    toks = rows // blocks
    per = S // G
    part = 3 * per * HD
    for f in range(G):
        qkv = jnp.dot(norm[z], ws[f * S][:, :part], preferred_element_type=F32)
        for s in range(1, S):
            qkv = qkv + jnp.dot(
                norm[z ^ s], ws[f * S + s][:, :part], preferred_element_type=F32
            )
        for t in range(per):
            q, k, v = (qkv[:, (p * per + t) * HD : (p * per + t + 1) * HD] for p in range(3))
            q = (norm88(q) * HD ** (-0.5)).astype(BF)
            k = norm88(k).astype(BF)
            v = v.astype(BF)
            scores = lax.dot_general(q, k, (((1,), (1,)), ((), ())), preferred_element_type=F32)
            probs = jnp.exp(scores)
            scaled = 1.0 / jnp.sum(probs, axis=-1, keepdims=True)
            mixed = jnp.dot(probs.astype(BF), v, preferred_element_type=F32)
            att[(c + G - f) % G * per + t] = (mixed * scaled).astype(BF)
    for f in range(G):
        whole = []
        for s in range(S):
            pieces = [
                ws[f * S + s][k * HD : (k + 1) * HD, part:] for k in range(blocks)
            ]
            whole.append(jnp.concatenate(pieces, axis=1))
        acc = jnp.dot(att[z], whole[0], preferred_element_type=F32)
        for s in range(1, S):
            acc = acc + jnp.dot(att[z ^ s], whole[s], preferred_element_type=F32)
        acc = acc.astype(BF)
        for k in range(blocks):
            outs[k][(c + G - f) % G] = acc[k * toks : (k + 1) * toks, :]


def result_kernel(G, S, Y, where, mods, base, *refs):
    blocks = Y * G
    parts, outs = refs[:blocks], refs[blocks:]
    toks = base.shape[1]
    local = toks // S
    halves = []
    for h in range(G):
        acc = parts[0][h].astype(F32)
        for k in range(1, blocks):
            acc = acc + parts[k][h].astype(F32)
        halves.append(acc)
    projected = jnp.concatenate(halves, axis=1)
    merged = jnp.concatenate([base[b] for b in range(blocks)], axis=1).astype(F32)
    gate = jnp.concatenate([mods[2 * blocks + b] for b in range(blocks)], axis=1)
    result = (merged + gate * projected).astype(BF)
    for s in range(S):
        outs[s][...] = result[s * local : (s + 1) * local, :]


def home_kernel(S, where, *refs):
    z = where[1]
    copy_all([(refs[s], refs[S].at[(z + s) % S]) for s in range(S)], refs[S + 1])


def in_planes(groups, n, hidden, skip, timestep, w_skip, w_mod, w_qkv, w_out):
    S, local, width = hidden.shape
    p = Place(groups, n, S)
    G, Y = p.G, p.Y
    blocks = Y * G
    cols, half = width // blocks, width // G
    toks, rows = S * local, w_skip.shape[0]
    part = 3 * (S // G) * HD
    every = blocks * toks

    def swap(value, e, f):
        return p.send(value, lambda x, z, y, c: (x, z, y + e, c + f))

    outs = [(rows, cols)]
    for e in range(Y):
        for f in range(G):
            more = (half if f and not e else 0) + (2 * cols if e and not f else 0)
            outs.append((HD, part + more))
    outs.append((HD, half))
    skips, *qkvs, rest = call(
        partial(cut_kernel, G, S, Y),
        outs,
        p.where,
        w_skip,
        w_qkv,
        w_out,
        scratch=[pltpu.VMEM(w.shape, BF) for w in (w_skip, w_qkv, w_out)],
        copies=3,
        fast=range(len(outs)),
        still=True,
    )
    (joined,) = call(
        join_kernel, [(2, S, local, width)], p.where, hidden, skip, copies=2, fast=[0], still=True
    )
    own = qkvs[0]
    qkvs[1 * G] = swap(qkvs[1 * G], 1, 0)
    parts = [
        p.send(joined, lambda x, z, y, c, e=e, d=d: (c - d, z, y - e, x))
        for e in range(Y)
        for d in range(G)
    ]
    for e in range(Y):
        for f in range(1, G):
            qkvs[e * G + f] = swap(after(qkvs[e * G + f], parts[G]), e, f)

    def step(value):
        return p.send(value, lambda x, z, y, c: (x, z + 1, y, c))

    def over_cores(held):
        return held + [swap(v, 0, f) for f in range(1, G) for v in held]

    (ring,) = call(
        partial(ring_kernel, Y, part),
        [(Y * rows, cols)],
        p.where,
        skips,
        *[qkvs[e * G] for e in range(1, Y)],
        fast=[0],
        fast_in=True,
    )
    (held,) = call(
        partial(shards_kernel, G, S, Y),
        [(blocks * HD, part + half // blocks)],
        p.where,
        *qkvs,
        rest,
        fast=[0],
        fast_in=True,
    )
    ws = [ring]
    ws.append(step(ring))
    ws.append(step(after(ws[1], *parts[:G])))
    ws.append(step(after(ws[2], *parts[G:])))
    ws = over_cores(ws)
    held = [after(held, ws[2])]
    held += [p.send(held[0], lambda x, z, y, c, k=k: (x, z ^ k, y, c)) for k in (1, 2)]

    times = p.send(timestep, lambda x, z, y, c: (c, z, y, x))
    mod = modulation(lax.dynamic_slice(times, (p.z,), (1,)), w_mod)
    mods = after(mod, p.where).reshape(3 * blocks, 1, cols)

    pieces = call(
        partial(merged_kernel, G, S, Y),
        [(blocks, local, cols)] * S,
        p.where,
        *parts,
        *ws,
        scratch=[
            pltpu.VMEM((blocks, S, local, 2 * width), BF),
            pltpu.VMEM((S, Y, G, rows, cols), BF),
            pltpu.VMEM((blocks, S, local, cols), BF),
        ],
        copies=2 * blocks + S * G * Y,
        flops=4 * every * width * cols,
        still=True,
        fast=range(S),
    )
    pieces = [pieces[0]] + [
        p.send(after(pieces[s], held[1], mods), lambda x, z, y, c, s=s: (x, z + s, y, c)) for s in range(1, S)
    ]
    (merged,) = call(stack_kernel, [(S, blocks, local, cols)], p.where, *pieces, copies=S)
    held.append(p.send(after(held[2], merged), lambda x, z, y, c: (x, z ^ 1, y, c)))
    merged = [
        p.send(merged, lambda x, z, y, c, e=e, d=d: (x - d, z, y - e, c)) if e or d else merged
        for e in range(Y)
        for d in range(G)
    ]
    early = [after(v, *merged[1:]) for v in held[:3]]
    held += [swap(v, 0, f) for f in range(1, G) for v in (*early, held[3])]
    norm, base = call(
        partial(norm_kernel, G, S, Y),
        [(blocks, every, cols), (blocks, toks, cols)],
        p.where,
        *merged,
        mods,
        fast=range(2),
        fast_in=True,
    )
    parts = call(
        partial(attend_kernel, G, S, Y),
        [(G, toks, half)] * blocks,
        p.where,
        norm,
        *held,
        scratch=[pltpu.VMEM((S, every, HD), BF)],
        flops=10 * every * width * cols,
        fast=range(blocks),
        fast_in=True,
    )
    parts = [
        p.send(parts[e * G + d], lambda x, z, y, c, e=e, d=d: (x + d, z, y + e, c))
        if e or d
        else parts[0]
        for e in range(Y)
        for d in range(G)
    ]
    result = call(
        partial(result_kernel, G, S, Y),
        [(local, width)] * S,
        p.where,
        mods,
        base,
        *parts,
        fast=range(S),
        fast_in=True,
    )
    result = [p.send(result[s], lambda x, z, y, c, s=s: (c, z - s, y, x)) for s in range(S)]
    (out,) = call(
        partial(home_kernel, S), [(S, local, width)], p.where, *result, copies=S
    )
    return out


def solution(mesh):
    groups, n = mesh.shape["group"], mesh.shape["seq"]

    def per_device(*args):
        hidden, w_out = args[0], args[6]
        seqs, _, width = hidden.shape
        blocks = n // seqs
        fits = (
            n % seqs == 0
            and blocks % groups == 0
            and blocks == seqs
            and seqs % groups == 0
            and w_out.shape[0] == HD
            and width % blocks == 0
            and (width // blocks) % 16 == 0
        )
        return in_planes(groups, n, *args) if fits else gathered(*args)

    placed = (
        P("group", "seq", None),
        P("group", "seq", None),
        P("group"),
        P("seq", None),
        P(),
        P("seq", None),
        P("seq", None),
    )
    return jax.shard_map(
        per_device, mesh=mesh, in_specs=placed, out_specs=P("group", "seq", None), check_vma=False
    )
```

```python
import math
from functools import partial

import jax
import jax.numpy as jnp
from jax import lax
from jax.experimental import pallas as pl
from jax.experimental.pallas import tpu as pltpu
from jax.sharding import PartitionSpec as P

H = 16
HD = 88
TDIM = 256
BF = jnp.bfloat16
F32 = jnp.float32


def layer_norm(x):
    mean = jnp.mean(x, axis=-1, keepdims=True)
    var = jnp.mean((x - mean) ** 2, axis=-1, keepdims=True)
    return (x - mean) * lax.rsqrt(var + 1e-06)


def modulation(timestep, w_mod):
    half = TDIM // 2
    freqs = jnp.exp(-math.log(10000.0) * jnp.arange(half, dtype=F32) / half)
    angles = timestep.astype(F32)[:, None] * freqs[None, :]
    embed = jnp.concatenate([jnp.cos(angles), jnp.sin(angles)], axis=1)
    act = jax.nn.silu(embed).astype(BF)
    return jnp.dot(act, w_mod, preferred_element_type=F32)


def attend_pair(trio):
    qpair, kpair, vpair = trio
    scores = jnp.einsum("qd,kd->qk", qpair, kpair, preferred_element_type=F32)
    probs = jax.nn.softmax(scores, axis=-1).astype(BF)
    return jnp.dot(probs, vpair, preferred_element_type=F32).astype(BF)


def to_heads(x, seqs, local):
    return jnp.transpose(x, (0, 2, 1, 3)).reshape(seqs * H, local, HD)


def gathered(hidden, skip, timestep, w_skip, w_mod, w_qkv, w_out):
    seqs, local, width = hidden.shape
    tok_rows = seqs * local
    combined = jnp.concatenate([hidden, skip], axis=2).reshape(tok_rows, 2 * width)
    full_skip = lax.all_gather(w_skip, "seq", axis=0, tiled=True)
    merged = jnp.dot(combined, full_skip, preferred_element_type=F32).astype(BF)
    mod = modulation(timestep, w_mod)
    shift, scale, gate = (mod[:, :width], mod[:, width : 2 * width], mod[:, 2 * width :])
    base = merged.astype(F32).reshape(seqs, local, width)
    normed = (layer_norm(base) * (1.0 + scale[:, None, :]) + shift[:, None, :]).astype(BF)
    full_qkv = lax.all_gather(w_qkv, "seq", axis=0, tiled=True)
    qkv = jnp.dot(normed.reshape(tok_rows, width), full_qkv, preferred_element_type=F32)
    qkv = qkv.reshape(seqs, local, 3, H, HD)
    query = (layer_norm(qkv[:, :, 0]) * HD ** (-0.5)).astype(BF)
    key = layer_norm(qkv[:, :, 1]).astype(BF)
    value = qkv[:, :, 2].astype(BF)
    trio = [
        lax.all_to_all(to_heads(x, seqs, local), "seq", split_axis=0, concat_axis=1, tiled=True)
        for x in (query, key, value)
    ]
    attended = lax.map(attend_pair, tuple(trio))
    attended = lax.all_to_all(attended, "seq", split_axis=1, concat_axis=0, tiled=True)
    attended = jnp.transpose(attended.reshape(seqs, H, local, HD), (0, 2, 1, 3))
    full_out = lax.all_gather(w_out, "seq", axis=0, tiled=True)
    projected = jnp.dot(
        attended.reshape(tok_rows, width), full_out, preferred_element_type=F32
    ).reshape(seqs, local, width)
    return (base + gate[:, None, :] * projected).astype(BF)


class Place:
    def __init__(self, groups, n, seqs):
        self.G, self.S = groups, seqs
        self.Y = n // seqs // groups
        self.n = n
        g, j = lax.axis_index("group"), lax.axis_index("seq")
        self.x, self.z = g, j // (n // seqs)
        self.y, self.c = (j // groups) % self.Y, j % groups
        self.where = jnp.stack([self.x, self.z, self.y, self.c]).astype(jnp.int32)
        self.cores = [[k * groups + f for f in range(groups)] for k in range(n // groups)]
        self.column = [[k * n // seqs + i for k in range(seqs)] for i in range(n // seqs)]

    def send(self, value, to):
        pairs = []
        for x in range(self.G):
            for z in range(self.S):
                for y in range(self.Y):
                    for c in range(self.G):
                        tx, tz, ty, tc = to(x, z, y, c)
                        there = (tx % self.G, tz % self.S, ty % self.Y, tc % self.G)
                        pairs.append((self.flat(x, z, y, c), self.flat(*there)))
        return lax.ppermute(value, ("group", "seq"), pairs)

    def flat(self, x, z, y, c):
        return x * self.n + (z * self.Y + y) * self.G + c


def call(kernel, outs, where, *arrays, scratch=(), copies=0, flops=0, fast=(), fast_in=(), still=False):
    moved = sum(a.size * a.dtype.itemsize for a in arrays)
    fast_in = range(len(arrays)) if fast_in is True else fast_in
    sems = [pltpu.SemaphoreType.DMA((copies,))] if copies else []
    return pl.pallas_call(
        kernel,
        out_shape=[jax.ShapeDtypeStruct(s, BF) for s in outs],
        in_specs=[pl.BlockSpec(memory_space=pltpu.SMEM)]
        + [
            pl.BlockSpec(memory_space=pltpu.VMEM if k in fast_in else pl.ANY)
            for k in range(len(arrays))
        ],
        out_specs=[
            pl.BlockSpec(memory_space=pltpu.VMEM if k in fast else pl.ANY)
            for k in range(len(outs))
        ],
        scratch_shapes=list(scratch) + sems,
        compiler_params=pltpu.CompilerParams(vmem_limit_bytes=40 * 2**20),
        cost_estimate=pl.CostEstimate(flops=flops, bytes_accessed=2 * moved, transcendentals=0),
    )(
        where,
        *(
            pltpu.with_memory_space_constraint(a, pltpu.HBM) if still and k not in fast_in else a
            for k, a in enumerate(arrays)
        ),
    )


def after(value, *others):
    return lax.optimization_barrier((value, *others))[0]


def copy_all(pairs, sems):
    copies = [pltpu.make_async_copy(a, b, sems.at[k]) for k, (a, b) in enumerate(pairs)]
    for copy in copies:
        copy.start()
    for copy in copies:
        copy.wait()


def join_kernel(where, hidden, skip, out, sems):
    copy_all([(hidden, out.at[0]), (skip, out.at[1])], sems)


def cut_kernel(G, S, Y, where, w_skip_any, w_qkv_any, w_out_any, *refs):
    outs, (w_skip, w_qkv, w_out, sems) = refs[:-4], refs[-4:]
    skips, qkvs, rest = outs[0], outs[1 : 1 + Y * G], outs[1 + Y * G]
    copy_all([(w_skip_any, w_skip), (w_qkv_any, w_qkv), (w_out_any, w_out)], sems)
    x, y, c = where[0], where[2], where[3]
    width = w_skip.shape[1]
    block, part, half = width // (G * Y), 3 * (S // G) * HD, width // G
    rows = w_skip.shape[0]
    for gx in range(G):
        for gy in range(Y):
            for e in range(Y):

                @pl.when((x == gx) & ((y + e) % Y == gy))
                def _():
                    b = gx * Y + gy
                    if e == 0:
                        skips[...] = w_skip[:, b * block : (b + 1) * block]
                    else:
                        for r in range(rows // HD):
                            qkvs[e * G][:, part + r * block : part + (r + 1) * block] = w_skip[
                                r * HD : (r + 1) * HD, b * block : (b + 1) * block
                            ]
                    for gc in range(G):
                        for f in range(G):

                            @pl.when((c + f) % G == gc)
                            def _():
                                for p in range(3):
                                    for t in range(S // G):
                                        head = ((gc * (S // G) + t) * Y + gy) * G + gx
                                        at = p * width + head * HD
                                        to = (p * (S // G) + t) * HD
                                        qkvs[e * G + f][:, to : to + HD] = w_qkv[:, at : at + HD]

    for gc in range(G):
        for f in range(G):

            @pl.when((c + f) % G == gc)
            def _():
                to = rest if f == 0 else qkvs[f]
                at = 0 if f == 0 else part
                to[:, at : at + half] = w_out[:, gc * half : (gc + 1) * half]

def stack_kernel(where, *refs):
    *pieces, out, sems = refs
    copy_all([(v, out.at[s]) for s, v in enumerate(pieces)], sems)


def ring_kernel(Y, part, where, own, *refs):
    others, out = refs[:-1], refs[-1]
    y = where[2]
    rows, cols = own.shape

    def place(e):
        return pl.multiple_of((y + Y - e) % Y * rows, 16)

    out[pl.ds(place(0), rows), :] = own[...]
    for e in range(1, Y):
        v = others[e - 1]
        both = [v[:, part + r * cols : part + (r + 1) * cols] for r in range(rows // HD)]
        out[pl.ds(place(e), rows), :] = jnp.concatenate(both, axis=0)


def shards_kernel(G, S, Y, where, *refs):
    qkvs, rest, out = refs[: Y * G], refs[Y * G], refs[Y * G + 1]
    x, y, c = where[0], where[2], where[3]
    part = 3 * (S // G) * HD
    wide = out.shape[1] - part
    for gy in range(Y):
        for gc in range(G):
            at = (gy * G + gc) * HD
            for e in range(Y):
                for f in range(G):

                    @pl.when(((y + Y - e) % Y == gy) & ((c + G - f) % G == gc))
                    def _():
                        out[at : at + HD, :part] = qkvs[e * G + f][:, :part]

            for f in range(G):

                @pl.when((c + G - f) % G == x)
                def _():
                    v, off = (qkvs[f], part) if f else (rest, 0)
                    k = gy * G + gc
                    out[at : at + HD, part:] = v[:, off + k * wide : off + (k + 1) * wide]


def merged_kernel(G, S, Y, where, *refs):
    z, c = where[1], where[3]
    blocks = Y * G
    parts, weights = refs[:blocks], refs[blocks : blocks + G * S]
    outs, (xs, ws, ms, sems) = refs[blocks + G * S : -4], refs[-4:]
    width = parts[0].shape[3]
    rows = weights[0].shape[0] // Y
    pairs = []
    for k in range(blocks):
        for h in range(2):
            pairs.append((parts[k].at[h], xs.at[k, :, :, pl.ds(h * width, width)]))
    for f in range(G):
        for s in range(S):
            for y in range(Y):
                to = ws.at[(z + S - s) % S, y, (c + G - f) % G]
                pairs.append((weights[f * S + s].at[pl.ds(y * rows, rows)], to))
    copy_all(pairs, sems)
    weight = ws[...].reshape(2 * width, ws.shape[-1])
    tokens = xs[...].reshape(-1, 2 * width)
    merged = jnp.dot(tokens, weight, preferred_element_type=F32).astype(BF)
    ms[...] = merged.reshape(ms.shape)
    for s in range(S):
        outs[s][...] = ms[:, (z + s) % S]


def norm88(v):
    mean = jnp.sum(v, axis=-1, keepdims=True) * (1.0 / HD)
    d = v - mean
    var = jnp.sum(d * d, axis=-1, keepdims=True) * (1.0 / HD)
    return d * lax.rsqrt(var + 1e-06)


def norm_kernel(G, S, Y, where, *refs):
    x, y = where[0], where[2]
    blocks = Y * G
    merged, mods, norm, base = refs[:blocks], refs[blocks], refs[blocks + 1], refs[blocks + 2]
    cols = merged[0].shape[3]
    toks = S * merged[0].shape[2]
    rows = blocks * toks
    width = cols * blocks

    total = jnp.zeros((rows, 1), F32)
    wide = []
    for e in range(Y):
        for d in range(G):
            own = [
                merged[e * G + d][:, (em - e) % Y * G + (dm - d) % G].reshape(toks, cols)
                for em in range(Y)
                for dm in range(G)
            ]
            base[(x + d) % G * Y + (y + e) % Y] = own[0]
            wide.append(jnp.concatenate(own, axis=0).astype(F32))
            total = total + jnp.sum(wide[-1], axis=-1, keepdims=True)
    mean = total * (1.0 / width)
    square = jnp.zeros((rows, 1), F32)
    for m in wide:
        square = square + jnp.sum((m - mean) ** 2, axis=-1, keepdims=True)
    inv = lax.rsqrt(square * (1.0 / width) + 1e-06)
    for e in range(Y):
        for d in range(G):
            b = (x + d) % G * Y + (y + e) % Y
            m = wide[e * G + d]
            norm[b] = ((m - mean) * inv * (1.0 + mods[blocks + b]) + mods[b]).astype(BF)


def attend_kernel(G, S, Y, where, norm, *refs):
    z, c = where[1], where[3]
    blocks = Y * G
    ws, refs = refs[: G * S], refs[G * S :]
    outs, att = refs[:blocks], refs[blocks]
    rows = norm.shape[1]
    toks = rows // blocks
    per = S // G
    part = 3 * per * HD
    for f in range(G):
        qkv = jnp.dot(norm[z], ws[f * S][:, :part], preferred_element_type=F32)
        for s in range(1, S):
            qkv = qkv + jnp.dot(
                norm[z ^ s], ws[f * S + s][:, :part], preferred_element_type=F32
            )
        for t in range(per):
            q, k, v = (qkv[:, (p * per + t) * HD : (p * per + t + 1) * HD] for p in range(3))
            q = (norm88(q) * HD ** (-0.5)).astype(BF)
            k = norm88(k).astype(BF)
            v = v.astype(BF)
            scores = lax.dot_general(q, k, (((1,), (1,)), ((), ())), preferred_element_type=F32)
            probs = jnp.exp(scores)
            scaled = 1.0 / jnp.sum(probs, axis=-1, keepdims=True)
            mixed = jnp.dot(probs.astype(BF), v, preferred_element_type=F32)
            att[(c + G - f) % G * per + t] = (mixed * scaled).astype(BF)
    for f in range(G):
        whole = []
        for s in range(S):
            pieces = [
                ws[f * S + s][k * HD : (k + 1) * HD, part:] for k in range(blocks)
            ]
            whole.append(jnp.concatenate(pieces, axis=1))
        acc = jnp.dot(att[z], whole[0], preferred_element_type=F32)
        for s in range(1, S):
            acc = acc + jnp.dot(att[z ^ s], whole[s], preferred_element_type=F32)
        acc = acc.astype(BF)
        for k in range(blocks):
            outs[k][(c + G - f) % G] = acc[k * toks : (k + 1) * toks, :]


def result_kernel(G, S, Y, where, mods, base, *refs):
    blocks = Y * G
    parts, outs = refs[:blocks], refs[blocks:]
    toks = base.shape[1]
    local = toks // S
    halves = []
    for h in range(G):
        acc = parts[0][h].astype(F32)
        for k in range(1, blocks):
            acc = acc + parts[k][h].astype(F32)
        halves.append(acc)
    projected = jnp.concatenate(halves, axis=1)
    merged = jnp.concatenate([base[b] for b in range(blocks)], axis=1).astype(F32)
    gate = jnp.concatenate([mods[2 * blocks + b] for b in range(blocks)], axis=1)
    result = (merged + gate * projected).astype(BF)
    for s in range(S):
        outs[s][...] = result[s * local : (s + 1) * local, :]


def home_kernel(S, where, *refs):
    z = where[1]
    copy_all([(refs[s], refs[S].at[(z + s) % S]) for s in range(S)], refs[S + 1])


def in_planes(groups, n, hidden, skip, timestep, w_skip, w_mod, w_qkv, w_out):
    S, local, width = hidden.shape
    p = Place(groups, n, S)
    G, Y = p.G, p.Y
    blocks = Y * G
    cols, half = width // blocks, width // G
    toks, rows = S * local, w_skip.shape[0]
    part = 3 * (S // G) * HD
    every = blocks * toks

    def swap(value, e, f):
        return p.send(value, lambda x, z, y, c: (x, z, y + e, c + f))

    outs = [(rows, cols)]
    for e in range(Y):
        for f in range(G):
            more = (half if f and not e else 0) + (2 * cols if e and not f else 0)
            outs.append((HD, part + more))
    outs.append((HD, half))
    skips, *qkvs, rest = call(
        partial(cut_kernel, G, S, Y),
        outs,
        p.where,
        w_skip,
        w_qkv,
        w_out,
        scratch=[pltpu.VMEM(w.shape, BF) for w in (w_skip, w_qkv, w_out)],
        copies=3,
        fast=range(len(outs)),
        still=True,
    )
    (joined,) = call(
        join_kernel, [(2, S, local, width)], p.where, hidden, skip, copies=2, fast=[0], still=True
    )
    qkvs[1 * G] = swap(qkvs[1 * G], 1, 0)
    parts = [
        p.send(joined, lambda x, z, y, c, e=e, d=d: (c - d, z, y - e, x))
        for e in range(Y)
        for d in range(G)
    ]
    for e in range(Y):
        for f in range(1, G):
            qkvs[e * G + f] = swap(after(qkvs[e * G + f], parts[G]), e, f)

    def step(value):
        return p.send(value, lambda x, z, y, c: (x, z + 1, y, c))

    def over_cores(held):
        return held + [swap(v, 0, f) for f in range(1, G) for v in held]

    (ring,) = call(
        partial(ring_kernel, Y, part),
        [(Y * rows, cols)],
        p.where,
        skips,
        *[qkvs[e * G] for e in range(1, Y)],
        fast=[0],
        fast_in=True,
    )
    (held,) = call(
        partial(shards_kernel, G, S, Y),
        [(blocks * HD, part + half // blocks)],
        p.where,
        *qkvs,
        rest,
        fast=[0],
        fast_in=True,
    )
    ws = [ring]
    ws.append(step(ring))
    ws.append(step(after(ws[1], *parts[:G])))
    ws.append(step(after(ws[2], *parts[G:])))
    ws = over_cores(ws)
    held = [after(held, ws[2])]
    held += [p.send(held[0], lambda x, z, y, c, k=k: (x, z ^ k, y, c)) for k in (1, 2)]

    times = p.send(timestep, lambda x, z, y, c: (c, z, y, x))
    mod = modulation(lax.dynamic_slice(times, (p.z,), (1,)), w_mod)
    mods = after(mod, p.where).reshape(3 * blocks, 1, cols)

    pieces = call(
        partial(merged_kernel, G, S, Y),
        [(blocks, local, cols)] * S,
        p.where,
        *parts,
        *ws,
        scratch=[
            pltpu.VMEM((blocks, S, local, 2 * width), BF),
            pltpu.VMEM((S, Y, G, rows, cols), BF),
            pltpu.VMEM((blocks, S, local, cols), BF),
        ],
        copies=2 * blocks + S * G * Y,
        flops=4 * every * width * cols,
        still=True,
        fast=range(S),
    )
    pieces = [pieces[0]] + [
        p.send(after(pieces[s], held[1], mods), lambda x, z, y, c, s=s: (x, z + s, y, c))
        for s in range(1, S)
    ]
    (merged,) = call(stack_kernel, [(S, blocks, local, cols)], p.where, *pieces, copies=S)
    held.append(p.send(after(held[2], merged), lambda x, z, y, c: (x, z ^ 1, y, c)))
    merged = [
        p.send(merged, lambda x, z, y, c, e=e, d=d: (x - d, z, y - e, c)) if e or d else merged
        for e in range(Y)
        for d in range(G)
    ]
    early = [after(v, *merged[1:]) for v in held[:3]]
    held += [swap(v, 0, f) for f in range(1, G) for v in (*early, held[3])]
    norm, base = call(
        partial(norm_kernel, G, S, Y),
        [(blocks, every, cols), (blocks, toks, cols)],
        p.where,
        *merged,
        mods,
        fast=range(2),
        fast_in=True,
    )
    parts = call(
        partial(attend_kernel, G, S, Y),
        [(G, toks, half)] * blocks,
        p.where,
        norm,
        *held,
        scratch=[pltpu.VMEM((S, every, HD), BF)],
        flops=10 * every * width * cols,
        fast=range(blocks),
        fast_in=True,
    )
    parts = [
        p.send(parts[e * G + d], lambda x, z, y, c, e=e, d=d: (x + d, z, y + e, c))
        if e or d
        else parts[0]
        for e in range(Y)
        for d in range(G)
    ]
    result = call(
        partial(result_kernel, G, S, Y),
        [(local, width)] * S,
        p.where,
        mods,
        base,
        *parts,
        fast=range(S),
        fast_in=True,
    )
    result = [p.send(result[s], lambda x, z, y, c, s=s: (c, z - s, y, x)) for s in range(S)]
    (out,) = call(
        partial(home_kernel, S), [(S, local, width)], p.where, *result, copies=S
    )
    return out


def solution(mesh):
    groups, n = mesh.shape["group"], mesh.shape["seq"]

    def per_device(*args):
        hidden, w_out = args[0], args[6]
        seqs, _, width = hidden.shape
        blocks = n // seqs
        fits = (
            groups == 2
            and blocks == groups * groups
            and n == seqs * blocks
            and blocks == seqs
            and w_out.shape[0] == HD
            and width % blocks == 0
            and (width // blocks) % 16 == 0
        )
        return in_planes(groups, n, *args) if fits else gathered(*args)

    placed = (
        P("group", "seq", None),
        P("group", "seq", None),
        P("group"),
        P("seq", None),
        P(),
        P("seq", None),
        P("seq", None),
    )
    return jax.shard_map(
        per_device, mesh=mesh, in_specs=placed, out_specs=P("group", "seq", None), check_vma=False
    )
```

```python
import math
from functools import partial

import jax
import jax.numpy as jnp
from jax import lax
from jax.experimental import pallas as pl
from jax.experimental.pallas import tpu as pltpu
from jax.sharding import PartitionSpec as P

H = 16
HD = 88
TDIM = 256
BF = jnp.bfloat16
F32 = jnp.float32


def layer_norm(x):
    mean = jnp.mean(x, axis=-1, keepdims=True)
    var = jnp.mean((x - mean) ** 2, axis=-1, keepdims=True)
    return (x - mean) * lax.rsqrt(var + 1e-06)


def modulation(timestep, w_mod):
    half = TDIM // 2
    freqs = jnp.exp(-math.log(10000.0) * jnp.arange(half, dtype=F32) / half)
    angles = timestep.astype(F32)[:, None] * freqs[None, :]
    embed = jnp.concatenate([jnp.cos(angles), jnp.sin(angles)], axis=1)
    act = jax.nn.silu(embed).astype(BF)
    return jnp.dot(act, w_mod, preferred_element_type=F32)


def attend_pair(trio):
    qpair, kpair, vpair = trio
    scores = jnp.einsum("qd,kd->qk", qpair, kpair, preferred_element_type=F32)
    probs = jax.nn.softmax(scores, axis=-1).astype(BF)
    return jnp.dot(probs, vpair, preferred_element_type=F32).astype(BF)


def to_heads(x, seqs, local):
    return jnp.transpose(x, (0, 2, 1, 3)).reshape(seqs * H, local, HD)


def gathered(hidden, skip, timestep, w_skip, w_mod, w_qkv, w_out):
    seqs, local, width = hidden.shape
    tok_rows = seqs * local
    combined = jnp.concatenate([hidden, skip], axis=2).reshape(tok_rows, 2 * width)
    full_skip = lax.all_gather(w_skip, "seq", axis=0, tiled=True)
    merged = jnp.dot(combined, full_skip, preferred_element_type=F32).astype(BF)
    mod = modulation(timestep, w_mod)
    shift, scale, gate = (mod[:, :width], mod[:, width : 2 * width], mod[:, 2 * width :])
    base = merged.astype(F32).reshape(seqs, local, width)
    normed = (layer_norm(base) * (1.0 + scale[:, None, :]) + shift[:, None, :]).astype(BF)
    full_qkv = lax.all_gather(w_qkv, "seq", axis=0, tiled=True)
    qkv = jnp.dot(normed.reshape(tok_rows, width), full_qkv, preferred_element_type=F32)
    qkv = qkv.reshape(seqs, local, 3, H, HD)
    query = (layer_norm(qkv[:, :, 0]) * HD ** (-0.5)).astype(BF)
    key = layer_norm(qkv[:, :, 1]).astype(BF)
    value = qkv[:, :, 2].astype(BF)
    trio = [
        lax.all_to_all(to_heads(x, seqs, local), "seq", split_axis=0, concat_axis=1, tiled=True)
        for x in (query, key, value)
    ]
    attended = lax.map(attend_pair, tuple(trio))
    attended = lax.all_to_all(attended, "seq", split_axis=1, concat_axis=0, tiled=True)
    attended = jnp.transpose(attended.reshape(seqs, H, local, HD), (0, 2, 1, 3))
    full_out = lax.all_gather(w_out, "seq", axis=0, tiled=True)
    projected = jnp.dot(
        attended.reshape(tok_rows, width), full_out, preferred_element_type=F32
    ).reshape(seqs, local, width)
    return (base + gate[:, None, :] * projected).astype(BF)


class Place:
    def __init__(self, groups, n, seqs):
        self.G, self.S = groups, seqs
        self.Y = n // seqs // groups
        self.n = n
        g, j = lax.axis_index("group"), lax.axis_index("seq")
        self.x, self.z = g, j // (n // seqs)
        self.y, self.c = (j // groups) % self.Y, j % groups
        self.where = jnp.stack([self.x, self.z, self.y, self.c]).astype(jnp.int32)
        self.cores = [[k * groups + f for f in range(groups)] for k in range(n // groups)]
        self.column = [[k * n // seqs + i for k in range(seqs)] for i in range(n // seqs)]

    def send(self, value, to):
        pairs = []
        for x in range(self.G):
            for z in range(self.S):
                for y in range(self.Y):
                    for c in range(self.G):
                        tx, tz, ty, tc = to(x, z, y, c)
                        there = (tx % self.G, tz % self.S, ty % self.Y, tc % self.G)
                        pairs.append((self.flat(x, z, y, c), self.flat(*there)))
        return lax.ppermute(value, ("group", "seq"), pairs)

    def flat(self, x, z, y, c):
        return x * self.n + (z * self.Y + y) * self.G + c


def call(kernel, outs, where, *arrays, scratch=(), copies=0, flops=0, fast=(), fast_in=(), still=False):
    moved = sum(a.size * a.dtype.itemsize for a in arrays)
    fast_in = range(len(arrays)) if fast_in is True else fast_in
    sems = [pltpu.SemaphoreType.DMA((copies,))] if copies else []
    return pl.pallas_call(
        kernel,
        out_shape=[jax.ShapeDtypeStruct(s, BF) for s in outs],
        in_specs=[pl.BlockSpec(memory_space=pltpu.SMEM)]
        + [
            pl.BlockSpec(memory_space=pltpu.VMEM if k in fast_in else pl.ANY)
            for k in range(len(arrays))
        ],
        out_specs=[
            pl.BlockSpec(memory_space=pltpu.VMEM if k in fast else pl.ANY)
            for k in range(len(outs))
        ],
        scratch_shapes=list(scratch) + sems,
        compiler_params=pltpu.CompilerParams(vmem_limit_bytes=40 * 2**20),
        cost_estimate=pl.CostEstimate(flops=flops, bytes_accessed=2 * moved, transcendentals=0),
    )(
        where,
        *(
            pltpu.with_memory_space_constraint(a, pltpu.HBM) if still and k not in fast_in else a
            for k, a in enumerate(arrays)
        ),
    )


def after(value, *others):
    return lax.optimization_barrier((value, *others))[0]


def copy_all(pairs, sems):
    copies = [pltpu.make_async_copy(a, b, sems.at[k]) for k, (a, b) in enumerate(pairs)]
    for copy in copies:
        copy.start()
    for copy in copies:
        copy.wait()


def join_kernel(where, hidden, skip, out, sems):
    copy_all([(hidden, out.at[0]), (skip, out.at[1])], sems)


def cut_kernel(G, S, Y, where, w_skip_any, w_qkv_any, w_out_any, *refs):
    outs, (w_skip, w_qkv, w_out, sems) = refs[:-4], refs[-4:]
    skips, qkvs, rest = outs[0], outs[1 : 1 + Y * G], outs[1 + Y * G]
    copy_all([(w_skip_any, w_skip), (w_qkv_any, w_qkv), (w_out_any, w_out)], sems)
    x, y, c = where[0], where[2], where[3]
    width = w_skip.shape[1]
    block, part, half = width // (G * Y), 3 * (S // G) * HD, width // G
    rows = w_skip.shape[0]
    for gx in range(G):
        for gy in range(Y):
            for e in range(Y):

                @pl.when((x == gx) & ((y + e) % Y == gy))
                def _():
                    b = gx * Y + gy
                    if e == 0:
                        skips[...] = w_skip[:, b * block : (b + 1) * block]
                    else:
                        for r in range(rows // HD):
                            qkvs[e * G][:, part + r * block : part + (r + 1) * block] = w_skip[
                                r * HD : (r + 1) * HD, b * block : (b + 1) * block
                            ]
                    for gc in range(G):
                        for f in range(G):

                            @pl.when((c + f) % G == gc)
                            def _():
                                for p in range(3):
                                    for t in range(S // G):
                                        head = ((gc * (S // G) + t) * Y + gy) * G + gx
                                        at = p * width + head * HD
                                        to = (p * (S // G) + t) * HD
                                        qkvs[e * G + f][:, to : to + HD] = w_qkv[:, at : at + HD]

    for gc in range(G):
        for f in range(G):

            @pl.when((c + f) % G == gc)
            def _():
                to = rest if f == 0 else qkvs[f]
                at = 0 if f == 0 else part
                to[:, at : at + half] = w_out[:, gc * half : (gc + 1) * half]

def stack_kernel(where, *refs):
    *pieces, out = refs
    for s, v in enumerate(pieces):
        out[s] = v[...]


def ring_kernel(Y, part, where, own, *refs):
    others, out = refs[:-1], refs[-1]
    y = where[2]
    rows, cols = own.shape

    def place(e):
        return pl.multiple_of((y + Y - e) % Y * rows, 16)

    out[pl.ds(place(0), rows), :] = own[...]
    for e in range(1, Y):
        v = others[e - 1]
        both = [v[:, part + r * cols : part + (r + 1) * cols] for r in range(rows // HD)]
        out[pl.ds(place(e), rows), :] = jnp.concatenate(both, axis=0)


def shards_kernel(G, S, Y, where, *refs):
    qkvs, rest, out = refs[: Y * G], refs[Y * G], refs[Y * G + 1]
    x, y, c = where[0], where[2], where[3]
    part = 3 * (S // G) * HD
    wide = out.shape[1] - part
    for gy in range(Y):
        for gc in range(G):
            at = (gy * G + gc) * HD
            for e in range(Y):
                for f in range(G):

                    @pl.when(((y + Y - e) % Y == gy) & ((c + G - f) % G == gc))
                    def _():
                        out[at : at + HD, :part] = qkvs[e * G + f][:, :part]

            for f in range(G):

                @pl.when((c + G - f) % G == x)
                def _():
                    v, off = (qkvs[f], part) if f else (rest, 0)
                    k = gy * G + gc
                    out[at : at + HD, part:] = v[:, off + k * wide : off + (k + 1) * wide]


def merged_kernel(G, S, Y, where, *refs):
    z, c = where[1], where[3]
    blocks = Y * G
    parts, weights = refs[:blocks], refs[blocks : blocks + G * S]
    outs, (xs, ws, ms, sems) = refs[blocks + G * S : -4], refs[-4:]
    width = parts[0].shape[3]
    rows = weights[0].shape[0] // Y
    pairs = []
    for k in range(blocks):
        for h in range(2):
            pairs.append((parts[k].at[h], xs.at[k, :, :, pl.ds(h * width, width)]))
    for f in range(G):
        for s in range(S):
            for y in range(Y):
                to = ws.at[(z + S - s) % S, y, (c + G - f) % G]
                pairs.append((weights[f * S + s].at[pl.ds(y * rows, rows)], to))
    copy_all(pairs, sems)
    weight = ws[...].reshape(2 * width, ws.shape[-1])
    tokens = xs[...].reshape(-1, 2 * width)
    merged = jnp.dot(tokens, weight, preferred_element_type=F32).astype(BF)
    ms[...] = merged.reshape(ms.shape)
    for s in range(S):
        outs[s][...] = ms[:, (z + s) % S]


def norm88(v):
    mean = jnp.sum(v, axis=-1, keepdims=True) * (1.0 / HD)
    d = v - mean
    var = jnp.sum(d * d, axis=-1, keepdims=True) * (1.0 / HD)
    return d * lax.rsqrt(var + 1e-06)


def norm_kernel(G, S, Y, where, *refs):
    x, y = where[0], where[2]
    blocks = Y * G
    merged, mods, norm, base = refs[:blocks], refs[blocks], refs[blocks + 1], refs[blocks + 2]
    cols = merged[0].shape[3]
    toks = S * merged[0].shape[2]
    rows = blocks * toks
    width = cols * blocks

    total = jnp.zeros((rows, 1), F32)
    wide = []
    for e in range(Y):
        for d in range(G):
            own = [
                merged[e * G + d][:, (em - e) % Y * G + (dm - d) % G].reshape(toks, cols)
                for em in range(Y)
                for dm in range(G)
            ]
            base[(x + d) % G * Y + (y + e) % Y] = own[0]
            wide.append(jnp.concatenate(own, axis=0).astype(F32))
            total = total + jnp.sum(wide[-1], axis=-1, keepdims=True)
    mean = total * (1.0 / width)
    square = jnp.zeros((rows, 1), F32)
    for m in wide:
        square = square + jnp.sum((m - mean) ** 2, axis=-1, keepdims=True)
    inv = lax.rsqrt(square * (1.0 / width) + 1e-06)
    for e in range(Y):
        for d in range(G):
            b = (x + d) % G * Y + (y + e) % Y
            m = wide[e * G + d]
            norm[b] = ((m - mean) * inv * (1.0 + mods[blocks + b]) + mods[b]).astype(BF)


def attend_kernel(G, S, Y, where, norm, *refs):
    z, c = where[1], where[3]
    blocks = Y * G
    ws, refs = refs[: G * S], refs[G * S :]
    outs, att = refs[:blocks], refs[blocks]
    rows = norm.shape[1]
    toks = rows // blocks
    per = S // G
    part = 3 * per * HD
    for f in range(G):
        qkv = jnp.dot(norm[z], ws[f * S][:, :part], preferred_element_type=F32)
        for s in range(1, S):
            qkv = qkv + jnp.dot(
                norm[z ^ s], ws[f * S + s][:, :part], preferred_element_type=F32
            )
        for t in range(per):
            q, k, v = (qkv[:, (p * per + t) * HD : (p * per + t + 1) * HD] for p in range(3))
            q = (norm88(q) * HD ** (-0.5)).astype(BF)
            k = norm88(k).astype(BF)
            v = v.astype(BF)
            scores = lax.dot_general(q, k, (((1,), (1,)), ((), ())), preferred_element_type=F32)
            probs = jnp.exp(scores)
            scaled = 1.0 / jnp.sum(probs, axis=-1, keepdims=True)
            mixed = jnp.dot(probs.astype(BF), v, preferred_element_type=F32)
            att[(c + G - f) % G * per + t] = (mixed * scaled).astype(BF)
    for f in range(G):
        whole = []
        for s in range(S):
            pieces = [
                ws[f * S + s][k * HD : (k + 1) * HD, part:] for k in range(blocks)
            ]
            whole.append(jnp.concatenate(pieces, axis=1))
        acc = jnp.dot(att[z], whole[0], preferred_element_type=F32)
        for s in range(1, S):
            acc = acc + jnp.dot(att[z ^ s], whole[s], preferred_element_type=F32)
        acc = acc.astype(BF)
        for k in range(blocks):
            outs[k][(c + G - f) % G] = acc[k * toks : (k + 1) * toks, :]


def result_kernel(G, S, Y, where, mods, base, *refs):
    blocks = Y * G
    parts, outs = refs[:blocks], refs[blocks:]
    toks = base.shape[1]
    local = toks // S
    halves = []
    for h in range(G):
        acc = parts[0][h].astype(F32)
        for k in range(1, blocks):
            acc = acc + parts[k][h].astype(F32)
        halves.append(acc)
    projected = jnp.concatenate(halves, axis=1)
    merged = jnp.concatenate([base[b] for b in range(blocks)], axis=1).astype(F32)
    gate = jnp.concatenate([mods[2 * blocks + b] for b in range(blocks)], axis=1)
    result = (merged + gate * projected).astype(BF)
    for s in range(S):
        outs[s][...] = result[s * local : (s + 1) * local, :]


def home_kernel(S, where, *refs):
    z = where[1]
    copy_all([(refs[s], refs[S].at[(z + s) % S]) for s in range(S)], refs[S + 1])


def in_planes(groups, n, hidden, skip, timestep, w_skip, w_mod, w_qkv, w_out):
    S, local, width = hidden.shape
    p = Place(groups, n, S)
    G, Y = p.G, p.Y
    blocks = Y * G
    cols, half = width // blocks, width // G
    toks, rows = S * local, w_skip.shape[0]
    part = 3 * (S // G) * HD
    every = blocks * toks

    def swap(value, e, f):
        return p.send(value, lambda x, z, y, c: (x, z, y + e, c + f))

    outs = [(rows, cols)]
    for e in range(Y):
        for f in range(G):
            more = (half if f and not e else 0) + (2 * cols if e and not f else 0)
            outs.append((HD, part + more))
    outs.append((HD, half))
    skips, *qkvs, rest = call(
        partial(cut_kernel, G, S, Y),
        outs,
        p.where,
        w_skip,
        w_qkv,
        w_out,
        scratch=[pltpu.VMEM(w.shape, BF) for w in (w_skip, w_qkv, w_out)],
        copies=3,
        fast=range(len(outs)),
        still=True,
    )
    (joined,) = call(
        join_kernel, [(2, S, local, width)], p.where, hidden, skip, copies=2, fast=[0], still=True
    )
    qkvs[1 * G] = swap(qkvs[1 * G], 1, 0)
    parts = [
        p.send(joined, lambda x, z, y, c, e=e, d=d: (c - d, z, y - e, x))
        for e in range(Y)
        for d in range(G)
    ]
    for e in range(Y):
        for f in range(1, G):
            qkvs[e * G + f] = swap(after(qkvs[e * G + f], parts[G]), e, f)

    def step(value):
        return p.send(value, lambda x, z, y, c: (x, z + 1, y, c))

    def over_cores(held):
        return held + [swap(v, 0, f) for f in range(1, G) for v in held]

    (ring,) = call(
        partial(ring_kernel, Y, part),
        [(Y * rows, cols)],
        p.where,
        skips,
        *[qkvs[e * G] for e in range(1, Y)],
        fast=[0],
        fast_in=True,
    )
    (held,) = call(
        partial(shards_kernel, G, S, Y),
        [(blocks * HD, part + half // blocks)],
        p.where,
        *qkvs,
        rest,
        fast=[0],
        fast_in=True,
    )
    ws = [ring]
    ws.append(step(ring))
    ws.append(step(after(ws[1], *parts[:G])))
    ws.append(step(after(ws[2], *parts[G:])))
    ws = over_cores(ws)
    held = [after(held, ws[2])]
    held += [p.send(held[0], lambda x, z, y, c, k=k: (x, z ^ k, y, c)) for k in (1, 2)]

    times = p.send(timestep, lambda x, z, y, c: (c, z, y, x))
    mod = modulation(lax.dynamic_slice(times, (p.z,), (1,)), w_mod)
    mods = after(mod, p.where).reshape(3 * blocks, 1, cols)

    pieces = call(
        partial(merged_kernel, G, S, Y),
        [(blocks, local, cols)] * S,
        p.where,
        *parts,
        *ws,
        scratch=[
            pltpu.VMEM((blocks, S, local, 2 * width), BF),
            pltpu.VMEM((S, Y, G, rows, cols), BF),
            pltpu.VMEM((blocks, S, local, cols), BF),
        ],
        copies=2 * blocks + S * G * Y,
        flops=4 * every * width * cols,
        still=True,
        fast=range(S),
    )
    pieces = [pieces[0]] + [
        p.send(after(pieces[s], held[1], mods), lambda x, z, y, c, s=s: (x, z + s, y, c))
        for s in range(1, S)
    ]
    (merged,) = call(stack_kernel, [(S, blocks, local, cols)], p.where, *pieces, fast=[0], fast_in=True)
    held.append(p.send(after(held[2], merged), lambda x, z, y, c: (x, z ^ 1, y, c)))
    merged = [
        p.send(merged, lambda x, z, y, c, e=e, d=d: (x - d, z, y - e, c)) if e or d else merged
        for e in range(Y)
        for d in range(G)
    ]
    early = [after(v, *merged[1:]) for v in held[:3]]
    held += [swap(v, 0, f) for f in range(1, G) for v in (*early, held[3])]
    norm, base = call(
        partial(norm_kernel, G, S, Y),
        [(blocks, every, cols), (blocks, toks, cols)],
        p.where,
        *merged,
        mods,
        fast=range(2),
        fast_in=True,
    )
    parts = call(
        partial(attend_kernel, G, S, Y),
        [(G, toks, half)] * blocks,
        p.where,
        norm,
        *held,
        scratch=[pltpu.VMEM((S, every, HD), BF)],
        flops=10 * every * width * cols,
        fast=range(blocks),
        fast_in=True,
    )
    parts = [
        p.send(parts[e * G + d], lambda x, z, y, c, e=e, d=d: (x + d, z, y + e, c))
        if e or d
        else parts[0]
        for e in range(Y)
        for d in range(G)
    ]
    result = call(
        partial(result_kernel, G, S, Y),
        [(local, width)] * S,
        p.where,
        mods,
        base,
        *parts,
        fast=range(S),
        fast_in=True,
    )
    result = [p.send(result[s], lambda x, z, y, c, s=s: (c, z - s, y, x)) for s in range(S)]
    (out,) = call(
        partial(home_kernel, S), [(S, local, width)], p.where, *result, copies=S
    )
    return out


def solution(mesh):
    groups, n = mesh.shape["group"], mesh.shape["seq"]

    def per_device(*args):
        hidden, w_out = args[0], args[6]
        seqs, _, width = hidden.shape
        blocks = n // seqs
        fits = (
            groups == 2
            and blocks == groups * groups
            and n == seqs * blocks
            and blocks == seqs
            and w_out.shape[0] == HD
            and width % blocks == 0
            and (width // blocks) % 16 == 0
        )
        return in_planes(groups, n, *args) if fits else gathered(*args)

    placed = (
        P("group", "seq", None),
        P("group", "seq", None),
        P("group"),
        P("seq", None),
        P(),
        P("seq", None),
        P("seq", None),
    )
    return jax.shard_map(
        per_device, mesh=mesh, in_specs=placed, out_specs=P("group", "seq", None), check_vma=False
    )
```

```python
import math
from functools import partial

import jax
import jax.numpy as jnp
from jax import lax
from jax.experimental import pallas as pl
from jax.experimental.pallas import tpu as pltpu
from jax.sharding import PartitionSpec as P

H = 16
HD = 88
TDIM = 256
BF = jnp.bfloat16
F32 = jnp.float32


def layer_norm(x):
    mean = jnp.mean(x, axis=-1, keepdims=True)
    var = jnp.mean((x - mean) ** 2, axis=-1, keepdims=True)
    return (x - mean) * lax.rsqrt(var + 1e-06)


def modulation(timestep, w_mod):
    half = TDIM // 2
    freqs = jnp.exp(-math.log(10000.0) * jnp.arange(half, dtype=F32) / half)
    angles = timestep.astype(F32)[:, None] * freqs[None, :]
    embed = jnp.concatenate([jnp.cos(angles), jnp.sin(angles)], axis=1)
    act = jax.nn.silu(embed).astype(BF)
    return jnp.dot(act, w_mod, preferred_element_type=F32)


def attend_pair(trio):
    qpair, kpair, vpair = trio
    scores = jnp.einsum("qd,kd->qk", qpair, kpair, preferred_element_type=F32)
    probs = jax.nn.softmax(scores, axis=-1).astype(BF)
    return jnp.dot(probs, vpair, preferred_element_type=F32).astype(BF)


def to_heads(x, seqs, local):
    return jnp.transpose(x, (0, 2, 1, 3)).reshape(seqs * H, local, HD)


def gathered(hidden, skip, timestep, w_skip, w_mod, w_qkv, w_out):
    seqs, local, width = hidden.shape
    tok_rows = seqs * local
    combined = jnp.concatenate([hidden, skip], axis=2).reshape(tok_rows, 2 * width)
    full_skip = lax.all_gather(w_skip, "seq", axis=0, tiled=True)
    merged = jnp.dot(combined, full_skip, preferred_element_type=F32).astype(BF)
    mod = modulation(timestep, w_mod)
    shift, scale, gate = (mod[:, :width], mod[:, width : 2 * width], mod[:, 2 * width :])
    base = merged.astype(F32).reshape(seqs, local, width)
    normed = (layer_norm(base) * (1.0 + scale[:, None, :]) + shift[:, None, :]).astype(BF)
    full_qkv = lax.all_gather(w_qkv, "seq", axis=0, tiled=True)
    qkv = jnp.dot(normed.reshape(tok_rows, width), full_qkv, preferred_element_type=F32)
    qkv = qkv.reshape(seqs, local, 3, H, HD)
    query = (layer_norm(qkv[:, :, 0]) * HD ** (-0.5)).astype(BF)
    key = layer_norm(qkv[:, :, 1]).astype(BF)
    value = qkv[:, :, 2].astype(BF)
    trio = [
        lax.all_to_all(to_heads(x, seqs, local), "seq", split_axis=0, concat_axis=1, tiled=True)
        for x in (query, key, value)
    ]
    attended = lax.map(attend_pair, tuple(trio))
    attended = lax.all_to_all(attended, "seq", split_axis=1, concat_axis=0, tiled=True)
    attended = jnp.transpose(attended.reshape(seqs, H, local, HD), (0, 2, 1, 3))
    full_out = lax.all_gather(w_out, "seq", axis=0, tiled=True)
    projected = jnp.dot(
        attended.reshape(tok_rows, width), full_out, preferred_element_type=F32
    ).reshape(seqs, local, width)
    return (base + gate[:, None, :] * projected).astype(BF)


class Place:
    def __init__(self, groups, n, seqs):
        self.G, self.S = groups, seqs
        self.Y = n // seqs // groups
        self.n = n
        g, j = lax.axis_index("group"), lax.axis_index("seq")
        self.x, self.z = g, j // (n // seqs)
        self.y, self.c = (j // groups) % self.Y, j % groups
        self.where = jnp.stack([self.x, self.z, self.y, self.c]).astype(jnp.int32)
        self.cores = [[k * groups + f for f in range(groups)] for k in range(n // groups)]
        self.column = [[k * n // seqs + i for k in range(seqs)] for i in range(n // seqs)]

    def send(self, value, to):
        pairs = []
        for x in range(self.G):
            for z in range(self.S):
                for y in range(self.Y):
                    for c in range(self.G):
                        tx, tz, ty, tc = to(x, z, y, c)
                        there = (tx % self.G, tz % self.S, ty % self.Y, tc % self.G)
                        pairs.append((self.flat(x, z, y, c), self.flat(*there)))
        return lax.ppermute(value, ("group", "seq"), pairs)

    def flat(self, x, z, y, c):
        return x * self.n + (z * self.Y + y) * self.G + c


def call(kernel, outs, where, *arrays, scratch=(), copies=0, flops=0, fast=(), fast_in=(), still=False):
    moved = sum(a.size * a.dtype.itemsize for a in arrays)
    fast_in = range(len(arrays)) if fast_in is True else fast_in
    sems = [pltpu.SemaphoreType.DMA((copies,))] if copies else []
    return pl.pallas_call(
        kernel,
        out_shape=[jax.ShapeDtypeStruct(s, BF) for s in outs],
        in_specs=[pl.BlockSpec(memory_space=pltpu.SMEM)]
        + [
            pl.BlockSpec(memory_space=pltpu.VMEM if k in fast_in else pl.ANY)
            for k in range(len(arrays))
        ],
        out_specs=[
            pl.BlockSpec(memory_space=pltpu.VMEM if k in fast else pl.ANY)
            for k in range(len(outs))
        ],
        scratch_shapes=list(scratch) + sems,
        compiler_params=pltpu.CompilerParams(vmem_limit_bytes=40 * 2**20),
        cost_estimate=pl.CostEstimate(flops=flops, bytes_accessed=2 * moved, transcendentals=0),
    )(
        where,
        *(
            pltpu.with_memory_space_constraint(a, pltpu.HBM) if still and k not in fast_in else a
            for k, a in enumerate(arrays)
        ),
    )


def after(value, *others):
    return lax.optimization_barrier((value, *others))[0]


def copy_all(pairs, sems):
    copies = [pltpu.make_async_copy(a, b, sems.at[k]) for k, (a, b) in enumerate(pairs)]
    for copy in copies:
        copy.start()
    for copy in copies:
        copy.wait()


def join_kernel(where, hidden, skip, out, sems):
    copy_all([(hidden, out.at[0]), (skip, out.at[1])], sems)


def cut_kernel(G, S, Y, where, w_skip_any, w_qkv_any, w_out_any, *refs):
    outs, (w_skip, w_qkv, w_out, sems) = refs[:-4], refs[-4:]
    skips, qkvs, rest = outs[0], outs[1 : 1 + Y * G], outs[1 + Y * G]
    copy_all([(w_skip_any, w_skip), (w_qkv_any, w_qkv), (w_out_any, w_out)], sems)
    x, y, c = where[0], where[2], where[3]
    width = w_skip.shape[1]
    block, part, half = width // (G * Y), 3 * (S // G) * HD, width // G
    rows = w_skip.shape[0]
    for gx in range(G):
        for gy in range(Y):
            for e in range(Y):

                @pl.when((x == gx) & ((y + e) % Y == gy))
                def _():
                    b = gx * Y + gy
                    if e == 0:
                        skips[...] = w_skip[:, b * block : (b + 1) * block]
                    else:
                        for r in range(rows // HD):
                            qkvs[e * G][:, part + r * block : part + (r + 1) * block] = w_skip[
                                r * HD : (r + 1) * HD, b * block : (b + 1) * block
                            ]
                    for gc in range(G):
                        for f in range(G):

                            @pl.when((c + f) % G == gc)
                            def _():
                                for p in range(3):
                                    for t in range(S // G):
                                        head = ((gc * (S // G) + t) * Y + gy) * G + gx
                                        at = p * width + head * HD
                                        to = (p * (S // G) + t) * HD
                                        qkvs[e * G + f][:, to : to + HD] = w_qkv[:, at : at + HD]

    for gc in range(G):
        for f in range(G):

            @pl.when((c + f) % G == gc)
            def _():
                to = rest if f == 0 else qkvs[f]
                at = 0 if f == 0 else part
                to[:, at : at + half] = w_out[:, gc * half : (gc + 1) * half]

def stack_kernel(where, *refs):
    *pieces, out = refs
    for s, v in enumerate(pieces):
        out[s] = v[...]


def ring_kernel(Y, part, where, own, *refs):
    others, out = refs[:-1], refs[-1]
    y = where[2]
    rows, cols = own.shape

    def place(e):
        return pl.multiple_of((y + Y - e) % Y * rows, 16)

    out[pl.ds(place(0), rows), :] = own[...]
    for e in range(1, Y):
        v = others[e - 1]
        both = [v[:, part + r * cols : part + (r + 1) * cols] for r in range(rows // HD)]
        out[pl.ds(place(e), rows), :] = jnp.concatenate(both, axis=0)


def shards_kernel(G, S, Y, where, *refs):
    qkvs, rest, out = refs[: Y * G], refs[Y * G], refs[Y * G + 1]
    x, y, c = where[0], where[2], where[3]
    part = 3 * (S // G) * HD
    wide = out.shape[1] - part
    for gy in range(Y):
        for gc in range(G):
            at = (gy * G + gc) * HD
            for e in range(Y):
                for f in range(G):

                    @pl.when(((y + Y - e) % Y == gy) & ((c + G - f) % G == gc))
                    def _():
                        out[at : at + HD, :part] = qkvs[e * G + f][:, :part]

            for f in range(G):

                @pl.when((c + G - f) % G == x)
                def _():
                    v, off = (qkvs[f], part) if f else (rest, 0)
                    k = gy * G + gc
                    out[at : at + HD, part:] = v[:, off + k * wide : off + (k + 1) * wide]


def merged_kernel(G, S, Y, where, *refs):
    z, c = where[1], where[3]
    blocks = Y * G
    parts, weights = refs[:blocks], refs[blocks : blocks + G * S]
    outs, (xs, ws, ms, sems) = refs[blocks + G * S : -4], refs[-4:]
    width = parts[0].shape[3]
    rows = weights[0].shape[0] // Y
    pairs = []
    for k in range(blocks):
        for h in range(2):
            pairs.append((parts[k].at[h], xs.at[k, :, :, pl.ds(h * width, width)]))
    for f in range(G):
        for s in range(S):
            for y in range(Y):
                to = ws.at[(z + S - s) % S, y, (c + G - f) % G]
                pairs.append((weights[f * S + s].at[pl.ds(y * rows, rows)], to))
    copy_all(pairs, sems)
    weight = ws[...].reshape(2 * width, ws.shape[-1])
    tokens = xs[...].reshape(-1, 2 * width)
    merged = jnp.dot(tokens, weight, preferred_element_type=F32).astype(BF)
    ms[...] = merged.reshape(ms.shape)
    for s in range(S):
        outs[s][...] = ms[:, (z + s) % S]


def norm88(v):
    mean = jnp.sum(v, axis=-1, keepdims=True) * (1.0 / HD)
    d = v - mean
    var = jnp.sum(d * d, axis=-1, keepdims=True) * (1.0 / HD)
    return d * lax.rsqrt(var + 1e-06)


def norm_kernel(G, S, Y, where, *refs):
    x, y = where[0], where[2]
    blocks = Y * G
    merged, mods, norm, base = refs[:blocks], refs[blocks], refs[blocks + 1], refs[blocks + 2]
    cols = merged[0].shape[3]
    toks = S * merged[0].shape[2]
    rows = blocks * toks
    width = cols * blocks

    total = jnp.zeros((rows, 1), F32)
    wide = []
    for e in range(Y):
        for d in range(G):
            own = [
                merged[e * G + d][:, (em - e) % Y * G + (dm - d) % G].reshape(toks, cols)
                for em in range(Y)
                for dm in range(G)
            ]
            base[(x + d) % G * Y + (y + e) % Y] = own[0]
            wide.append(jnp.concatenate(own, axis=0).astype(F32))
            total = total + jnp.sum(wide[-1], axis=-1, keepdims=True)
    mean = total * (1.0 / width)
    square = jnp.zeros((rows, 1), F32)
    for m in wide:
        square = square + jnp.sum((m - mean) ** 2, axis=-1, keepdims=True)
    inv = lax.rsqrt(square * (1.0 / width) + 1e-06)
    for e in range(Y):
        for d in range(G):
            b = (x + d) % G * Y + (y + e) % Y
            m = wide[e * G + d]
            norm[b] = ((m - mean) * inv * (1.0 + mods[blocks + b]) + mods[b]).astype(BF)


def attend_kernel(G, S, Y, where, norm, *refs):
    z, c = where[1], where[3]
    blocks = Y * G
    ws, refs = refs[: G * S], refs[G * S :]
    outs, att = refs[:blocks], refs[blocks]
    rows = norm.shape[1]
    toks = rows // blocks
    per = S // G
    part = 3 * per * HD
    for f in range(G):
        qkv = jnp.dot(norm[z], ws[f * S][:, :part], preferred_element_type=F32)
        for s in range(1, S):
            qkv = qkv + jnp.dot(
                norm[z ^ s], ws[f * S + s][:, :part], preferred_element_type=F32
            )
        for t in range(per):
            q, k, v = (qkv[:, (p * per + t) * HD : (p * per + t + 1) * HD] for p in range(3))
            q = (norm88(q) * HD ** (-0.5)).astype(BF)
            k = norm88(k).astype(BF)
            v = v.astype(BF)
            scores = lax.dot_general(q, k, (((1,), (1,)), ((), ())), preferred_element_type=F32)
            probs = jnp.exp(scores)
            scaled = 1.0 / jnp.sum(probs, axis=-1, keepdims=True)
            mixed = jnp.dot(probs.astype(BF), v, preferred_element_type=F32)
            att[(c + G - f) % G * per + t] = (mixed * scaled).astype(BF)
    for f in range(G):
        whole = []
        for s in range(S):
            pieces = [
                ws[f * S + s][k * HD : (k + 1) * HD, part:] for k in range(blocks)
            ]
            whole.append(jnp.concatenate(pieces, axis=1))
        acc = jnp.dot(att[z], whole[0], preferred_element_type=F32)
        for s in range(1, S):
            acc = acc + jnp.dot(att[z ^ s], whole[s], preferred_element_type=F32)
        acc = acc.astype(BF)
        for k in range(blocks):
            outs[k][(c + G - f) % G] = acc[k * toks : (k + 1) * toks, :]


def result_kernel(G, S, Y, where, mods, base, *refs):
    blocks = Y * G
    parts, outs = refs[:blocks], refs[blocks:]
    toks = base.shape[1]
    local = toks // S
    halves = []
    for h in range(G):
        acc = parts[0][h].astype(F32)
        for k in range(1, blocks):
            acc = acc + parts[k][h].astype(F32)
        halves.append(acc)
    projected = jnp.concatenate(halves, axis=1)
    merged = jnp.concatenate([base[b] for b in range(blocks)], axis=1).astype(F32)
    gate = jnp.concatenate([mods[2 * blocks + b] for b in range(blocks)], axis=1)
    result = (merged + gate * projected).astype(BF)
    for s in range(S):
        outs[s][...] = result[s * local : (s + 1) * local, :]


def home_kernel(S, where, *refs):
    z = where[1]
    copy_all([(refs[s], refs[S].at[(z + s) % S]) for s in range(S)], refs[S + 1])


def in_planes(groups, n, hidden, skip, timestep, w_skip, w_mod, w_qkv, w_out):
    S, local, width = hidden.shape
    p = Place(groups, n, S)
    G, Y = p.G, p.Y
    blocks = Y * G
    cols, half = width // blocks, width // G
    toks, rows = S * local, w_skip.shape[0]
    part = 3 * (S // G) * HD
    every = blocks * toks

    def swap(value, e, f):
        return p.send(value, lambda x, z, y, c: (x, z, y + e, c + f))

    outs = [(rows, cols)]
    for e in range(Y):
        for f in range(G):
            more = (half if f and not e else 0) + (2 * cols if e and not f else 0)
            outs.append((HD, part + more))
    outs.append((HD, half))
    skips, *qkvs, rest = call(
        partial(cut_kernel, G, S, Y),
        outs,
        p.where,
        w_skip,
        w_qkv,
        w_out,
        scratch=[pltpu.VMEM(w.shape, BF) for w in (w_skip, w_qkv, w_out)],
        copies=3,
        fast=range(len(outs)),
        still=True,
    )
    (joined,) = call(
        join_kernel, [(2, S, local, width)], p.where, hidden, skip, copies=2, fast=[0], still=True
    )
    qkvs[1 * G] = swap(qkvs[1 * G], 1, 0)
    parts = [
        p.send(joined, lambda x, z, y, c, e=e, d=d: (c - d, z, y - e, x))
        for e in range(Y)
        for d in range(G)
    ]
    for e in range(Y):
        for f in range(1, G):
            qkvs[e * G + f] = swap(after(qkvs[e * G + f], parts[G]), e, f)

    def step(value):
        return p.send(value, lambda x, z, y, c: (x, z + 1, y, c))

    def over_cores(held):
        return held + [swap(v, 0, f) for f in range(1, G) for v in held]

    (ring,) = call(
        partial(ring_kernel, Y, part),
        [(Y * rows, cols)],
        p.where,
        skips,
        *[qkvs[e * G] for e in range(1, Y)],
        fast=[0],
        fast_in=True,
    )
    (held,) = call(
        partial(shards_kernel, G, S, Y),
        [(blocks * HD, part + half // blocks)],
        p.where,
        *qkvs,
        rest,
        fast=[0],
        fast_in=True,
    )
    ws = [ring]
    ws.append(step(ring))
    ws.append(step(after(ws[1], *parts[:G])))
    ws.append(step(after(ws[2], *parts[G:])))
    ws = over_cores(ws)
    held = [after(held, ws[2])]
    held += [p.send(held[0], lambda x, z, y, c, k=k: (x, z ^ k, y, c)) for k in (1, 2)]

    times = p.send(timestep, lambda x, z, y, c: (c, z, y, x))
    mod = modulation(lax.dynamic_slice(times, (p.z,), (1,)), w_mod)
    mods = mod.reshape(3 * blocks, 1, cols)

    pieces = call(
        partial(merged_kernel, G, S, Y),
        [(blocks, local, cols)] * S,
        p.where,
        *parts,
        *ws,
        scratch=[
            pltpu.VMEM((blocks, S, local, 2 * width), BF),
            pltpu.VMEM((S, Y, G, rows, cols), BF),
            pltpu.VMEM((blocks, S, local, cols), BF),
        ],
        copies=2 * blocks + S * G * Y,
        flops=4 * every * width * cols,
        still=True,
        fast=range(S),
    )
    pieces = [pieces[0]] + [
        p.send(after(pieces[s], held[1], mods), lambda x, z, y, c, s=s: (x, z + s, y, c))
        for s in range(1, S)
    ]
    (merged,) = call(stack_kernel, [(S, blocks, local, cols)], p.where, *pieces, fast=[0], fast_in=True)
    held.append(p.send(after(held[2], merged), lambda x, z, y, c: (x, z ^ 1, y, c)))
    merged = [
        p.send(merged, lambda x, z, y, c, e=e, d=d: (x - d, z, y - e, c)) if e or d else merged
        for e in range(Y)
        for d in range(G)
    ]
    early = [after(v, *merged[1:]) for v in held[:3]]
    held += [swap(v, 0, f) for f in range(1, G) for v in (*early, held[3])]
    norm, base = call(
        partial(norm_kernel, G, S, Y),
        [(blocks, every, cols), (blocks, toks, cols)],
        p.where,
        *merged,
        mods,
        fast=range(2),
        fast_in=True,
    )
    parts = call(
        partial(attend_kernel, G, S, Y),
        [(G, toks, half)] * blocks,
        p.where,
        norm,
        *held,
        scratch=[pltpu.VMEM((S, every, HD), BF)],
        flops=10 * every * width * cols,
        fast=range(blocks),
        fast_in=True,
    )
    parts = [
        p.send(parts[e * G + d], lambda x, z, y, c, e=e, d=d: (x + d, z, y + e, c))
        if e or d
        else parts[0]
        for e in range(Y)
        for d in range(G)
    ]
    result = call(
        partial(result_kernel, G, S, Y),
        [(local, width)] * S,
        p.where,
        mods,
        base,
        *parts,
        fast=range(S),
        fast_in=True,
    )
    result = [p.send(result[s], lambda x, z, y, c, s=s: (c, z - s, y, x)) for s in range(S)]
    (out,) = call(
        partial(home_kernel, S), [(S, local, width)], p.where, *result, copies=S
    )
    return out


def solution(mesh):
    groups, n = mesh.shape["group"], mesh.shape["seq"]

    def per_device(*args):
        hidden, w_out = args[0], args[6]
        seqs, _, width = hidden.shape
        blocks = n // seqs
        fits = (
            groups == 2
            and blocks == groups * groups
            and n == seqs * blocks
            and blocks == seqs
            and w_out.shape[0] == HD
            and width % blocks == 0
            and (width // blocks) % 16 == 0
        )
        return in_planes(groups, n, *args) if fits else gathered(*args)

    placed = (
        P("group", "seq", None),
        P("group", "seq", None),
        P("group"),
        P("seq", None),
        P(),
        P("seq", None),
        P("seq", None),
    )
    return jax.shard_map(
        per_device, mesh=mesh, in_specs=placed, out_specs=P("group", "seq", None), check_vma=False
    )
```
